32 devices in a mesh: dp: 2 (over y), seq: 16 (over z, x, core).
Axes of the slice: x: 2, y: 2, z: 4, core: 2. Of those that a mesh axis runs over, the one named last changes fastest.
Arguments:
- grad_out: bfloat16 [2, 2048, 2048], P('dp', None, 'seq'), may hold values from -6 to 6
- gate: bfloat16 [2, 2048, 2048], P('dp', None, 'seq'), may hold values from -6 to 6
- value: bfloat16 [2, 2048, 2048], P('dp', None, 'seq'), may hold values from -6 to 6
- filter_taps: bfloat16 [2048, 2048], P(None, 'seq'), may hold values from -2 to 2
Outputs:
- grad_gate: bfloat16 [2, 2048, 2048], P('dp', None, 'seq')
- grad_value: bfloat16 [2, 2048, 2048], P('dp', None, 'seq')
- grad_filter: float32 [2048, 2048], P('seq', 'dp')
The draws below stay inside these ranges and needn't reach their ends.
All inputs are finite; a program needn't handle non-finite values.
Results may differ from the reference program's by a relative error of at most 0.017.
Values may be sent and summed in bfloat16 or wider, within the bound.
No kernel may reach another device: no remote copies, remote signals or barrier semaphores. Data moves between devices by JAX's collectives and lax.ppermute only.
A program may use at most 128 MiB of HBM per device.

```python
import math
import jax
import jax.numpy as jnp
from jax import lax

CH = 2048
LEN = 2048
BATCH = 2


def draw_filter_taps(key, part):
    key_reach = jax.random.fold_in(key, 11)
    key_taps = jax.random.fold_in(key, 12)
    lowest = 30.0
    highest = LEN * 2.0
    fraction = jax.random.uniform(key_reach, (CH, 1), jnp.float32)
    reach = lowest * jnp.exp(fraction * jnp.log(highest / lowest))
    taps = jnp.clip(jax.random.normal(key_taps, (CH, LEN), jnp.float32), -6.0, 6.0)
    places = lax.broadcasted_iota(jnp.float32, (CH, LEN), 1)
    return (taps * jnp.sqrt(2.0 / reach) * jnp.exp(-places / reach)).astype(jnp.bfloat16)


def shard_levels(own_key, extent, cuts, smallest, high):
    level, own = 1.0, jax.random.fold_in(own_key, 6)
    for dim, shards_of in cuts:
        heights = jnp.exp(jax.random.uniform(jax.random.fold_in(own, dim), (shards_of,), jnp.float32, smallest / len(cuts), high / len(cuts)))
        level = level * jnp.repeat(heights, extent[dim] // shards_of).reshape([-1 if axis == dim else 1 for axis in range(len(extent))])
    return level


def centred(stream_key, shape, spread, bound, cuts=(), kind=jnp.bfloat16):
    level = shard_levels(stream_key, shape, cuts, -0.22, 0.18) if cuts else 1.0
    drawn = jax.random.normal(stream_key, shape, jnp.float32) * spread * level
    return jnp.minimum(jnp.maximum(drawn, -bound), bound).astype(kind)


def setup_inputs(seed: int = 0) -> dict:
    streams_of = jax.random.split(jax.random.key(seed), 5)
    return {
        "grad_out": centred(streams_of[0], (BATCH, CH, LEN), 1.0, 6.0, ((0, 2), (2, 16))),
        "gate": centred(streams_of[1], (BATCH, CH, LEN), 1.0, 6.0, ((0, 2), (2, 16))),
        "value": centred(streams_of[2], (BATCH, CH, LEN), 1.0, 6.0, ((0, 2), (2, 16))),
        "filter_taps": draw_filter_taps(jax.random.fold_in(streams_of[4], 71), 0),
    }


def per_block(pieces):
    grad_block, gate_block, value_block, filter_block = pieces
    size_n = 2 * LEN
    gated = (grad_block.astype(jnp.float32) * gate_block.astype(jnp.float32)).astype(jnp.bfloat16)
    gated = lax.optimization_barrier(gated).astype(jnp.float32)
    spec_gated = jnp.fft.rfft(gated, n=size_n, axis=-1)
    spec_value = jnp.fft.rfft(value_block.astype(jnp.float32), n=size_n, axis=-1)
    spec_filter = jnp.fft.rfft(filter_block.astype(jnp.float32), n=size_n, axis=-1)[None]
    conv = jnp.fft.irfft(spec_filter * spec_value, n=size_n, axis=-1)[..., :LEN].astype(jnp.bfloat16)
    conv = lax.optimization_barrier(conv)
    grad_gate = (grad_block.astype(jnp.float32) * conv.astype(jnp.float32)).astype(jnp.bfloat16)
    grad_value = jnp.fft.irfft(jnp.conj(spec_filter) * spec_gated, n=size_n, axis=-1)[..., :LEN].astype(jnp.bfloat16)
    cross = jnp.fft.irfft(jnp.conj(spec_value) * spec_gated, n=size_n, axis=-1)[..., :LEN]
    factor = 1.0 / (BATCH * math.sqrt(LEN))
    grad_filter = (lax.optimization_barrier(jnp.sum(cross, axis=0)) * factor).astype(jnp.float32)
    return (grad_gate, grad_value, grad_filter)

def reference(grad_out, gate, value, filter_taps):
    lanes = 128
    count = CH // lanes

    def split_rows(array):
        return array.reshape(BATCH, count, lanes, LEN).transpose(1, 0, 2, 3)
    pieces = (split_rows(grad_out), split_rows(gate), split_rows(value), filter_taps.reshape(count, lanes, LEN))
    grad_gate, grad_value, grad_filter = lax.map(per_block, pieces)
    grad_gate = grad_gate.transpose(1, 0, 2, 3).reshape(BATCH, CH, LEN)
    grad_value = grad_value.transpose(1, 0, 2, 3).reshape(BATCH, CH, LEN)
    return (grad_gate, grad_value, grad_filter.reshape(CH, LEN))
```

```python
import functools
import math

import jax
import jax.numpy as jnp
import numpy as np
from jax import lax
from jax.experimental import pallas as pl
from jax.experimental.pallas import tpu as pltpu
from jax.sharding import PartitionSpec as P

ROWS = 16


def inner_tables(blocks, width):
    total = 2 * blocks * width
    pos = np.arange(width)
    tables = []
    for outer in range(blocks + 1):
        turns = pos[:, None] * (outer + 2 * blocks * pos[None, :]) % total
        angle = 2.0 * np.pi / total * turns
        cos, sin = np.cos(angle), np.sin(angle)
        tables.append(np.block([[cos, -sin], [sin, cos]]))
    table = np.stack(tables)
    weight = np.full((blocks + 1, 1, 1), 2.0 / total)
    weight[0] = weight[blocks] = 1.0 / total
    return (
        table.astype(jnp.bfloat16),
        (table.transpose(0, 2, 1) * weight).astype(jnp.bfloat16),
    )


def turn(number, cos, sin):
    real, imag = number
    if abs(sin) < 1e-9:
        return (real, imag) if cos > 0 else (-real, -imag)
    if abs(cos) < 1e-9:
        return (imag, -real) if sin > 0 else (-imag, real)
    return (real * cos + imag * sin, imag * cos - real * sin)


def add(left, right):
    return (left[0] + right[0], left[1] + right[1])


def sub(left, right):
    return (left[0] - right[0], left[1] - right[1])


def complex_dft(items, sign):
    count = len(items)
    if count == 1:
        return items
    half = count // 2
    low, high = items[:half], items[half:]
    even = complex_dft([add(a, b) for a, b in zip(low, high)], sign)
    odd = []
    for n, (a, b) in enumerate(zip(low, high)):
        angle = 2.0 * math.pi * n / count
        odd.append(turn(sub(a, b), math.cos(angle), sign * math.sin(angle)))
    odd = complex_dft(odd, sign)
    return [item for pair in zip(even, odd) for item in pair]


def odd_outputs(items, period):
    quarter = len(items) // 2
    turned = []
    for n in range(quarter):
        angle = 2.0 * math.pi * n / period
        turned.append(turn((items[n], -items[n + quarter]), math.cos(angle), math.sin(angle)))
    found = {}
    for m, (real, imag) in enumerate(complex_dft(turned, 1)):
        freq = 4 * m + 1
        if freq > period // 2:
            freq, imag = period - freq, -imag
        found[freq] = (real, imag)
    return found


def real_dft(items):
    count = len(items)
    if count == 1:
        return {0: (items[0], None)}
    if count == 2:
        return {0: (items[0] + items[1], None), 1: (items[0] - items[1], None)}
    half = count // 2
    low, high = items[:half], items[half:]
    found = {2 * k: v for k, v in real_dft([a + b for a, b in zip(low, high)]).items()}
    found.update(odd_outputs([a - b for a, b in zip(low, high)], count))
    return found


def padded_dft(items):
    found = {2 * k: v for k, v in real_dft(items).items()}
    found.update(odd_outputs(items, 2 * len(items)))
    return found


def odd_inputs(freqs, period):
    quarter = period // 4
    items = []
    for m in range(quarter):
        freq = 4 * m + 1
        if freq > period // 2:
            real, imag = freqs[period - freq]
            items.append((real, -imag))
        else:
            items.append(freqs[freq])
    low, high = [], []
    for n, item in enumerate(complex_dft(items, -1)):
        angle = 2.0 * math.pi * n / period
        real, imag = turn(item, math.cos(angle), -math.sin(angle))
        low.append(real)
        high.append(-imag)
    return low + high


def real_inverse(freqs, count):
    if count == 1:
        return [freqs[0][0]]
    if count == 2:
        return [freqs[0][0] + freqs[1][0], freqs[0][0] - freqs[1][0]]
    even = real_inverse({k // 2: v for k, v in freqs.items() if k % 2 == 0}, count // 2)
    odd = odd_inputs(freqs, count)
    return [a + b for a, b in zip(even, odd)] + [a - b for a, b in zip(even, odd)]


def padded_inverse(freqs, count):
    even = real_inverse({k // 2: v for k, v in freqs.items() if k % 2 == 0}, count)
    return [a + b for a, b in zip(even, odd_inputs(freqs, 2 * count))]


def outer_forward(source, mid, base):
    blocks, group, width = source.shape

    def body(step, carry):
        start = pl.multiple_of(step * ROWS, ROWS)
        rows = pl.ds(start, ROWS)
        found = padded_dft([source[n, rows, :].astype(jnp.float32) for n in range(blocks)])
        out_rows = pl.ds(pl.multiple_of(start + base, ROWS), ROWS)
        for freq, (real, imag) in found.items():
            if imag is None:
                imag = jnp.zeros_like(real)
            mid[freq, out_rows, 0:width] = real.astype(jnp.bfloat16)
            mid[freq, out_rows, width : 2 * width] = imag.astype(jnp.bfloat16)
        return carry

    lax.fori_loop(0, group // ROWS, body, 0)


def outer_inverse(mid, base, dest):
    blocks, group, width = dest.shape

    def body(step, carry):
        start = pl.multiple_of(step * ROWS, ROWS)
        rows = pl.ds(pl.multiple_of(start + base, ROWS), ROWS)
        freqs = {
            k: (mid[k, rows, 0:width], mid[k, rows, width : 2 * width]) for k in range(blocks + 1)
        }
        for n, item in enumerate(padded_inverse(freqs, blocks)):
            dest[n, pl.ds(start, ROWS), :] = item.astype(dest.dtype)
        return carry

    lax.fori_loop(0, group // ROWS, body, 0)


def product(left, right, width, conjugate):
    left_real, left_imag = left[:, :width], left[:, width:]
    right_real, right_imag = right[:, :width], right[:, width:]
    if conjugate:
        left_imag = -left_imag
    real = left_real * right_real - left_imag * right_imag
    imag = left_real * right_imag + left_imag * right_real
    return jnp.concatenate([real.astype(jnp.bfloat16), imag.astype(jnp.bfloat16)], 1)


def conv_kernel(value, taps, forward, inverse, conv, spec_value, spec_taps, mid, back):
    blocks, group, width = value.shape
    outer_forward(value, mid, 0)
    outer_forward(taps, mid, group)

    def body(k, carry):
        spec = jnp.dot(mid[k], forward[k], preferred_element_type=jnp.float32)
        left, right = spec[:group], spec[group:]
        spec_value[k] = left
        spec_taps[k] = right
        back[k] = jnp.dot(
            product(right, left, width, False), inverse[k], preferred_element_type=jnp.float32
        )
        return carry

    lax.fori_loop(0, blocks + 1, body, 0)
    outer_inverse(back, 0, conv)


def grad_kernel(gated, spec_value, spec_taps, forward, inverse, grad_value, cross, mid, back):
    blocks, group, width = gated.shape
    outer_forward(gated, mid, 0)

    def body(k, carry):
        spec = jnp.dot(mid[k], forward[k], preferred_element_type=jnp.float32)
        both = jnp.concatenate(
            [
                product(spec_taps[k], spec, width, True),
                product(spec_value[k], spec, width, True),
            ],
            0,
        )
        back[k] = jnp.dot(both, inverse[k], preferred_element_type=jnp.float32)
        return carry

    lax.fori_loop(0, blocks + 1, body, 0)
    outer_inverse(back, 0, grad_value)
    outer_inverse(back, group, cross)


def vmem(count):
    return [pl.BlockSpec(memory_space=pltpu.VMEM)] * count


def call(kernel, outs, scratch, *operands):
    return pl.pallas_call(
        kernel,
        out_shape=outs,
        in_specs=vmem(len(operands)),
        out_specs=tuple(vmem(len(outs))),
        scratch_shapes=scratch,
        compiler_params=pltpu.CompilerParams(vmem_limit_bytes=40 * 1024 * 1024),
        cost_estimate=pl.CostEstimate(flops=10**9, bytes_accessed=10**7, transcendentals=0),
    )(*operands)


def on_device(grad_out, gate, value, filter_taps):
    nseq = lax.axis_size("seq")
    ndp = lax.axis_size("dp")
    chans = grad_out.shape[1]
    width = grad_out.shape[2]
    group = chans // nseq
    blocks = nseq
    forward, inverse = (jnp.asarray(t) for t in inner_tables(blocks, width))

    def exchange(array):
        return lax.all_to_all(array, "seq", split_axis=0, concat_axis=0, tiled=True)

    value_cols = exchange(value[0].reshape(nseq, group, width))
    taps_cols = exchange(filter_taps.reshape(nseq, group, width))
    gated = (grad_out[0].astype(jnp.float32) * gate[0].astype(jnp.float32)).astype(jnp.bfloat16)
    gated_cols = exchange(gated.reshape(nseq, group, width))

    block = functools.partial(jax.ShapeDtypeStruct, (blocks, group, width))
    spec = jax.ShapeDtypeStruct((blocks + 1, group, 2 * width), jnp.float32)
    mid_of = lambda n: pltpu.VMEM((blocks + 1, n * group, 2 * width), jnp.bfloat16)
    back_of = lambda n: pltpu.VMEM((blocks + 1, n * group, 2 * width), jnp.float32)
    conv, spec_value, spec_taps = call(
        conv_kernel,
        (block(jnp.bfloat16), spec, spec),
        [mid_of(2), back_of(1)],
        value_cols,
        taps_cols,
        forward,
        inverse,
    )
    back_conv = exchange(conv)
    grad_value, cross = call(
        grad_kernel,
        (block(jnp.bfloat16), block(jnp.float32)),
        [mid_of(1), back_of(2)],
        gated_cols,
        spec_value,
        spec_taps,
        forward,
        inverse,
    )
    back_grad = exchange(grad_value)
    grad_gate = (
        grad_out[0].astype(jnp.float32) * back_conv.reshape(chans, width).astype(jnp.float32)
    ).astype(jnp.bfloat16)

    factor = 1.0 / (ndp * math.sqrt(nseq * width))
    cross = cross.reshape(ndp, blocks // ndp, group, width)
    here = lax.axis_index("dp")
    total = lax.dynamic_index_in_dim(cross, here, 0, keepdims=False)
    for step in range(1, ndp):
        other = lax.dynamic_index_in_dim(cross, (here + step) % ndp, 0, keepdims=False)
        total = total + lax.ppermute(other, "dp", [(i, (i + step) % ndp) for i in range(ndp)])
    summed = (total * factor).transpose(1, 0, 2).reshape(group, blocks // ndp * width)
    return (grad_gate[None], back_grad.reshape(chans, width)[None], summed)


def solution(mesh):
    return jax.shard_map(
        on_device,
        mesh=mesh,
        in_specs=(P("dp", None, "seq"), P("dp", None, "seq"), P("dp", None, "seq"), P(None, "seq")),
        out_specs=(P("dp", None, "seq"), P("dp", None, "seq"), P("seq", "dp")),
        check_vma=False,
    )
```

```python
import functools
import math

import jax
import jax.numpy as jnp
import numpy as np
from jax import lax
from jax.experimental import pallas as pl
from jax.experimental.pallas import tpu as pltpu
from jax.sharding import PartitionSpec as P

ROWS = 16


def inner_tables(blocks, width):
    total = 2 * blocks * width
    pos = np.arange(width)
    tables = []
    for outer in range(blocks + 1):
        turns = pos[:, None] * (outer + 2 * blocks * pos[None, :]) % total
        angle = 2.0 * np.pi / total * turns
        cos, sin = np.cos(angle), np.sin(angle)
        tables.append(np.block([[cos, -sin], [sin, cos]]))
    table = np.stack(tables)
    weight = np.full((blocks + 1, 1, 1), 2.0 / total)
    weight[0] = weight[blocks] = 1.0 / total
    return (
        table.astype(jnp.bfloat16),
        (table.transpose(0, 2, 1) * weight).astype(jnp.bfloat16),
    )


def turn(number, cos, sin):
    real, imag = number
    if abs(sin) < 1e-9:
        return (real, imag) if cos > 0 else (-real, -imag)
    if abs(cos) < 1e-9:
        return (imag, -real) if sin > 0 else (-imag, real)
    return (real * cos + imag * sin, imag * cos - real * sin)


def add(left, right):
    return (left[0] + right[0], left[1] + right[1])


def sub(left, right):
    return (left[0] - right[0], left[1] - right[1])


def complex_dft(items, sign):
    count = len(items)
    if count == 1:
        return items
    half = count // 2
    low, high = items[:half], items[half:]
    even = complex_dft([add(a, b) for a, b in zip(low, high)], sign)
    odd = []
    for n, (a, b) in enumerate(zip(low, high)):
        angle = 2.0 * math.pi * n / count
        odd.append(turn(sub(a, b), math.cos(angle), sign * math.sin(angle)))
    odd = complex_dft(odd, sign)
    return [item for pair in zip(even, odd) for item in pair]


def odd_outputs(items, period):
    quarter = len(items) // 2
    turned = []
    for n in range(quarter):
        angle = 2.0 * math.pi * n / period
        turned.append(turn((items[n], -items[n + quarter]), math.cos(angle), math.sin(angle)))
    found = {}
    for m, (real, imag) in enumerate(complex_dft(turned, 1)):
        freq = 4 * m + 1
        if freq > period // 2:
            freq, imag = period - freq, -imag
        found[freq] = (real, imag)
    return found


def real_dft(items):
    count = len(items)
    if count == 1:
        return {0: (items[0], None)}
    if count == 2:
        return {0: (items[0] + items[1], None), 1: (items[0] - items[1], None)}
    half = count // 2
    low, high = items[:half], items[half:]
    found = {2 * k: v for k, v in real_dft([a + b for a, b in zip(low, high)]).items()}
    found.update(odd_outputs([a - b for a, b in zip(low, high)], count))
    return found


def padded_dft(items):
    found = {2 * k: v for k, v in real_dft(items).items()}
    found.update(odd_outputs(items, 2 * len(items)))
    return found


def odd_inputs(freqs, period):
    quarter = period // 4
    items = []
    for m in range(quarter):
        freq = 4 * m + 1
        if freq > period // 2:
            real, imag = freqs[period - freq]
            items.append((real, -imag))
        else:
            items.append(freqs[freq])
    low, high = [], []
    for n, item in enumerate(complex_dft(items, -1)):
        angle = 2.0 * math.pi * n / period
        real, imag = turn(item, math.cos(angle), -math.sin(angle))
        low.append(real)
        high.append(-imag)
    return low + high


def real_inverse(freqs, count):
    if count == 1:
        return [freqs[0][0]]
    if count == 2:
        return [freqs[0][0] + freqs[1][0], freqs[0][0] - freqs[1][0]]
    even = real_inverse({k // 2: v for k, v in freqs.items() if k % 2 == 0}, count // 2)
    odd = odd_inputs(freqs, count)
    return [a + b for a, b in zip(even, odd)] + [a - b for a, b in zip(even, odd)]


def padded_inverse(freqs, count):
    even = real_inverse({k // 2: v for k, v in freqs.items() if k % 2 == 0}, count)
    return [a + b for a, b in zip(even, odd_inputs(freqs, 2 * count))]


def outer_forward(source, mid, base):
    blocks, group, width = source.shape

    def body(step, carry):
        start = pl.multiple_of(step * ROWS, ROWS)
        rows = pl.ds(start, ROWS)
        found = padded_dft([source[n, rows, :].astype(jnp.float32) for n in range(blocks)])
        out_rows = pl.ds(pl.multiple_of(start + base, ROWS), ROWS)
        for freq, (real, imag) in found.items():
            if imag is None:
                imag = jnp.zeros_like(real)
            mid[freq, out_rows, 0:width] = real.astype(jnp.bfloat16)
            mid[freq, out_rows, width : 2 * width] = imag.astype(jnp.bfloat16)
        return carry

    lax.fori_loop(0, group // ROWS, body, 0)


def outer_inverse(mid, base, dest):
    blocks, group, width = dest.shape

    def body(step, carry):
        start = pl.multiple_of(step * ROWS, ROWS)
        rows = pl.ds(pl.multiple_of(start + base, ROWS), ROWS)
        freqs = {
            k: (mid[k, rows, 0:width], mid[k, rows, width : 2 * width]) for k in range(blocks + 1)
        }
        for n, item in enumerate(padded_inverse(freqs, blocks)):
            dest[n, pl.ds(start, ROWS), :] = item.astype(dest.dtype)
        return carry

    lax.fori_loop(0, group // ROWS, body, 0)


def product(left, right, width, conjugate):
    left_real, left_imag = left[:, :width], left[:, width:]
    right_real, right_imag = right[:, :width], right[:, width:]
    if conjugate:
        left_imag = -left_imag
    real = left_real * right_real - left_imag * right_imag
    imag = left_real * right_imag + left_imag * right_real
    return jnp.concatenate([real.astype(jnp.bfloat16), imag.astype(jnp.bfloat16)], 1)


def pack_kernel(nseq, grad_out, gate, value, taps, *parts):
    here = lax.axis_index("seq")
    group = value.shape[0] // nseq
    for mask, part in enumerate(parts):
        rows = pl.ds(pl.multiple_of((here ^ mask) * group, ROWS), group)
        part[0] = value[rows, :]
        part[1] = taps[rows, :]
        part[2] = (grad_out[rows, :].astype(jnp.float32) * gate[rows, :].astype(jnp.float32)).astype(
            jnp.bfloat16
        )


def main_kernel(nseq, ndp, factor, *refs):
    parts, refs = refs[:nseq], refs[nseq:]
    forward, inverse = refs[:2]
    outs, refs = refs[2 : 2 + nseq], refs[2 + nseq :]
    sums, refs = refs[:ndp], refs[ndp:]
    signals, results, cross, mid, back = refs
    here = lax.axis_index("seq")
    here_dp = lax.axis_index("dp")
    blocks, group, width = cross.shape
    for mask, part in enumerate(parts):
        for which in range(3):
            signals[which, here ^ mask] = part[which]
    for which in range(3):
        outer_forward(signals.at[which], mid, which * group)

    def body(k, carry):
        spec = jnp.dot(mid[k], forward[k], preferred_element_type=jnp.float32)
        value, taps, gated = spec[:group], spec[group : 2 * group], spec[2 * group :]
        three = jnp.concatenate(
            [
                product(taps, value, width, False),
                product(taps, gated, width, True),
                product(value, gated, width, True),
            ],
            0,
        )
        back[k] = jnp.dot(three, inverse[k], preferred_element_type=jnp.float32)
        return carry

    lax.fori_loop(0, blocks + 1, body, 0)
    outer_inverse(back, 0, results.at[0])
    outer_inverse(back, group, results.at[1])
    outer_inverse(back, 2 * group, cross)
    for mask, out in enumerate(outs):
        for which in range(2):
            out[which] = results[which, here ^ mask]
    share = blocks // ndp
    for step, total in enumerate(sums):
        first = lax.rem(here_dp + step, ndp) * share
        for n in range(share):
            total[:, n * width : (n + 1) * width] = cross[first + n] * factor


def unpack_kernel(nseq, ndp, *refs):
    parts, refs = refs[:nseq], refs[nseq:]
    sums, refs = refs[:ndp], refs[ndp:]
    grad_out, grad_gate, grad_value, grad_taps = refs
    here = lax.axis_index("seq")
    group = grad_out.shape[0] // nseq
    for mask, part in enumerate(parts):
        rows = pl.ds(pl.multiple_of((here ^ mask) * group, ROWS), group)
        grad_gate[rows, :] = (
            grad_out[rows, :].astype(jnp.float32) * part[0].astype(jnp.float32)
        ).astype(jnp.bfloat16)
        grad_value[rows, :] = part[1]
    total = sums[0][...]
    for other in sums[1:]:
        total = total + other[...]
    grad_taps[...] = total


def vmem(count):
    return [pl.BlockSpec(memory_space=pltpu.VMEM)] * count


def call(kernel, outs, scratch, *operands):
    return pl.pallas_call(
        kernel,
        out_shape=outs,
        in_specs=vmem(len(operands)),
        out_specs=tuple(vmem(len(outs))),
        scratch_shapes=scratch,
        compiler_params=pltpu.CompilerParams(vmem_limit_bytes=40 * 1024 * 1024),
        cost_estimate=pl.CostEstimate(flops=10**9, bytes_accessed=10**7, transcendentals=0),
    )(*operands)


def exchange(parts):
    count = len(parts)
    got = [parts[0]]
    for mask in range(1, count):
        got.append(lax.ppermute(parts[mask], "seq", [(i, i ^ mask) for i in range(count)]))
    return got


def on_device(grad_out, gate, value, filter_taps):
    nseq = lax.axis_size("seq")
    ndp = lax.axis_size("dp")
    chans = grad_out.shape[1]
    width = grad_out.shape[2]
    group = chans // nseq
    blocks = nseq
    forward, inverse = (jnp.asarray(t) for t in inner_tables(blocks, width))
    factor = 1.0 / (ndp * math.sqrt(nseq * width))
    shape = jax.ShapeDtypeStruct

    parts = call(
        functools.partial(pack_kernel, nseq),
        [shape((3, group, width), jnp.bfloat16)] * nseq,
        [],
        grad_out[0],
        gate[0],
        value[0],
        filter_taps,
    )
    parts = exchange(parts)
    outs = call(
        functools.partial(main_kernel, nseq, ndp, factor),
        [shape((2, group, width), jnp.bfloat16)] * nseq
        + [shape((group, blocks // ndp * width), jnp.float32)] * ndp,
        [
            pltpu.VMEM((3, blocks, group, width), jnp.bfloat16),
            pltpu.VMEM((2, blocks, group, width), jnp.bfloat16),
            pltpu.VMEM((blocks, group, width), jnp.float32),
            pltpu.VMEM((blocks + 1, 3 * group, 2 * width), jnp.bfloat16),
            pltpu.VMEM((blocks + 1, 3 * group, 2 * width), jnp.float32),
        ],
        *parts,
        forward,
        inverse,
    )
    sums = [outs[nseq]]
    for step in range(1, ndp):
        pairs = [(i, (i + step) % ndp) for i in range(ndp)]
        sums.append(lax.ppermute(outs[nseq + step], "dp", pairs))
    backs = exchange(outs[:nseq])
    grad_gate, grad_value, grad_taps = call(
        functools.partial(unpack_kernel, nseq, ndp),
        [shape((chans, width), jnp.bfloat16)] * 2
        + [shape((group, blocks // ndp * width), jnp.float32)],
        [],
        *backs,
        *sums,
        grad_out[0],
    )
    return (grad_gate[None], grad_value[None], grad_taps)


def solution(mesh):
    return jax.shard_map(
        on_device,
        mesh=mesh,
        in_specs=(P("dp", None, "seq"), P("dp", None, "seq"), P("dp", None, "seq"), P(None, "seq")),
        out_specs=(P("dp", None, "seq"), P("dp", None, "seq"), P("seq", "dp")),
        check_vma=False,
    )
```

```python
import functools
import math

import jax
import jax.numpy as jnp
import numpy as np
from jax import lax
from jax.experimental import pallas as pl
from jax.experimental.pallas import tpu as pltpu
from jax.sharding import PartitionSpec as P

ROWS = 16


def inner_tables(blocks, width):
    total = 2 * blocks * width
    pos = np.arange(width)
    tables = []
    for outer in range(blocks + 1):
        turns = pos[:, None] * (outer + 2 * blocks * pos[None, :]) % total
        angle = 2.0 * np.pi / total * turns
        cos, sin = np.cos(angle), np.sin(angle)
        tables.append(np.block([[cos, -sin], [sin, cos]]))
    table = np.stack(tables)
    weight = np.full((blocks + 1, 1, 1), 2.0 / total)
    weight[0] = weight[blocks] = 1.0 / total
    return (
        table.astype(jnp.bfloat16),
        (table.transpose(0, 2, 1) * weight).astype(jnp.bfloat16),
    )


def turn(number, cos, sin):
    real, imag = number
    if abs(sin) < 1e-9:
        return (real, imag) if cos > 0 else (-real, -imag)
    if abs(cos) < 1e-9:
        return (imag, -real) if sin > 0 else (-imag, real)
    return (real * cos + imag * sin, imag * cos - real * sin)


def add(left, right):
    return (left[0] + right[0], left[1] + right[1])


def sub(left, right):
    return (left[0] - right[0], left[1] - right[1])


def complex_dft(items, sign):
    count = len(items)
    if count == 1:
        return items
    half = count // 2
    low, high = items[:half], items[half:]
    even = complex_dft([add(a, b) for a, b in zip(low, high)], sign)
    odd = []
    for n, (a, b) in enumerate(zip(low, high)):
        angle = 2.0 * math.pi * n / count
        odd.append(turn(sub(a, b), math.cos(angle), sign * math.sin(angle)))
    odd = complex_dft(odd, sign)
    return [item for pair in zip(even, odd) for item in pair]


def odd_outputs(items, period):
    quarter = len(items) // 2
    turned = []
    for n in range(quarter):
        angle = 2.0 * math.pi * n / period
        turned.append(turn((items[n], -items[n + quarter]), math.cos(angle), math.sin(angle)))
    found = {}
    for m, (real, imag) in enumerate(complex_dft(turned, 1)):
        freq = 4 * m + 1
        if freq > period // 2:
            freq, imag = period - freq, -imag
        found[freq] = (real, imag)
    return found


def real_dft(items):
    count = len(items)
    if count == 1:
        return {0: (items[0], None)}
    if count == 2:
        return {0: (items[0] + items[1], None), 1: (items[0] - items[1], None)}
    half = count // 2
    low, high = items[:half], items[half:]
    found = {2 * k: v for k, v in real_dft([a + b for a, b in zip(low, high)]).items()}
    found.update(odd_outputs([a - b for a, b in zip(low, high)], count))
    return found


def padded_dft(items):
    found = {2 * k: v for k, v in real_dft(items).items()}
    found.update(odd_outputs(items, 2 * len(items)))
    return found


def odd_inputs(freqs, period):
    quarter = period // 4
    items = []
    for m in range(quarter):
        freq = 4 * m + 1
        if freq > period // 2:
            real, imag = freqs[period - freq]
            items.append((real, -imag))
        else:
            items.append(freqs[freq])
    low, high = [], []
    for n, item in enumerate(complex_dft(items, -1)):
        angle = 2.0 * math.pi * n / period
        real, imag = turn(item, math.cos(angle), -math.sin(angle))
        low.append(real)
        high.append(-imag)
    return low + high


def real_inverse(freqs, count):
    if count == 1:
        return [freqs[0][0]]
    if count == 2:
        return [freqs[0][0] + freqs[1][0], freqs[0][0] - freqs[1][0]]
    even = real_inverse({k // 2: v for k, v in freqs.items() if k % 2 == 0}, count // 2)
    odd = odd_inputs(freqs, count)
    return [a + b for a, b in zip(even, odd)] + [a - b for a, b in zip(even, odd)]


def padded_inverse(freqs, count):
    even = real_inverse({k // 2: v for k, v in freqs.items() if k % 2 == 0}, count)
    return [a + b for a, b in zip(even, odd_inputs(freqs, 2 * count))]


def outer_forward(source, mid, base):
    blocks, group, width = source.shape

    def body(step, carry):
        start = pl.multiple_of(step * ROWS, ROWS)
        rows = pl.ds(start, ROWS)
        found = padded_dft([source[n, rows, :].astype(jnp.float32) for n in range(blocks)])
        out_rows = pl.ds(pl.multiple_of(start + base, ROWS), ROWS)
        for freq, (real, imag) in found.items():
            if imag is None:
                imag = jnp.zeros_like(real)
            mid[freq, out_rows, 0:width] = real.astype(jnp.bfloat16)
            mid[freq, out_rows, width : 2 * width] = imag.astype(jnp.bfloat16)
        return carry

    lax.fori_loop(0, group // ROWS, body, 0)


def outer_inverse(mid, base, dest):
    blocks, group, width = dest.shape

    def body(step, carry):
        start = pl.multiple_of(step * ROWS, ROWS)
        rows = pl.ds(pl.multiple_of(start + base, ROWS), ROWS)
        freqs = {
            k: (mid[k, rows, 0:width], mid[k, rows, width : 2 * width]) for k in range(blocks + 1)
        }
        for n, item in enumerate(padded_inverse(freqs, blocks)):
            dest[n, pl.ds(start, ROWS), :] = item.astype(dest.dtype)
        return carry

    lax.fori_loop(0, group // ROWS, body, 0)


def product(left, right, width, conjugate):
    left_real, left_imag = left[:, :width], left[:, width:]
    right_real, right_imag = right[:, :width], right[:, width:]
    if conjugate:
        left_imag = -left_imag
    real = left_real * right_real - left_imag * right_imag
    imag = left_real * right_imag + left_imag * right_real
    return jnp.concatenate([real.astype(jnp.bfloat16), imag.astype(jnp.bfloat16)], 1)


def pack_kernel(nseq, grad_out, gate, value, taps, *parts):
    here = lax.axis_index("seq")
    group = value.shape[0] // nseq
    for mask, part in enumerate(parts):
        rows = pl.ds(pl.multiple_of((here ^ mask) * group, ROWS), group)
        part[0] = value[rows, :]
        part[1] = taps[rows, :]
        part[2] = (grad_out[rows, :].astype(jnp.float32) * gate[rows, :].astype(jnp.float32)).astype(
            jnp.bfloat16
        )


def main_kernel(nseq, ndp, factor, *refs):
    parts, refs = refs[:nseq], refs[nseq:]
    forward, inverse = refs[:2]
    outs, refs = refs[2 : 2 + nseq], refs[2 + nseq :]
    sums, refs = refs[:ndp], refs[ndp:]
    signals, results, cross, mid, back = refs
    here = lax.axis_index("seq")
    here_dp = lax.axis_index("dp")
    blocks, group, width = cross.shape
    for mask, part in enumerate(parts):
        for which in range(3):
            signals[which, here ^ mask] = part[which]
    for which in range(3):
        outer_forward(signals.at[which], mid, which * group)

    def body(k, carry):
        spec = jnp.dot(mid[k], forward[k], preferred_element_type=jnp.float32)
        value, taps, gated = spec[:group], spec[group : 2 * group], spec[2 * group :]
        three = jnp.concatenate(
            [
                product(taps, value, width, False),
                product(taps, gated, width, True),
                product(value, gated, width, True),
            ],
            0,
        )
        back[k] = jnp.dot(three, inverse[k], preferred_element_type=jnp.float32)
        return carry

    lax.fori_loop(0, blocks + 1, body, 0)
    outer_inverse(back, 0, results.at[0])
    outer_inverse(back, group, results.at[1])
    outer_inverse(back, 2 * group, cross)
    for mask, out in enumerate(outs):
        for which in range(2):
            out[which] = results[which, here ^ mask]
    share = blocks // ndp
    for step, total in enumerate(sums):
        first = lax.rem(here_dp + step, ndp) * share
        for n in range(share):
            total[:, n * width : (n + 1) * width] = cross[first + n] * factor


def unpack_kernel(nseq, ndp, *refs):
    parts, refs = refs[:nseq], refs[nseq:]
    sums, refs = refs[:ndp], refs[ndp:]
    grad_out, grad_gate, grad_value, grad_taps = refs
    here = lax.axis_index("seq")
    group = grad_out.shape[0] // nseq
    for mask, part in enumerate(parts):
        rows = pl.ds(pl.multiple_of((here ^ mask) * group, ROWS), group)
        grad_gate[rows, :] = (
            grad_out[rows, :].astype(jnp.float32) * part[0].astype(jnp.float32)
        ).astype(jnp.bfloat16)
        grad_value[rows, :] = part[1]
    total = sums[0][...]
    for other in sums[1:]:
        total = total + other[...]
    grad_taps[...] = total


def vmem(count):
    return [pl.BlockSpec(memory_space=pltpu.VMEM)] * count


def call(kernel, outs, scratch, *operands):
    return pl.pallas_call(
        kernel,
        out_shape=outs,
        in_specs=vmem(len(operands)),
        out_specs=tuple(vmem(len(outs))),
        scratch_shapes=scratch,
        compiler_params=pltpu.CompilerParams(vmem_limit_bytes=40 * 1024 * 1024),
        cost_estimate=pl.CostEstimate(flops=10**9, bytes_accessed=10**7, transcendentals=0),
    )(*operands)


def mask_order(count):
    far = list(range(count - 1, count // 2 - 1, -1))
    near = list(range(count // 2 - 1, 0, -1))
    order = []
    while far or near:
        order += far[:2] + near[:1]
        far, near = far[2:], near[1:]
    return order


def exchange(parts):
    count = len(parts)
    got = list(parts)
    for mask in mask_order(count):
        got[mask] = lax.ppermute(parts[mask], "seq", [(i, i ^ mask) for i in range(count)])
    return got


def on_device(grad_out, gate, value, filter_taps):
    nseq = lax.axis_size("seq")
    ndp = lax.axis_size("dp")
    chans = grad_out.shape[1]
    width = grad_out.shape[2]
    group = chans // nseq
    blocks = nseq
    forward, inverse = (jnp.asarray(t) for t in inner_tables(blocks, width))
    factor = 1.0 / (ndp * math.sqrt(nseq * width))
    shape = jax.ShapeDtypeStruct

    parts = call(
        functools.partial(pack_kernel, nseq),
        [shape((3, group, width), jnp.bfloat16)] * nseq,
        [],
        grad_out[0],
        gate[0],
        value[0],
        filter_taps,
    )
    parts = exchange(parts)
    outs = call(
        functools.partial(main_kernel, nseq, ndp, factor),
        [shape((2, group, width), jnp.bfloat16)] * nseq
        + [shape((group, blocks // ndp * width), jnp.float32)] * ndp,
        [
            pltpu.VMEM((3, blocks, group, width), jnp.bfloat16),
            pltpu.VMEM((2, blocks, group, width), jnp.bfloat16),
            pltpu.VMEM((blocks, group, width), jnp.float32),
            pltpu.VMEM((blocks + 1, 3 * group, 2 * width), jnp.bfloat16),
            pltpu.VMEM((blocks + 1, 3 * group, 2 * width), jnp.float32),
        ],
        *parts,
        forward,
        inverse,
    )
    sums = [outs[nseq]]
    for step in range(1, ndp):
        pairs = [(i, (i + step) % ndp) for i in range(ndp)]
        sums.append(lax.ppermute(outs[nseq + step], "dp", pairs))
    backs = exchange(outs[:nseq])
    grad_gate, grad_value, grad_taps = call(
        functools.partial(unpack_kernel, nseq, ndp),
        [shape((chans, width), jnp.bfloat16)] * 2
        + [shape((group, blocks // ndp * width), jnp.float32)],
        [],
        *backs,
        *sums,
        grad_out[0],
    )
    return (grad_gate[None], grad_value[None], grad_taps)


def solution(mesh):
    return jax.shard_map(
        on_device,
        mesh=mesh,
        in_specs=(P("dp", None, "seq"), P("dp", None, "seq"), P("dp", None, "seq"), P(None, "seq")),
        out_specs=(P("dp", None, "seq"), P("dp", None, "seq"), P("seq", "dp")),
        check_vma=False,
    )
```

```python
import functools
import math

import jax
import jax.numpy as jnp
import numpy as np
from jax import lax
from jax.experimental import pallas as pl
from jax.experimental.pallas import tpu as pltpu
from jax.sharding import PartitionSpec as P

ROWS = 16


def inner_tables(blocks, width):
    total = 2 * blocks * width
    pos = np.arange(width)
    tables = []
    for outer in range(blocks + 1):
        turns = pos[:, None] * (outer + 2 * blocks * pos[None, :]) % total
        angle = 2.0 * np.pi / total * turns
        cos, sin = np.cos(angle), np.sin(angle)
        tables.append(np.block([[cos, -sin], [sin, cos]]))
    table = np.stack(tables)
    weight = np.full((blocks + 1, 1, 1), 2.0 / total)
    weight[0] = weight[blocks] = 1.0 / total
    return (
        table.astype(jnp.bfloat16),
        (table.transpose(0, 2, 1) * weight).astype(jnp.bfloat16),
    )


def turn(number, cos, sin):
    real, imag = number
    if abs(sin) < 1e-9:
        return (real, imag) if cos > 0 else (-real, -imag)
    if abs(cos) < 1e-9:
        return (imag, -real) if sin > 0 else (-imag, real)
    return (real * cos + imag * sin, imag * cos - real * sin)


def add(left, right):
    return (left[0] + right[0], left[1] + right[1])


def sub(left, right):
    return (left[0] - right[0], left[1] - right[1])


def complex_dft(items, sign):
    count = len(items)
    if count == 1:
        return items
    half = count // 2
    low, high = items[:half], items[half:]
    even = complex_dft([add(a, b) for a, b in zip(low, high)], sign)
    odd = []
    for n, (a, b) in enumerate(zip(low, high)):
        angle = 2.0 * math.pi * n / count
        odd.append(turn(sub(a, b), math.cos(angle), sign * math.sin(angle)))
    odd = complex_dft(odd, sign)
    return [item for pair in zip(even, odd) for item in pair]


def odd_outputs(items, period):
    quarter = len(items) // 2
    turned = []
    for n in range(quarter):
        angle = 2.0 * math.pi * n / period
        turned.append(turn((items[n], -items[n + quarter]), math.cos(angle), math.sin(angle)))
    found = {}
    for m, (real, imag) in enumerate(complex_dft(turned, 1)):
        freq = 4 * m + 1
        if freq > period // 2:
            freq, imag = period - freq, -imag
        found[freq] = (real, imag)
    return found


def real_dft(items):
    count = len(items)
    if count == 1:
        return {0: (items[0], None)}
    if count == 2:
        return {0: (items[0] + items[1], None), 1: (items[0] - items[1], None)}
    half = count // 2
    low, high = items[:half], items[half:]
    found = {2 * k: v for k, v in real_dft([a + b for a, b in zip(low, high)]).items()}
    found.update(odd_outputs([a - b for a, b in zip(low, high)], count))
    return found


def padded_dft(items):
    found = {2 * k: v for k, v in real_dft(items).items()}
    found.update(odd_outputs(items, 2 * len(items)))
    return found


def odd_inputs(freqs, period):
    quarter = period // 4
    items = []
    for m in range(quarter):
        freq = 4 * m + 1
        if freq > period // 2:
            real, imag = freqs[period - freq]
            items.append((real, -imag))
        else:
            items.append(freqs[freq])
    low, high = [], []
    for n, item in enumerate(complex_dft(items, -1)):
        angle = 2.0 * math.pi * n / period
        real, imag = turn(item, math.cos(angle), -math.sin(angle))
        low.append(real)
        high.append(-imag)
    return low + high


def real_inverse(freqs, count):
    if count == 1:
        return [freqs[0][0]]
    if count == 2:
        return [freqs[0][0] + freqs[1][0], freqs[0][0] - freqs[1][0]]
    even = real_inverse({k // 2: v for k, v in freqs.items() if k % 2 == 0}, count // 2)
    odd = odd_inputs(freqs, count)
    return [a + b for a, b in zip(even, odd)] + [a - b for a, b in zip(even, odd)]


def padded_inverse(freqs, count):
    even = real_inverse({k // 2: v for k, v in freqs.items() if k % 2 == 0}, count)
    return [a + b for a, b in zip(even, odd_inputs(freqs, 2 * count))]


def outer_forward(source, mid, base):
    blocks, group, width = source.shape

    def body(step, carry):
        start = pl.multiple_of(step * ROWS, ROWS)
        rows = pl.ds(start, ROWS)
        found = padded_dft([source[n, rows, :].astype(jnp.float32) for n in range(blocks)])
        out_rows = pl.ds(pl.multiple_of(start + base, ROWS), ROWS)
        for freq, (real, imag) in found.items():
            if imag is None:
                imag = jnp.zeros_like(real)
            mid[freq, out_rows, 0:width] = real.astype(jnp.bfloat16)
            mid[freq, out_rows, width : 2 * width] = imag.astype(jnp.bfloat16)
        return carry

    lax.fori_loop(0, group // ROWS, body, 0)


def outer_inverse(mid, base, dest):
    blocks, group, width = dest.shape

    def body(step, carry):
        start = pl.multiple_of(step * ROWS, ROWS)
        rows = pl.ds(pl.multiple_of(start + base, ROWS), ROWS)
        freqs = {
            k: (mid[k, rows, 0:width], mid[k, rows, width : 2 * width]) for k in range(blocks + 1)
        }
        for n, item in enumerate(padded_inverse(freqs, blocks)):
            dest[n, pl.ds(start, ROWS), :] = item.astype(dest.dtype)
        return carry

    lax.fori_loop(0, group // ROWS, body, 0)


def product(left, right, width, conjugate):
    left_real, left_imag = left[:, :width], left[:, width:]
    right_real, right_imag = right[:, :width], right[:, width:]
    if conjugate:
        left_imag = -left_imag
    real = left_real * right_real - left_imag * right_imag
    imag = left_real * right_imag + left_imag * right_real
    return jnp.concatenate([real.astype(jnp.bfloat16), imag.astype(jnp.bfloat16)], 1)


def pack_kernel(nseq, grad_out, gate, value, taps, *parts):
    here = lax.axis_index("seq")
    group = value.shape[0] // nseq
    for mask, part in zip(mask_order(nseq), parts):
        rows = pl.ds(pl.multiple_of((here ^ mask) * group, ROWS), group)
        part[0] = value[rows, :]
        part[1] = taps[rows, :]
        part[2] = (grad_out[rows, :].astype(jnp.float32) * gate[rows, :].astype(jnp.float32)).astype(
            jnp.bfloat16
        )


def main_kernel(nseq, ndp, factor, *refs):
    parts, refs = refs[:nseq], refs[nseq:]
    forward, inverse = refs[:2]
    outs, refs = refs[2 : 2 + nseq], refs[2 + nseq :]
    sums, refs = refs[:ndp], refs[ndp:]
    signals, results, cross, mid, back = refs
    here = lax.axis_index("seq")
    here_dp = lax.axis_index("dp")
    blocks, group, width = cross.shape
    for mask, part in zip(mask_order(nseq), parts):
        for which in range(3):
            signals[which, here ^ mask] = part[which]
    for which in range(3):
        outer_forward(signals.at[which], mid, which * group)

    def body(k, carry):
        spec = jnp.dot(mid[k], forward[k], preferred_element_type=jnp.float32)
        value, taps, gated = spec[:group], spec[group : 2 * group], spec[2 * group :]
        three = jnp.concatenate(
            [
                product(taps, value, width, False),
                product(taps, gated, width, True),
                product(value, gated, width, True),
            ],
            0,
        )
        back[k] = jnp.dot(three, inverse[k], preferred_element_type=jnp.float32)
        return carry

    lax.fori_loop(0, blocks + 1, body, 0)
    outer_inverse(back, 0, results.at[0])
    outer_inverse(back, group, results.at[1])
    outer_inverse(back, 2 * group, cross)
    for mask, out in zip(mask_order(nseq), outs):
        for which in range(2):
            out[which] = results[which, here ^ mask]
    share = blocks // ndp
    for step, total in enumerate(sums):
        first = lax.rem(here_dp + step, ndp) * share
        for n in range(share):
            total[:, n * width : (n + 1) * width] = cross[first + n] * factor


def unpack_kernel(nseq, ndp, *refs):
    parts, refs = refs[:nseq], refs[nseq:]
    sums, refs = refs[:ndp], refs[ndp:]
    grad_out, grad_gate, grad_value, grad_taps = refs
    here = lax.axis_index("seq")
    group = grad_out.shape[0] // nseq
    for mask, part in zip(mask_order(nseq), parts):
        rows = pl.ds(pl.multiple_of((here ^ mask) * group, ROWS), group)
        grad_gate[rows, :] = (
            grad_out[rows, :].astype(jnp.float32) * part[0].astype(jnp.float32)
        ).astype(jnp.bfloat16)
        grad_value[rows, :] = part[1]
    total = sums[0][...]
    for other in sums[1:]:
        total = total + other[...]
    grad_taps[...] = total


def vmem(count):
    return [pl.BlockSpec(memory_space=pltpu.VMEM)] * count


def call(kernel, outs, scratch, *operands):
    return pl.pallas_call(
        kernel,
        out_shape=outs,
        in_specs=vmem(len(operands)),
        out_specs=tuple(vmem(len(outs))),
        scratch_shapes=scratch,
        compiler_params=pltpu.CompilerParams(vmem_limit_bytes=40 * 1024 * 1024),
        cost_estimate=pl.CostEstimate(flops=10**9, bytes_accessed=10**7, transcendentals=0),
    )(*operands)


def mask_order(count):
    far = list(range(count - 1, count // 2 - 1, -1))
    near = list(range(count // 2 - 1, 0, -1))
    order = [0]
    while far or near:
        order += far[:2] + near[:1]
        far, near = far[2:], near[1:]
    return order


def exchange(parts):
    count = len(parts)
    return [
        lax.ppermute(part, "seq", [(i, i ^ mask) for i in range(count)]) if mask else part
        for mask, part in zip(mask_order(count), parts)
    ]


def on_device(grad_out, gate, value, filter_taps):
    nseq = lax.axis_size("seq")
    ndp = lax.axis_size("dp")
    chans = grad_out.shape[1]
    width = grad_out.shape[2]
    group = chans // nseq
    blocks = nseq
    forward, inverse = (jnp.asarray(t) for t in inner_tables(blocks, width))
    factor = 1.0 / (ndp * math.sqrt(nseq * width))
    shape = jax.ShapeDtypeStruct

    parts = call(
        functools.partial(pack_kernel, nseq),
        [shape((3, group, width), jnp.bfloat16)] * nseq,
        [],
        grad_out[0],
        gate[0],
        value[0],
        filter_taps,
    )
    parts = exchange(parts)
    outs = call(
        functools.partial(main_kernel, nseq, ndp, factor),
        [shape((2, group, width), jnp.bfloat16)] * nseq
        + [shape((group, blocks // ndp * width), jnp.float32)] * ndp,
        [
            pltpu.VMEM((3, blocks, group, width), jnp.bfloat16),
            pltpu.VMEM((2, blocks, group, width), jnp.bfloat16),
            pltpu.VMEM((blocks, group, width), jnp.float32),
            pltpu.VMEM((blocks + 1, 3 * group, 2 * width), jnp.bfloat16),
            pltpu.VMEM((blocks + 1, 3 * group, 2 * width), jnp.float32),
        ],
        *parts,
        forward,
        inverse,
    )
    sums = [outs[nseq]]
    for step in range(1, ndp):
        pairs = [(i, (i + step) % ndp) for i in range(ndp)]
        sums.append(lax.ppermute(outs[nseq + step], "dp", pairs))
    backs = exchange(outs[:nseq])
    grad_gate, grad_value, grad_taps = call(
        functools.partial(unpack_kernel, nseq, ndp),
        [shape((chans, width), jnp.bfloat16)] * 2
        + [shape((group, blocks // ndp * width), jnp.float32)],
        [],
        *backs,
        *sums,
        grad_out[0],
    )
    return (grad_gate[None], grad_value[None], grad_taps)


def solution(mesh):
    return jax.shard_map(
        on_device,
        mesh=mesh,
        in_specs=(P("dp", None, "seq"), P("dp", None, "seq"), P("dp", None, "seq"), P(None, "seq")),
        out_specs=(P("dp", None, "seq"), P("dp", None, "seq"), P("seq", "dp")),
        check_vma=False,
    )
```

```python
import functools
import math

import jax
import jax.numpy as jnp
import numpy as np
from jax import lax
from jax.experimental import pallas as pl
from jax.experimental.pallas import tpu as pltpu
from jax.sharding import PartitionSpec as P

ROWS = 16


def inner_tables(blocks, width):
    total = 2 * blocks * width
    pos = np.arange(width)
    tables = []
    for outer in range(blocks + 1):
        turns = pos[:, None] * (outer + 2 * blocks * pos[None, :]) % total
        angle = 2.0 * np.pi / total * turns
        cos, sin = np.cos(angle), np.sin(angle)
        tables.append(np.block([[cos, -sin], [sin, cos]]))
    table = np.stack(tables)
    weight = np.full((blocks + 1, 1, 1), 2.0 / total)
    weight[0] = weight[blocks] = 1.0 / total
    return (
        table.astype(jnp.bfloat16),
        (table.transpose(0, 2, 1) * weight).astype(jnp.bfloat16),
    )


def turn(number, cos, sin):
    real, imag = number
    if abs(sin) < 1e-9:
        return (real, imag) if cos > 0 else (-real, -imag)
    if abs(cos) < 1e-9:
        return (imag, -real) if sin > 0 else (-imag, real)
    return (real * cos + imag * sin, imag * cos - real * sin)


def add(left, right):
    return (left[0] + right[0], left[1] + right[1])


def sub(left, right):
    return (left[0] - right[0], left[1] - right[1])


def complex_dft(items, sign):
    count = len(items)
    if count == 1:
        return items
    half = count // 2
    low, high = items[:half], items[half:]
    even = complex_dft([add(a, b) for a, b in zip(low, high)], sign)
    odd = []
    for n, (a, b) in enumerate(zip(low, high)):
        angle = 2.0 * math.pi * n / count
        odd.append(turn(sub(a, b), math.cos(angle), sign * math.sin(angle)))
    odd = complex_dft(odd, sign)
    return [item for pair in zip(even, odd) for item in pair]


def odd_outputs(items, period):
    quarter = len(items) // 2
    turned = []
    for n in range(quarter):
        angle = 2.0 * math.pi * n / period
        turned.append(turn((items[n], -items[n + quarter]), math.cos(angle), math.sin(angle)))
    found = {}
    for m, (real, imag) in enumerate(complex_dft(turned, 1)):
        freq = 4 * m + 1
        if freq > period // 2:
            freq, imag = period - freq, -imag
        found[freq] = (real, imag)
    return found


def real_dft(items):
    count = len(items)
    if count == 1:
        return {0: (items[0], None)}
    if count == 2:
        return {0: (items[0] + items[1], None), 1: (items[0] - items[1], None)}
    half = count // 2
    low, high = items[:half], items[half:]
    found = {2 * k: v for k, v in real_dft([a + b for a, b in zip(low, high)]).items()}
    found.update(odd_outputs([a - b for a, b in zip(low, high)], count))
    return found


def padded_dft(items):
    found = {2 * k: v for k, v in real_dft(items).items()}
    found.update(odd_outputs(items, 2 * len(items)))
    return found


def odd_inputs(freqs, period):
    quarter = period // 4
    items = []
    for m in range(quarter):
        freq = 4 * m + 1
        if freq > period // 2:
            real, imag = freqs[period - freq]
            items.append((real, -imag))
        else:
            items.append(freqs[freq])
    low, high = [], []
    for n, item in enumerate(complex_dft(items, -1)):
        angle = 2.0 * math.pi * n / period
        real, imag = turn(item, math.cos(angle), -math.sin(angle))
        low.append(real)
        high.append(-imag)
    return low + high


def real_inverse(freqs, count):
    if count == 1:
        return [freqs[0][0]]
    if count == 2:
        return [freqs[0][0] + freqs[1][0], freqs[0][0] - freqs[1][0]]
    even = real_inverse({k // 2: v for k, v in freqs.items() if k % 2 == 0}, count // 2)
    odd = odd_inputs(freqs, count)
    return [a + b for a, b in zip(even, odd)] + [a - b for a, b in zip(even, odd)]


def padded_inverse(freqs, count):
    even = real_inverse({k // 2: v for k, v in freqs.items() if k % 2 == 0}, count)
    return [a + b for a, b in zip(even, odd_inputs(freqs, 2 * count))]


def outer_forward(source, mid, base):
    blocks, group, width = source.shape

    def body(step, carry):
        start = pl.multiple_of(step * ROWS, ROWS)
        rows = pl.ds(start, ROWS)
        found = padded_dft([source[n, rows, :].astype(jnp.float32) for n in range(blocks)])
        out_rows = pl.ds(pl.multiple_of(start + base, ROWS), ROWS)
        for freq, (real, imag) in found.items():
            if imag is None:
                imag = jnp.zeros_like(real)
            mid[freq, out_rows, 0:width] = real.astype(jnp.bfloat16)
            mid[freq, out_rows, width : 2 * width] = imag.astype(jnp.bfloat16)
        return carry

    lax.fori_loop(0, group // ROWS, body, 0)


def outer_inverse(mid, base, dest):
    blocks, group, width = dest.shape

    def body(step, carry):
        start = pl.multiple_of(step * ROWS, ROWS)
        rows = pl.ds(pl.multiple_of(start + base, ROWS), ROWS)
        freqs = {
            k: (mid[k, rows, 0:width], mid[k, rows, width : 2 * width]) for k in range(blocks + 1)
        }
        for n, item in enumerate(padded_inverse(freqs, blocks)):
            dest[n, pl.ds(start, ROWS), :] = item.astype(dest.dtype)
        return carry

    lax.fori_loop(0, group // ROWS, body, 0)


def product(left, right, width, conjugate):
    left_real, left_imag = left[:, :width], left[:, width:]
    right_real, right_imag = right[:, :width], right[:, width:]
    if conjugate:
        left_imag = -left_imag
    real = left_real * right_real - left_imag * right_imag
    imag = left_real * right_imag + left_imag * right_real
    return jnp.concatenate([real.astype(jnp.bfloat16), imag.astype(jnp.bfloat16)], 1)


def place(inner):
    here = lax.axis_index("seq")
    return here // inner, lax.rem(here, inner)


def pack_kernel(inner, outer, group, source, *refs):
    parts, sems = refs[:inner], refs[inner]
    rows = parts[0].shape[1]
    _, low = place(inner)
    first = lax.axis_index("dp") * rows if rows < group else 0
    copies = []
    for mask, part in enumerate(parts):
        for plane in range(outer):
            start = pl.multiple_of((plane * inner + (low ^ mask)) * group + first, ROWS)
            copies.append(
                pltpu.make_async_copy(
                    source.at[pl.ds(start, rows), :], part.at[plane], sems.at[mask, plane]
                )
            )
            copies[-1].start()
    for copy in copies:
        copy.wait()


def gated_kernel(inner, outer, grad_out, gate, *refs):
    parts, (left, right, sems) = refs[:inner], refs[inner:]
    group = parts[0].shape[1]
    _, low = place(inner)
    copies = []
    for mask in range(inner):
        for plane in range(outer):
            start = pl.multiple_of((plane * inner + (low ^ mask)) * group, ROWS)
            rows = pl.ds(start, group)
            pair = [
                pltpu.make_async_copy(
                    source.at[rows, :], held.at[mask, plane], sems.at[which, mask, plane]
                )
                for which, (source, held) in enumerate(((grad_out, left), (gate, right)))
            ]
            for copy in pair:
                copy.start()
            copies.append(pair)
    for mask, part in enumerate(parts):
        for plane in range(outer):
            for copy in copies[mask * outer + plane]:
                copy.wait()
            part[plane] = (
                left[mask, plane].astype(jnp.float32) * right[mask, plane].astype(jnp.float32)
            ).astype(jnp.bfloat16)


def turn_kernel(inner, outer, *refs):
    parts, outs = refs[:inner], refs[inner:]
    plane, low = place(inner)
    for mask, part in enumerate(parts):
        for far, out in enumerate(outs):
            out[low ^ mask] = part[plane ^ far]


def gather(inner, parts, signal):
    plane, _ = place(inner)
    for far, part in enumerate(parts):
        for low in range(inner):
            signal[(plane ^ far) * inner + low] = part[low]


def collect_kernel(inner, outer, *refs):
    gather(inner, refs[:outer], refs[outer])


def scatter(inner, outer, signal, outs):
    _, low = place(inner)
    for mask, out in enumerate(outs):
        for plane in range(outer):
            out[plane] = signal[plane * inner + (low ^ mask)]


def taps_kernel(shares, *refs):
    pieces, (forward, spec, signal, mid) = refs[:shares], refs[shares:]
    rows = pieces[0].shape[1]
    for step, piece in enumerate(pieces):
        if shares == 1:
            first = 0
        else:
            first = pl.multiple_of(lax.rem(lax.axis_index("dp") + shares - step, shares) * rows, ROWS)
        for n in range(piece.shape[0]):
            signal[n, pl.ds(first, rows), :] = piece[n]
    outer_forward(signal, mid, 0)

    def body(k, carry):
        spec[k] = jnp.dot(mid[k], forward[k], preferred_element_type=jnp.float32)
        return carry

    lax.fori_loop(0, mid.shape[0], body, 0)


def pair_kernel(inner, outer, conjugate, *refs):
    parts, refs = refs[:outer], refs[outer:]
    spec_taps, forward, inverse = refs[:3]
    outs, (spec, signal, mid, back) = refs[3 : 3 + inner], refs[3 + inner :]
    width = signal.shape[2]
    gather(inner, parts, signal)
    outer_forward(signal, mid, 0)

    def body(k, carry):
        here = jnp.dot(mid[k], forward[k], preferred_element_type=jnp.float32)
        spec[k] = here
        back[k] = jnp.dot(
            product(spec_taps[k], here, width, conjugate),
            inverse[k],
            preferred_element_type=jnp.float32,
        )
        return carry

    lax.fori_loop(0, mid.shape[0], body, 0)
    outer_inverse(back, 0, signal)
    scatter(inner, outer, signal, outs)


def cross_kernel(ndp, factor, spec_value, spec_gated, inverse, *refs):
    sums, (cross, back) = refs[:ndp], refs[ndp:]
    blocks, group, width = cross.shape

    def body(k, carry):
        back[k] = jnp.dot(
            product(spec_value[k], spec_gated[k], width, True),
            inverse[k],
            preferred_element_type=jnp.float32,
        )
        return carry

    lax.fori_loop(0, blocks + 1, body, 0)
    outer_inverse(back, 0, cross)
    share = blocks // ndp
    for step, total in enumerate(sums):
        first = lax.rem(lax.axis_index("dp") + step, ndp) * share
        for n in range(share):
            total[:, n * width : (n + 1) * width] = cross[first + n] * factor


def gate_kernel(inner, outer, *refs):
    parts, (grad_out, grad_gate) = refs[:outer], refs[outer:]
    group = parts[0].shape[1]
    plane, _ = place(inner)
    for far, part in enumerate(parts):
        for low in range(inner):
            start = pl.multiple_of(((plane ^ far) * inner + low) * group, ROWS)
            rows = pl.ds(start, group)
            grad_gate[rows, :] = (
                grad_out[rows, :].astype(jnp.float32) * part[low].astype(jnp.float32)
            ).astype(jnp.bfloat16)


def land_kernel(inner, outer, *refs):
    parts, (dest, sems) = refs[:outer], refs[outer:]
    group = parts[0].shape[1]
    plane, _ = place(inner)
    copies = []
    for far, part in enumerate(parts):
        for low in range(inner):
            start = pl.multiple_of(((plane ^ far) * inner + low) * group, ROWS)
            copies.append(
                pltpu.make_async_copy(part.at[low], dest.at[pl.ds(start, group), :], sems.at[far, low])
            )
            copies[-1].start()
    for copy in copies:
        copy.wait()


def vmem(count):
    return [pl.BlockSpec(memory_space=pltpu.VMEM)] * count


def anywhere(count):
    return [pl.BlockSpec(memory_space=pl.ANY)] * count


def call(kernel, outs, scratch, operands, ins=None, dests=None, mib=4, flops=10**9):
    return pl.pallas_call(
        kernel,
        out_shape=outs,
        in_specs=ins or vmem(len(operands)),
        out_specs=dests or vmem(len(outs)),
        scratch_shapes=scratch,
        compiler_params=pltpu.CompilerParams(vmem_limit_bytes=mib * 1024 * 1024),
        cost_estimate=pl.CostEstimate(flops=flops, bytes_accessed=10**6, transcendentals=0),
    )(*operands)


def permute(array, axis, target):
    count = lax.axis_size(axis)
    return lax.ppermute(array, axis, [(i, target(i)) for i in range(count)])


def on_device(grad_out, gate, value, filter_taps):
    nseq = lax.axis_size("seq")
    ndp = lax.axis_size("dp")
    chans = grad_out.shape[1]
    width = grad_out.shape[2]
    group = chans // nseq
    blocks = nseq
    inner = 1 << (nseq.bit_length() - 1) // 2
    outer = nseq // inner
    shares = ndp if group % (ndp * ROWS) == 0 else 1
    forward, inverse = (jnp.asarray(t) for t in inner_tables(blocks, width))
    factor = 1.0 / (ndp * math.sqrt(nseq * width))
    shape = jax.ShapeDtypeStruct
    bf16, f32 = jnp.bfloat16, jnp.float32

    def in_plane(parts):
        return [
            permute(part, "seq", lambda i: i ^ mask) if mask else part
            for mask, part in enumerate(parts)
        ]

    def over_planes(parts):
        rows = parts[0].shape[1]
        parts = call(
            functools.partial(turn_kernel, inner, outer),
            [shape((inner, rows, width), bf16)] * outer,
            [],
            parts,
        )
        return [
            permute(part, "seq", lambda i: i ^ (far * inner)) if far else part
            for far, part in enumerate(parts)
        ]

    def pack(source, rows):
        return call(
            functools.partial(pack_kernel, inner, outer, group),
            [shape((outer, rows, width), bf16)] * inner,
            [pltpu.SemaphoreType.DMA((inner, outer))],
            [source],
            ins=anywhere(1),
        )

    rows = group // shares
    taps_parts = over_planes(in_plane(pack(filter_taps, rows)))
    value_parts = over_planes(in_plane(pack(value[0], group)))
    gated_parts = over_planes(
        in_plane(
            call(
                functools.partial(gated_kernel, inner, outer),
                [shape((outer, group, width), bf16)] * inner,
                [pltpu.VMEM((inner, outer, group, width), bf16)] * 2
                + [pltpu.SemaphoreType.DMA((2, inner, outer))],
                [grad_out[0], gate[0]],
                ins=anywhere(2),
            )
        )
    )

    taps_mine = call(
        functools.partial(collect_kernel, inner, outer),
        [shape((blocks, rows, width), bf16)],
        [],
        taps_parts,
    )[0]
    pieces = [taps_mine]
    for step in range(1, shares):
        pieces.append(permute(taps_mine, "dp", lambda i: (i + step) % ndp))
    spec = shape((blocks + 1, group, 2 * width), f32)
    signal = pltpu.VMEM((blocks, group, width), bf16)
    mid = pltpu.VMEM((blocks + 1, group, 2 * width), bf16)
    back = pltpu.VMEM((blocks + 1, group, 2 * width), f32)
    spec_taps = call(
        functools.partial(taps_kernel, shares),
        [spec],
        [signal, mid],
        pieces + [forward],
        mib=16,
        flops=2 * 10**9,
    )[0]

    def pair(parts, conjugate):
        outs = call(
            functools.partial(pair_kernel, inner, outer, conjugate),
            [shape((outer, group, width), bf16)] * inner + [spec],
            [signal, mid, back],
            parts + [spec_taps, forward, inverse],
            mib=16,
            flops=4 * 10**9,
        )
        return outs[:inner], outs[inner]

    conv_parts, spec_value = pair(value_parts, False)
    back_conv = over_planes(in_plane(conv_parts))
    grad_parts, spec_gated = pair(gated_parts, True)
    back_grad = over_planes(in_plane(grad_parts))

    sums = call(
        functools.partial(cross_kernel, ndp, factor),
        [shape((group, blocks // ndp * width), f32)] * ndp,
        [pltpu.VMEM((blocks, group, width), f32), back],
        [spec_value, spec_gated, inverse],
        mib=16,
        flops=3 * 10**9,
    )
    grad_taps = sums[0]
    for step in range(1, ndp):
        grad_taps = grad_taps + permute(sums[step], "dp", lambda i: (i + step) % ndp)

    grad_gate = call(
        functools.partial(gate_kernel, inner, outer),
        [shape((chans, width), bf16)],
        [],
        back_conv + [grad_out[0]],
    )[0]
    grad_value = call(
        functools.partial(land_kernel, inner, outer),
        [shape((chans, width), bf16)],
        [pltpu.SemaphoreType.DMA((outer, inner))],
        back_grad,
        dests=anywhere(1),
    )[0]
    return (grad_gate[None], grad_value[None], grad_taps)


def solution(mesh):
    return jax.shard_map(
        on_device,
        mesh=mesh,
        in_specs=(P("dp", None, "seq"), P("dp", None, "seq"), P("dp", None, "seq"), P(None, "seq")),
        out_specs=(P("dp", None, "seq"), P("dp", None, "seq"), P("seq", "dp")),
        check_vma=False,
    )
```

```python
import functools
import math

import jax
import jax.numpy as jnp
import numpy as np
from jax import lax
from jax.experimental import pallas as pl
from jax.experimental.pallas import tpu as pltpu
from jax.sharding import PartitionSpec as P

ROWS = 16


def inner_tables(blocks, width):
    total = 2 * blocks * width
    pos = np.arange(width)
    tables = []
    for outer in range(blocks + 1):
        turns = pos[:, None] * (outer + 2 * blocks * pos[None, :]) % total
        angle = 2.0 * np.pi / total * turns
        cos, sin = np.cos(angle), np.sin(angle)
        tables.append(np.block([[cos, -sin], [sin, cos]]))
    table = np.stack(tables)
    weight = np.full((blocks + 1, 1, 1), 2.0 / total)
    weight[0] = weight[blocks] = 1.0 / total
    return (
        table.astype(jnp.bfloat16),
        (table.transpose(0, 2, 1) * weight).astype(jnp.bfloat16),
    )


def turn(number, cos, sin):
    real, imag = number
    if abs(sin) < 1e-9:
        return (real, imag) if cos > 0 else (-real, -imag)
    if abs(cos) < 1e-9:
        return (imag, -real) if sin > 0 else (-imag, real)
    return (real * cos + imag * sin, imag * cos - real * sin)


def add(left, right):
    return (left[0] + right[0], left[1] + right[1])


def sub(left, right):
    return (left[0] - right[0], left[1] - right[1])


def complex_dft(items, sign):
    count = len(items)
    if count == 1:
        return items
    half = count // 2
    low, high = items[:half], items[half:]
    even = complex_dft([add(a, b) for a, b in zip(low, high)], sign)
    odd = []
    for n, (a, b) in enumerate(zip(low, high)):
        angle = 2.0 * math.pi * n / count
        odd.append(turn(sub(a, b), math.cos(angle), sign * math.sin(angle)))
    odd = complex_dft(odd, sign)
    return [item for pair in zip(even, odd) for item in pair]


def odd_outputs(items, period):
    quarter = len(items) // 2
    turned = []
    for n in range(quarter):
        angle = 2.0 * math.pi * n / period
        turned.append(turn((items[n], -items[n + quarter]), math.cos(angle), math.sin(angle)))
    found = {}
    for m, (real, imag) in enumerate(complex_dft(turned, 1)):
        freq = 4 * m + 1
        if freq > period // 2:
            freq, imag = period - freq, -imag
        found[freq] = (real, imag)
    return found


def real_dft(items):
    count = len(items)
    if count == 1:
        return {0: (items[0], None)}
    if count == 2:
        return {0: (items[0] + items[1], None), 1: (items[0] - items[1], None)}
    half = count // 2
    low, high = items[:half], items[half:]
    found = {2 * k: v for k, v in real_dft([a + b for a, b in zip(low, high)]).items()}
    found.update(odd_outputs([a - b for a, b in zip(low, high)], count))
    return found


def padded_dft(items):
    found = {2 * k: v for k, v in real_dft(items).items()}
    found.update(odd_outputs(items, 2 * len(items)))
    return found


def odd_inputs(freqs, period):
    quarter = period // 4
    items = []
    for m in range(quarter):
        freq = 4 * m + 1
        if freq > period // 2:
            real, imag = freqs[period - freq]
            items.append((real, -imag))
        else:
            items.append(freqs[freq])
    low, high = [], []
    for n, item in enumerate(complex_dft(items, -1)):
        angle = 2.0 * math.pi * n / period
        real, imag = turn(item, math.cos(angle), -math.sin(angle))
        low.append(real)
        high.append(-imag)
    return low + high


def real_inverse(freqs, count):
    if count == 1:
        return [freqs[0][0]]
    if count == 2:
        return [freqs[0][0] + freqs[1][0], freqs[0][0] - freqs[1][0]]
    even = real_inverse({k // 2: v for k, v in freqs.items() if k % 2 == 0}, count // 2)
    odd = odd_inputs(freqs, count)
    return [a + b for a, b in zip(even, odd)] + [a - b for a, b in zip(even, odd)]


def padded_inverse(freqs, count):
    even = real_inverse({k // 2: v for k, v in freqs.items() if k % 2 == 0}, count)
    return [a + b for a, b in zip(even, odd_inputs(freqs, 2 * count))]


def each(count, body):
    step = max(s for s in range(1, 18) if count % s == 0)

    def several(turn_no, carry):
        for k in range(step):
            body(turn_no * step + k)
        return carry

    if step == count:
        several(0, 0)
    else:
        lax.fori_loop(0, count // step, several, 0)


def outer_forward(source, mid, base):
    blocks, group, width = source.shape

    def body(step, carry):
        start = pl.multiple_of(step * ROWS, ROWS)
        rows = pl.ds(start, ROWS)
        found = padded_dft([source[n, rows, :].astype(jnp.float32) for n in range(blocks)])
        out_rows = pl.ds(pl.multiple_of(start + base, ROWS), ROWS)
        for freq, (real, imag) in found.items():
            if imag is None:
                imag = jnp.zeros_like(real)
            mid[freq, out_rows, 0:width] = real.astype(jnp.bfloat16)
            mid[freq, out_rows, width : 2 * width] = imag.astype(jnp.bfloat16)
        return carry

    lax.fori_loop(0, group // ROWS, body, 0)


def outer_inverse(mid, base, dest):
    blocks, group, width = dest.shape

    def body(step, carry):
        start = pl.multiple_of(step * ROWS, ROWS)
        rows = pl.ds(pl.multiple_of(start + base, ROWS), ROWS)
        freqs = {
            k: (mid[k, rows, 0:width], mid[k, rows, width : 2 * width]) for k in range(blocks + 1)
        }
        for n, item in enumerate(padded_inverse(freqs, blocks)):
            dest[n, pl.ds(start, ROWS), :] = item.astype(dest.dtype)
        return carry

    lax.fori_loop(0, group // ROWS, body, 0)


def product(left, right, width, conjugate):
    left_real, left_imag = left[:, :width], left[:, width:]
    right_real, right_imag = right[:, :width], right[:, width:]
    if conjugate:
        left_imag = -left_imag
    real = left_real * right_real - left_imag * right_imag
    imag = left_real * right_imag + left_imag * right_real
    return jnp.concatenate([real.astype(jnp.bfloat16), imag.astype(jnp.bfloat16)], 1)


def place(inner):
    here = lax.axis_index("seq")
    return here // inner, lax.rem(here, inner)


def pack_kernel(inner, outer, taps, value, *refs):
    taps_parts, value_parts = refs[:inner], refs[inner : inner + outer]
    taps_sems, value_sems = refs[inner + outer :]
    group = value_parts[0].shape[1]
    plane, low = place(inner)
    copies = []
    for far, part in enumerate(value_parts):
        for there in range(inner):
            start = pl.multiple_of(((plane ^ far) * inner + there) * group, ROWS)
            source = value.at[pl.ds(start, group), :]
            copies.append(pltpu.make_async_copy(source, part.at[there], value_sems.at[far, there]))
    for mask, part in enumerate(taps_parts):
        for there in range(outer):
            start = pl.multiple_of((there * inner + (low ^ mask)) * group, ROWS)
            source = taps.at[pl.ds(start, group), :]
            copies.append(
                pltpu.make_async_copy(source, part.at[0, there], taps_sems.at[mask, there])
            )
    for copy in copies:
        copy.start()
    for copy in copies:
        copy.wait()


def gated_kernel(inner, outer, grad_out, gate, *refs):
    parts, (left, right, sems) = refs[:inner], refs[inner:]
    group = left.shape[2]
    _, low = place(inner)
    copies = []
    for mask in range(inner):
        for plane in range(outer):
            start = pl.multiple_of((plane * inner + (low ^ mask)) * group, ROWS)
            rows = pl.ds(start, group)
            pair = [
                pltpu.make_async_copy(
                    source.at[rows, :], held.at[mask, plane], sems.at[which, mask, plane]
                )
                for which, (source, held) in enumerate(((grad_out, left), (gate, right)))
            ]
            for copy in pair:
                copy.start()
            copies.append(pair)
    for mask, part in enumerate(parts):
        for plane in range(outer):
            for copy in copies[mask * outer + plane]:
                copy.wait()
            part[0, plane] = (
                left[mask, plane].astype(jnp.float32) * right[mask, plane].astype(jnp.float32)
            ).astype(jnp.bfloat16)


def turn_kernel(inner, outer, which, *refs):
    parts, outs = refs[:inner], refs[inner:]
    plane, low = place(inner)
    for mask, part in enumerate(parts):
        for far, out in enumerate(outs):
            out[low ^ mask] = part[which, plane ^ far]


def turn_back_kernel(inner, outer, *refs):
    parts, gated, outs = refs[:outer], refs[outer : outer + inner], refs[outer + inner :]
    plane, low = place(inner)
    for mask, out in enumerate(outs):
        for far, part in enumerate(parts):
            out[0, plane ^ far] = part[low ^ mask]
        out[1] = gated[mask][0]


def gather(inner, parts, signal):
    plane, _ = place(inner)
    for far, part in enumerate(parts):
        for low in range(inner):
            signal[(plane ^ far) * inner + low] = part[low]


def scatter(inner, outer, signal, outs):
    _, low = place(inner)
    for mask, out in enumerate(outs):
        for plane in range(outer):
            out[0, plane] = signal[plane * inner + (low ^ mask)]


def taps_kernel(inner, outer, *refs):
    parts, (forward, spec, signal, mid) = refs[:outer], refs[outer:]
    gather(inner, parts, signal)
    outer_forward(signal, mid, 0)

    def body(k):
        spec[k] = jnp.dot(mid[k], forward[k], preferred_element_type=jnp.float32)

    each(mid.shape[0], body)


def conv_kernel(inner, outer, *refs):
    parts, (spec_taps, forward, inverse) = refs[:inner], refs[inner : inner + 3]
    outs, (spec, signal, mid, back) = refs[inner + 3 : -4], refs[-4:]
    width = signal.shape[2]
    _, low = place(inner)
    for mask, part in enumerate(parts):
        for plane in range(outer):
            signal[plane * inner + (low ^ mask)] = part[0, plane]
    outer_forward(signal, mid, 0)

    def body(k):
        value = jnp.dot(mid[k], forward[k], preferred_element_type=jnp.float32)
        spec[k] = value
        back[k] = jnp.dot(
            product(spec_taps[k], value, width, False),
            inverse[k],
            preferred_element_type=jnp.float32,
        )

    each(mid.shape[0], body)
    outer_inverse(back, 0, signal)
    scatter(inner, outer, signal, outs)


def grad_kernel(inner, outer, ndp, factor, *refs):
    parts, (spec_taps, spec_value, forward, inverse) = refs[:outer], refs[outer : outer + 4]
    outs, sums = refs[outer + 4 : outer + 4 + inner], refs[outer + 4 + inner : -4]
    signal, cross, mid, back = refs[-4:]
    blocks, group, width = signal.shape
    gather(inner, parts, signal)
    outer_forward(signal, mid, 0)

    def body(k):
        gated = jnp.dot(mid[k], forward[k], preferred_element_type=jnp.float32)
        both = jnp.concatenate(
            [
                product(spec_taps[k], gated, width, True),
                product(spec_value[k], gated, width, True),
            ],
            0,
        )
        back[k] = jnp.dot(both, inverse[k], preferred_element_type=jnp.float32)

    each(mid.shape[0], body)
    outer_inverse(back, 0, signal)
    scatter(inner, outer, signal, outs)
    outer_inverse(back, group, cross)
    share = blocks // ndp
    for step, total in enumerate(sums):
        first = lax.rem(lax.axis_index("dp") + step, ndp) * share
        for n in range(share):
            total[:, n * width : (n + 1) * width] = (cross[first + n] * factor).astype(total.dtype)


def gate_kernel(inner, outer, *refs):
    parts, grad_out, sums = refs[:outer], refs[outer], refs[outer + 1 : -2]
    grad_gate, grad_taps = refs[-2:]
    total = sums[0][...]
    for other in sums[1:]:
        total = total + other[...].astype(jnp.float32)
    grad_taps[...] = total
    group = parts[0].shape[1]
    plane, _ = place(inner)
    for far, part in enumerate(parts):
        for low in range(inner):
            start = pl.multiple_of(((plane ^ far) * inner + low) * group, ROWS)
            rows = pl.ds(start, group)
            grad_gate[rows, :] = (
                grad_out[rows, :].astype(jnp.float32) * part[low].astype(jnp.float32)
            ).astype(jnp.bfloat16)


def land_kernel(inner, outer, *refs):
    parts, (dest, sems) = refs[:outer], refs[outer:]
    group = parts[0].shape[1]
    plane, _ = place(inner)
    copies = []
    for far, part in enumerate(parts):
        for low in range(inner):
            start = pl.multiple_of(((plane ^ far) * inner + low) * group, ROWS)
            copies.append(
                pltpu.make_async_copy(part.at[low], dest.at[pl.ds(start, group), :], sems.at[far, low])
            )
            copies[-1].start()
    for copy in copies:
        copy.wait()


def vmem(count):
    return [pl.BlockSpec(memory_space=pltpu.VMEM)] * count


def anywhere(count):
    return [pl.BlockSpec(memory_space=pl.ANY)] * count


def call(kernel, outs, scratch, operands, ins=None, dests=None, mib=4, flops=10**9, after=()):
    count = len(operands)

    def ordered(*refs):
        kernel(*refs[len(after) :])

    return pl.pallas_call(
        ordered,
        out_shape=list(outs),
        in_specs=anywhere(len(after)) + (ins or vmem(count)),
        out_specs=dests or vmem(len(outs)),
        scratch_shapes=scratch,
        compiler_params=pltpu.CompilerParams(vmem_limit_bytes=mib * 1024 * 1024),
        cost_estimate=pl.CostEstimate(flops=flops, bytes_accessed=10**6, transcendentals=0),
        name=kernel.func.__name__,
    )(*after, *operands)


def permute(array, axis, target):
    count = lax.axis_size(axis)
    return lax.ppermute(array, axis, [(i, target(i)) for i in range(count)])


def on_device(grad_out, gate, value, filter_taps):
    nseq = lax.axis_size("seq")
    ndp = lax.axis_size("dp")
    chans = grad_out.shape[1]
    width = grad_out.shape[2]
    group = chans // nseq
    blocks = nseq
    inner = 1 << (nseq.bit_length() - 1) // 2
    outer = nseq // inner
    forward, inverse = (jnp.asarray(t) for t in inner_tables(blocks, width))
    factor = 1.0 / (ndp * math.sqrt(nseq * width))
    shape = jax.ShapeDtypeStruct
    bf16, f32 = jnp.bfloat16, jnp.float32
    by_plane = [shape((inner, group, width), bf16)] * outer
    by_low = [shape((1, outer, group, width), bf16)] * inner

    def in_plane(parts):
        return [
            permute(part, "seq", lambda i: i ^ mask) if mask else part
            for mask, part in enumerate(parts)
        ]

    def over_planes(parts):
        return [
            permute(part, "seq", lambda i: i ^ (far * inner)) if far else part
            for far, part in enumerate(parts)
        ]

    def turned(parts, which, after):
        kernel = functools.partial(turn_kernel, inner, outer, which)
        return call(kernel, by_plane, [], parts, after=after)

    packed = call(
        functools.partial(pack_kernel, inner, outer),
        by_low + by_plane,
        [pltpu.SemaphoreType.DMA((inner, outer)), pltpu.SemaphoreType.DMA((outer, inner))],
        [filter_taps, value[0]],
        ins=anywhere(2),
        mib=56,
    )
    taps_low, value_plane = in_plane(packed[:inner]), over_planes(packed[inner:])
    gated_packed = call(
        functools.partial(gated_kernel, inner, outer),
        by_low,
        [pltpu.VMEM((inner, outer, group, width), bf16)] * 2
        + [pltpu.SemaphoreType.DMA((2, inner, outer))],
        [grad_out[0], gate[0]],
        ins=anywhere(2),
        mib=16,
        after=packed[:1],
    )
    taps_turned = turned(taps_low, 0, value_plane[1:] + list(gated_packed[:1]))
    taps_plane = over_planes(taps_turned)
    both_low = in_plane(
        call(
            functools.partial(turn_back_kernel, inner, outer),
            [shape((2, outer, group, width), bf16)] * inner,
            [],
            value_plane + list(gated_packed),
            after=taps_turned[:1],
        )
    )
    gated_turned = turned(both_low, 1, taps_plane[:0:-1])
    gated_plane = over_planes(gated_turned)

    spec = shape((blocks + 1, group, 2 * width), f32)
    signal = pltpu.VMEM((blocks, group, width), bf16)
    mid = pltpu.VMEM((blocks + 1, group, 2 * width), bf16)
    spec_taps = call(
        functools.partial(taps_kernel, inner, outer),
        [spec],
        [signal, mid],
        taps_plane + [forward],
        mib=16,
        after=gated_turned[:1],
    )[0]
    outs = call(
        functools.partial(conv_kernel, inner, outer),
        by_low + [spec],
        [signal, mid, pltpu.VMEM((blocks + 1, group, 2 * width), f32)],
        both_low + [spec_taps, forward, inverse],
        mib=16,
    )
    conv_low, spec_value = in_plane(outs[:inner]), outs[inner]
    conv_turned = turned(conv_low, 0, gated_plane[1:])
    conv_plane = over_planes(conv_turned)
    wide = (group, blocks // ndp * width)
    outs = call(
        functools.partial(grad_kernel, inner, outer, ndp, factor),
        by_low + [shape(wide, f32)] + [shape(wide, bf16)] * (ndp - 1),
        [
            signal,
            pltpu.VMEM((blocks, group, width), f32),
            mid,
            pltpu.VMEM((blocks + 1, 2 * group, 2 * width), f32),
        ],
        gated_plane + [spec_taps, spec_value, forward, inverse],
        mib=24,
        after=conv_turned[:1],
    )
    sums = list(outs[inner:])
    for step in range(1, ndp):
        sums[step] = permute(sums[step], "dp", lambda i: (i + step) % ndp)
    grad_plane = over_planes(turned(in_plane(outs[:inner]), 0, conv_plane[1:]))
    grad_gate, grad_taps = call(
        functools.partial(gate_kernel, inner, outer),
        [shape((chans, width), bf16), shape(wide, f32)],
        [],
        conv_plane + [grad_out[0]] + sums,
    )
    grad_value = call(
        functools.partial(land_kernel, inner, outer),
        [shape((chans, width), bf16)],
        [pltpu.SemaphoreType.DMA((outer, inner))],
        grad_plane,
        dests=anywhere(1),
        after=[grad_gate],
    )[0]
    return (grad_gate[None], grad_value[None], grad_taps)


def solution(mesh):
    return jax.shard_map(
        on_device,
        mesh=mesh,
        in_specs=(P("dp", None, "seq"), P("dp", None, "seq"), P("dp", None, "seq"), P(None, "seq")),
        out_specs=(P("dp", None, "seq"), P("dp", None, "seq"), P("seq", "dp")),
        check_vma=False,
    )
```

```python
import functools
import math

import jax
import jax.numpy as jnp
import numpy as np
from jax import lax
from jax.experimental import pallas as pl
from jax.experimental.pallas import tpu as pltpu
from jax.sharding import PartitionSpec as P

ROWS = 16


def inner_tables(blocks, width):
    total = 2 * blocks * width
    pos = np.arange(width)
    tables = []
    for outer in range(blocks + 1):
        turns = pos[:, None] * (outer + 2 * blocks * pos[None, :]) % total
        angle = 2.0 * np.pi / total * turns
        cos, sin = np.cos(angle), np.sin(angle)
        tables.append(np.block([[cos, -sin], [sin, cos]]))
    table = np.stack(tables)
    weight = np.full((blocks + 1, 1, 1), 2.0 / total)
    weight[0] = weight[blocks] = 1.0 / total
    return (
        table.astype(jnp.bfloat16),
        (table.transpose(0, 2, 1) * weight).astype(jnp.bfloat16),
    )


def turn(number, cos, sin):
    real, imag = number
    if abs(sin) < 1e-9:
        return (real, imag) if cos > 0 else (-real, -imag)
    if abs(cos) < 1e-9:
        return (imag, -real) if sin > 0 else (-imag, real)
    return (real * cos + imag * sin, imag * cos - real * sin)


def add(left, right):
    return (left[0] + right[0], left[1] + right[1])


def sub(left, right):
    return (left[0] - right[0], left[1] - right[1])


def complex_dft(items, sign):
    count = len(items)
    if count == 1:
        return items
    half = count // 2
    low, high = items[:half], items[half:]
    even = complex_dft([add(a, b) for a, b in zip(low, high)], sign)
    odd = []
    for n, (a, b) in enumerate(zip(low, high)):
        angle = 2.0 * math.pi * n / count
        odd.append(turn(sub(a, b), math.cos(angle), sign * math.sin(angle)))
    odd = complex_dft(odd, sign)
    return [item for pair in zip(even, odd) for item in pair]


def odd_outputs(items, period):
    quarter = len(items) // 2
    turned = []
    for n in range(quarter):
        angle = 2.0 * math.pi * n / period
        turned.append(turn((items[n], -items[n + quarter]), math.cos(angle), math.sin(angle)))
    found = {}
    for m, (real, imag) in enumerate(complex_dft(turned, 1)):
        freq = 4 * m + 1
        if freq > period // 2:
            freq, imag = period - freq, -imag
        found[freq] = (real, imag)
    return found


def real_dft(items):
    count = len(items)
    if count == 1:
        return {0: (items[0], None)}
    if count == 2:
        return {0: (items[0] + items[1], None), 1: (items[0] - items[1], None)}
    half = count // 2
    low, high = items[:half], items[half:]
    found = {2 * k: v for k, v in real_dft([a + b for a, b in zip(low, high)]).items()}
    found.update(odd_outputs([a - b for a, b in zip(low, high)], count))
    return found


def padded_dft(items):
    found = {2 * k: v for k, v in real_dft(items).items()}
    found.update(odd_outputs(items, 2 * len(items)))
    return found


def odd_inputs(freqs, period):
    quarter = period // 4
    items = []
    for m in range(quarter):
        freq = 4 * m + 1
        if freq > period // 2:
            real, imag = freqs[period - freq]
            items.append((real, -imag))
        else:
            items.append(freqs[freq])
    low, high = [], []
    for n, item in enumerate(complex_dft(items, -1)):
        angle = 2.0 * math.pi * n / period
        real, imag = turn(item, math.cos(angle), -math.sin(angle))
        low.append(real)
        high.append(-imag)
    return low + high


def real_inverse(freqs, count):
    if count == 1:
        return [freqs[0][0]]
    if count == 2:
        return [freqs[0][0] + freqs[1][0], freqs[0][0] - freqs[1][0]]
    even = real_inverse({k // 2: v for k, v in freqs.items() if k % 2 == 0}, count // 2)
    odd = odd_inputs(freqs, count)
    return [a + b for a, b in zip(even, odd)] + [a - b for a, b in zip(even, odd)]


def padded_inverse(freqs, count):
    even = real_inverse({k // 2: v for k, v in freqs.items() if k % 2 == 0}, count)
    return [a + b for a, b in zip(even, odd_inputs(freqs, 2 * count))]


def each(count, body):
    step = max(s for s in range(1, 18) if count % s == 0)

    def several(turn_no, carry):
        for k in range(step):
            body(turn_no * step + k)
        return carry

    if step == count:
        several(0, 0)
    else:
        lax.fori_loop(0, count // step, several, 0)


def outer_forward(source, mid, base):
    blocks, group, width = source.shape

    def body(step, carry):
        start = pl.multiple_of(step * ROWS, ROWS)
        rows = pl.ds(start, ROWS)
        found = padded_dft([source[n, rows, :].astype(jnp.float32) for n in range(blocks)])
        out_rows = pl.ds(pl.multiple_of(start + base, ROWS), ROWS)
        for freq, (real, imag) in found.items():
            if imag is None:
                imag = jnp.zeros_like(real)
            mid[freq, out_rows, 0:width] = real.astype(jnp.bfloat16)
            mid[freq, out_rows, width : 2 * width] = imag.astype(jnp.bfloat16)
        return carry

    lax.fori_loop(0, group // ROWS, body, 0)


def outer_inverse(mid, base, dest):
    blocks, group, width = dest.shape

    def body(step, carry):
        start = pl.multiple_of(step * ROWS, ROWS)
        rows = pl.ds(pl.multiple_of(start + base, ROWS), ROWS)
        freqs = {
            k: (mid[k, rows, 0:width], mid[k, rows, width : 2 * width]) for k in range(blocks + 1)
        }
        for n, item in enumerate(padded_inverse(freqs, blocks)):
            dest[n, pl.ds(start, ROWS), :] = item.astype(dest.dtype)
        return carry

    lax.fori_loop(0, group // ROWS, body, 0)


def product(left, right, width, conjugate):
    left_real, left_imag = left[:, :width], left[:, width:]
    right_real, right_imag = right[:, :width], right[:, width:]
    if conjugate:
        left_imag = -left_imag
    real = left_real * right_real - left_imag * right_imag
    imag = left_real * right_imag + left_imag * right_real
    return jnp.concatenate([real.astype(jnp.bfloat16), imag.astype(jnp.bfloat16)], 1)


def place(inner):
    here = lax.axis_index("seq")
    return here // inner, lax.rem(here, inner)


def pack_kernel(inner, outer, *refs):
    parts, sems = refs[-1 - outer : -1], refs[-1]
    group = parts[0].shape[2]
    plane, _ = place(inner)
    copies = []
    for far, part in enumerate(parts):
        for which, source in enumerate(refs[: -1 - outer]):
            start = pl.multiple_of((plane ^ far) * inner * group, ROWS)
            for low in range(inner):
                rows = pl.ds(start + low * group, group)
                copies.append(
                    pltpu.make_async_copy(
                        source.at[rows, :], part.at[which, low], sems.at[which, far, low]
                    )
                )
    for copy in copies:
        copy.start()
    for copy in copies:
        copy.wait()


def gated_kernel(inner, outer, grad_out, gate, *refs):
    parts, (left, right, sems) = refs[:inner], refs[inner:]
    group = left.shape[2]
    _, low = place(inner)
    copies = []
    for mask in range(inner):
        for plane in range(outer):
            start = pl.multiple_of((plane * inner + (low ^ mask)) * group, ROWS)
            rows = pl.ds(start, group)
            pair = [
                pltpu.make_async_copy(
                    source.at[rows, :], held.at[mask, plane], sems.at[which, mask, plane]
                )
                for which, (source, held) in enumerate(((grad_out, left), (gate, right)))
            ]
            for copy in pair:
                copy.start()
            copies.append(pair)
    for mask, part in enumerate(parts):
        for plane in range(outer):
            for copy in copies[mask * outer + plane]:
                copy.wait()
            part[0, plane] = (
                left[mask, plane].astype(jnp.float32) * right[mask, plane].astype(jnp.float32)
            ).astype(jnp.bfloat16)


def turn_kernel(inner, outer, *refs):
    parts, outs = refs[:inner], refs[inner:]
    plane, low = place(inner)
    for mask, part in enumerate(parts):
        for far, out in enumerate(outs):
            for which in range(part.shape[0]):
                out[which, low ^ mask] = part[which, plane ^ far]


def turn_back_kernel(inner, outer, *refs):
    parts, outs = refs[:outer], refs[outer:]
    plane, low = place(inner)
    for far, part in enumerate(parts):
        for mask, out in enumerate(outs):
            for which in range(part.shape[0]):
                out[which, plane ^ far] = part[which, low ^ mask]


def gather_planes(inner, outer, parts, signal):
    plane, _ = place(inner)
    for far, part in enumerate(parts):
        for low in range(inner):
            signal[(plane ^ far) * inner + low] = part[0, low]


def gather_lows(inner, outer, parts, which, signal):
    _, low = place(inner)
    for mask, part in enumerate(parts):
        for plane in range(outer):
            signal[plane * inner + (low ^ mask)] = part[which, plane]


def scatter(inner, outer, signal, outs):
    _, low = place(inner)
    for mask, out in enumerate(outs):
        for plane in range(outer):
            out[0, plane] = signal[plane * inner + (low ^ mask)]


def taps_kernel(inner, outer, *refs):
    parts, (forward, spec, signal, mid) = refs[:inner], refs[inner:]
    gather_lows(inner, outer, parts, 1, signal)
    outer_forward(signal, mid, 0)

    def body(k):
        spec[k] = jnp.dot(mid[k], forward[k], preferred_element_type=jnp.float32)

    each(mid.shape[0], body)


def conv_kernel(inner, outer, *refs):
    parts, (spec_taps, forward, inverse) = refs[:inner], refs[inner : inner + 3]
    outs, (spec, signal, mid, back) = refs[inner + 3 : inner + 3 + outer], refs[-4:]
    width = signal.shape[2]
    gather_lows(inner, outer, parts, 0, signal)
    outer_forward(signal, mid, 0)

    def body(k):
        value = jnp.dot(mid[k], forward[k], preferred_element_type=jnp.float32)
        spec[k] = value
        back[k] = jnp.dot(
            product(spec_taps[k], value, width, False),
            inverse[k],
            preferred_element_type=jnp.float32,
        )

    each(mid.shape[0], body)
    outer_inverse(back, 0, signal)
    plane, _ = place(inner)
    for far, out in enumerate(outs):
        for low in range(inner):
            out[0, low] = signal[(plane ^ far) * inner + low]


def grad_kernel(inner, outer, ndp, factor, *refs):
    parts, (spec_taps, spec_value, forward, inverse) = refs[:outer], refs[outer : outer + 4]
    outs, sums = refs[outer + 4 : outer + 4 + inner], refs[outer + 4 + inner : -4]
    signal, cross, mid, back = refs[-4:]
    blocks, group, width = signal.shape
    gather_planes(inner, outer, parts, signal)
    outer_forward(signal, mid, 0)

    def body(k):
        gated = jnp.dot(mid[k], forward[k], preferred_element_type=jnp.float32)
        both = jnp.concatenate(
            [
                product(spec_taps[k], gated, width, True),
                product(spec_value[k], gated, width, True),
            ],
            0,
        )
        back[k] = jnp.dot(both, inverse[k], preferred_element_type=jnp.float32)

    each(mid.shape[0], body)
    outer_inverse(back, 0, signal)
    scatter(inner, outer, signal, outs)
    outer_inverse(back, group, cross)
    share = blocks // ndp
    for step, total in enumerate(sums):
        first = lax.rem(lax.axis_index("dp") + step, ndp) * share
        for n in range(share):
            total[:, n * width : (n + 1) * width] = (cross[first + n] * factor).astype(total.dtype)


def final_kernel(inner, outer, ndp, *refs):
    grad_parts, conv_parts, refs = refs[:outer], refs[outer : outer + inner], refs[outer + inner :]
    sums, refs = refs[:ndp], refs[ndp:]
    grad_out, grad_gate, grad_value, grad_taps, product_of, total, sems, sum_sem = refs
    group = product_of.shape[2]
    plane, low = place(inner)
    copies = []

    def send(source, dest, sem):
        copies.append(pltpu.make_async_copy(source, dest, sem))
        copies[-1].start()

    def rows_of(there, where):
        return pl.ds(pl.multiple_of((there * inner + where) * group, ROWS), group)

    for far, part in enumerate(grad_parts):
        for where in range(inner):
            rows = rows_of(plane ^ far, where)
            send(part.at[0, where], grad_value.at[rows, :], sems.at[0, far, where])
    total[...] = sums[0][...]
    for other in sums[1:]:
        total[...] += other[...].astype(jnp.float32)
    send(total, grad_taps, sum_sem.at[0])
    for mask, part in enumerate(conv_parts):
        for there in range(outer):
            rows = rows_of(there, low ^ mask)
            product_of[there, mask] = (
                grad_out[rows, :].astype(jnp.float32) * part[0, there].astype(jnp.float32)
            ).astype(jnp.bfloat16)
            send(product_of.at[there, mask], grad_gate.at[rows, :], sems.at[1, there, mask])
    for copy in copies:
        copy.wait()


def vmem(count):
    return [pl.BlockSpec(memory_space=pltpu.VMEM)] * count


def anywhere(count):
    return [pl.BlockSpec(memory_space=pl.ANY)] * count


def call(kernel, outs, scratch, operands, ins=None, dests=None, mib=4, flops=10**9, after=()):
    count = len(operands)

    def ordered(*refs):
        kernel(*refs[len(after) :])

    return pl.pallas_call(
        ordered,
        out_shape=list(outs),
        in_specs=anywhere(len(after)) + (ins or vmem(count)),
        out_specs=dests or vmem(len(outs)),
        scratch_shapes=scratch,
        compiler_params=pltpu.CompilerParams(vmem_limit_bytes=mib * 1024 * 1024),
        cost_estimate=pl.CostEstimate(flops=flops, bytes_accessed=10**6, transcendentals=0),
        name=kernel.func.__name__,
    )(*after, *operands)


def permute(array, axis, target):
    count = lax.axis_size(axis)
    return lax.ppermute(array, axis, [(i, target(i)) for i in range(count)])


def on_device(grad_out, gate, value, filter_taps):
    nseq = lax.axis_size("seq")
    ndp = lax.axis_size("dp")
    chans = grad_out.shape[1]
    width = grad_out.shape[2]
    group = chans // nseq
    blocks = nseq
    inner = 1 << (nseq.bit_length() - 1) // 2
    outer = nseq // inner
    forward, inverse = (jnp.asarray(t) for t in inner_tables(blocks, width))
    factor = 1.0 / (ndp * math.sqrt(nseq * width))
    shape = jax.ShapeDtypeStruct
    bf16, f32 = jnp.bfloat16, jnp.float32

    def by_plane(count=1):
        return [shape((count, inner, group, width), bf16)] * outer

    def by_low(count=1):
        return [shape((count, outer, group, width), bf16)] * inner

    def far_first(parts):
        half = outer // 2
        order = [outer - 1, *range(1, half), *range(half, outer - 1)]
        return [parts[far] for far in order]

    def in_plane(parts):
        return [
            permute(part, "seq", lambda i: i ^ mask) if mask else part
            for mask, part in enumerate(parts)
        ]

    def over_planes(parts):
        return [
            permute(part, "seq", lambda i: i ^ (far * inner)) if far else part
            for far, part in enumerate(parts)
        ]

    def turned(parts, after):
        kernel = functools.partial(turn_kernel, inner, outer)
        return call(kernel, by_plane(), [], parts, after=after)

    def turned_back(parts, count, after=()):
        kernel = functools.partial(turn_back_kernel, inner, outer)
        return call(kernel, by_low(count), [], parts, after=after)

    both_plane = over_planes(
        call(
            functools.partial(pack_kernel, inner, outer),
            by_plane(2),
            [pltpu.SemaphoreType.DMA((2, outer, inner))],
            [value[0], filter_taps],
            ins=anywhere(2),
            mib=56,
        )
    )
    gated_low = in_plane(
        call(
            functools.partial(gated_kernel, inner, outer),
            by_low(),
            [pltpu.VMEM((inner, outer, group, width), bf16)] * 2
            + [pltpu.SemaphoreType.DMA((2, inner, outer))],
            [grad_out[0], gate[0]],
            ins=anywhere(2),
            mib=16,
            after=both_plane[1:2],
        )
    )
    gated_turned = turned(gated_low, far_first(both_plane))
    gated_plane = over_planes(gated_turned)
    both_low = in_plane(turned_back(both_plane, 2, gated_turned[:1]))

    spec = shape((blocks + 1, group, 2 * width), f32)
    signal = pltpu.VMEM((blocks, group, width), bf16)
    mid = pltpu.VMEM((blocks + 1, group, 2 * width), bf16)
    spec_taps = call(
        functools.partial(taps_kernel, inner, outer),
        [spec],
        [signal, mid],
        both_low + [forward],
        mib=16,
    )[0]
    outs = call(
        functools.partial(conv_kernel, inner, outer),
        by_plane() + [spec],
        [signal, mid, pltpu.VMEM((blocks + 1, group, 2 * width), f32)],
        both_low + [spec_taps, forward, inverse],
        mib=16,
    )
    conv_plane, spec_value = over_planes(outs[:outer]), outs[outer]
    wide = (group, blocks // ndp * width)
    outs = call(
        functools.partial(grad_kernel, inner, outer, ndp, factor),
        by_low() + [shape(wide, f32)] + [shape(wide, bf16)] * (ndp - 1),
        [
            signal,
            pltpu.VMEM((blocks, group, width), f32),
            mid,
            pltpu.VMEM((blocks + 1, 2 * group, 2 * width), f32),
        ],
        gated_plane + [spec_taps, spec_value, forward, inverse],
        mib=24,
        after=far_first(gated_plane),
    )
    sums = list(outs[inner:])
    for step in range(1, ndp):
        sums[step] = permute(sums[step], "dp", lambda i: (i + step) % ndp)
    grad_turned = turned(in_plane(outs[:inner]), far_first(conv_plane))
    grad_plane = over_planes(grad_turned)
    conv_low = in_plane(turned_back(conv_plane, 1))
    grad_gate, grad_value, grad_taps = call(
        functools.partial(final_kernel, inner, outer, ndp),
        [shape((chans, width), bf16)] * 2 + [shape(wide, f32)],
        [
            pltpu.VMEM((outer, inner, group, width), bf16),
            pltpu.VMEM(wide, f32),
            pltpu.SemaphoreType.DMA((2, outer, inner)),
            pltpu.SemaphoreType.DMA((1,)),
        ],
        grad_plane + conv_low + sums + [grad_out[0]],
        dests=anywhere(3),
        mib=8,
        after=far_first(grad_plane),
    )
    return (grad_gate[None], grad_value[None], grad_taps)


def solution(mesh):
    return jax.shard_map(
        on_device,
        mesh=mesh,
        in_specs=(P("dp", None, "seq"), P("dp", None, "seq"), P("dp", None, "seq"), P(None, "seq")),
        out_specs=(P("dp", None, "seq"), P("dp", None, "seq"), P("seq", "dp")),
        check_vma=False,
    )
```

```python
import functools
import math

import jax
import jax.numpy as jnp
import numpy as np
from jax import lax
from jax.experimental import pallas as pl
from jax.experimental.pallas import tpu as pltpu
from jax.sharding import PartitionSpec as P

ROWS = 16


def inner_tables(blocks, width):
    total = 2 * blocks * width
    pos = np.arange(width)
    tables = []
    for outer in range(blocks + 1):
        turns = pos[:, None] * (outer + 2 * blocks * pos[None, :]) % total
        angle = 2.0 * np.pi / total * turns
        cos, sin = np.cos(angle), np.sin(angle)
        tables.append(np.block([[cos, -sin], [sin, cos]]))
    table = np.stack(tables)
    weight = np.full((blocks + 1, 1, 1), 2.0 / total)
    weight[0] = weight[blocks] = 1.0 / total
    return (
        table.astype(jnp.bfloat16),
        (table.transpose(0, 2, 1) * weight).astype(jnp.bfloat16),
    )


def turn(number, cos, sin):
    real, imag = number
    if abs(sin) < 1e-9:
        return (real, imag) if cos > 0 else (-real, -imag)
    if abs(cos) < 1e-9:
        return (imag, -real) if sin > 0 else (-imag, real)
    return (real * cos + imag * sin, imag * cos - real * sin)


def add(left, right):
    return (left[0] + right[0], left[1] + right[1])


def sub(left, right):
    return (left[0] - right[0], left[1] - right[1])


def complex_dft(items, sign):
    count = len(items)
    if count == 1:
        return items
    half = count // 2
    low, high = items[:half], items[half:]
    even = complex_dft([add(a, b) for a, b in zip(low, high)], sign)
    odd = []
    for n, (a, b) in enumerate(zip(low, high)):
        angle = 2.0 * math.pi * n / count
        odd.append(turn(sub(a, b), math.cos(angle), sign * math.sin(angle)))
    odd = complex_dft(odd, sign)
    return [item for pair in zip(even, odd) for item in pair]


def odd_outputs(items, period):
    quarter = len(items) // 2
    turned = []
    for n in range(quarter):
        angle = 2.0 * math.pi * n / period
        turned.append(turn((items[n], -items[n + quarter]), math.cos(angle), math.sin(angle)))
    found = {}
    for m, (real, imag) in enumerate(complex_dft(turned, 1)):
        freq = 4 * m + 1
        if freq > period // 2:
            freq, imag = period - freq, -imag
        found[freq] = (real, imag)
    return found


def real_dft(items):
    count = len(items)
    if count == 1:
        return {0: (items[0], None)}
    if count == 2:
        return {0: (items[0] + items[1], None), 1: (items[0] - items[1], None)}
    half = count // 2
    low, high = items[:half], items[half:]
    found = {2 * k: v for k, v in real_dft([a + b for a, b in zip(low, high)]).items()}
    found.update(odd_outputs([a - b for a, b in zip(low, high)], count))
    return found


def padded_dft(items):
    found = {2 * k: v for k, v in real_dft(items).items()}
    found.update(odd_outputs(items, 2 * len(items)))
    return found


def odd_inputs(freqs, period):
    quarter = period // 4
    items = []
    for m in range(quarter):
        freq = 4 * m + 1
        if freq > period // 2:
            real, imag = freqs[period - freq]
            items.append((real, -imag))
        else:
            items.append(freqs[freq])
    low, high = [], []
    for n, item in enumerate(complex_dft(items, -1)):
        angle = 2.0 * math.pi * n / period
        real, imag = turn(item, math.cos(angle), -math.sin(angle))
        low.append(real)
        high.append(-imag)
    return low + high


def real_inverse(freqs, count):
    if count == 1:
        return [freqs[0][0]]
    if count == 2:
        return [freqs[0][0] + freqs[1][0], freqs[0][0] - freqs[1][0]]
    even = real_inverse({k // 2: v for k, v in freqs.items() if k % 2 == 0}, count // 2)
    odd = odd_inputs(freqs, count)
    return [a + b for a, b in zip(even, odd)] + [a - b for a, b in zip(even, odd)]


def padded_inverse(freqs, count):
    even = real_inverse({k // 2: v for k, v in freqs.items() if k % 2 == 0}, count)
    return [a + b for a, b in zip(even, odd_inputs(freqs, 2 * count))]


def each(count, body):
    step = max(s for s in range(1, 18) if count % s == 0)

    def several(turn_no, carry):
        for k in range(step):
            body(turn_no * step + k)
        return carry

    if step == count:
        several(0, 0)
    else:
        lax.fori_loop(0, count // step, several, 0)


def outer_forward(source, mid, base):
    blocks, group, width = source.shape

    def body(step, carry):
        start = pl.multiple_of(step * ROWS, ROWS)
        rows = pl.ds(start, ROWS)
        found = padded_dft([source[n, rows, :].astype(jnp.float32) for n in range(blocks)])
        out_rows = pl.ds(pl.multiple_of(start + base, ROWS), ROWS)
        for freq, (real, imag) in found.items():
            if imag is None:
                imag = jnp.zeros_like(real)
            mid[freq, out_rows, 0:width] = real.astype(jnp.bfloat16)
            mid[freq, out_rows, width : 2 * width] = imag.astype(jnp.bfloat16)
        return carry

    lax.fori_loop(0, group // ROWS, body, 0)


def outer_inverse(mid, base, dest):
    blocks, group, width = dest.shape

    def body(step, carry):
        start = pl.multiple_of(step * ROWS, ROWS)
        rows = pl.ds(pl.multiple_of(start + base, ROWS), ROWS)
        freqs = {
            k: (mid[k, rows, 0:width], mid[k, rows, width : 2 * width]) for k in range(blocks + 1)
        }
        for n, item in enumerate(padded_inverse(freqs, blocks)):
            dest[n, pl.ds(start, ROWS), :] = item.astype(dest.dtype)
        return carry

    lax.fori_loop(0, group // ROWS, body, 0)


def product(left, right, width, conjugate):
    left_real, left_imag = left[:, :width], left[:, width:]
    right_real, right_imag = right[:, :width], right[:, width:]
    if conjugate:
        left_imag = -left_imag
    real = left_real * right_real - left_imag * right_imag
    imag = left_real * right_imag + left_imag * right_real
    return jnp.concatenate([real.astype(jnp.bfloat16), imag.astype(jnp.bfloat16)], 1)


def place(inner):
    here = lax.axis_index("seq")
    return here // inner, lax.rem(here, inner)


def ahead(plane, far, outer):
    return lax.rem(plane + far, outer)


def behind(plane, far, outer):
    return lax.rem(plane + outer - far, outer)


def pack_kernel(inner, outer, *refs):
    parts, sems = refs[-1 - outer : -1], refs[-1]
    group = parts[0].shape[2]
    plane, _ = place(inner)
    copies = []
    for far, part in enumerate(parts):
        for which, source in enumerate(refs[: -1 - outer]):
            start = pl.multiple_of(ahead(plane, far, outer) * inner * group, ROWS)
            for low in range(inner):
                rows = pl.ds(start + low * group, group)
                copies.append(
                    pltpu.make_async_copy(
                        source.at[rows, :], part.at[which, low], sems.at[which, far, low]
                    )
                )
    for copy in copies:
        copy.start()
    for copy in copies:
        copy.wait()


def gated_kernel(inner, outer, grad_out, gate, *refs):
    parts, (left, right, sems) = refs[:inner], refs[inner:]
    group = left.shape[2]
    _, low = place(inner)
    copies = []
    for mask in range(inner):
        for plane in range(outer):
            start = pl.multiple_of((plane * inner + (low ^ mask)) * group, ROWS)
            rows = pl.ds(start, group)
            pair = [
                pltpu.make_async_copy(
                    source.at[rows, :], held.at[mask, plane], sems.at[which, mask, plane]
                )
                for which, (source, held) in enumerate(((grad_out, left), (gate, right)))
            ]
            for copy in pair:
                copy.start()
            copies.append(pair)
    for mask, part in enumerate(parts):
        for plane in range(outer):
            for copy in copies[mask * outer + plane]:
                copy.wait()
            part[0, plane] = (
                left[mask, plane].astype(jnp.float32) * right[mask, plane].astype(jnp.float32)
            ).astype(jnp.bfloat16)


def turn_kernel(inner, outer, *refs):
    parts, outs = refs[:inner], refs[inner:]
    plane, low = place(inner)
    for mask, part in enumerate(parts):
        for far, out in enumerate(outs):
            for which in range(part.shape[0]):
                out[which, low ^ mask] = part[which, ahead(plane, far, outer)]


def turn_back_kernel(inner, outer, *refs):
    parts, outs = refs[:outer], refs[outer:]
    plane, low = place(inner)
    for far, part in enumerate(parts):
        for mask, out in enumerate(outs):
            for which in range(part.shape[0]):
                out[which, behind(plane, far, outer)] = part[which, low ^ mask]


def gather_planes(inner, outer, parts, signal):
    plane, _ = place(inner)
    for far, part in enumerate(parts):
        for low in range(inner):
            signal[behind(plane, far, outer) * inner + low] = part[0, low]


def gather_lows(inner, outer, parts, which, signal):
    _, low = place(inner)
    for mask, part in enumerate(parts):
        for plane in range(outer):
            signal[plane * inner + (low ^ mask)] = part[which, plane]


def scatter(inner, outer, signal, outs):
    _, low = place(inner)
    for mask, out in enumerate(outs):
        for plane in range(outer):
            out[0, plane] = signal[plane * inner + (low ^ mask)]


def taps_kernel(inner, outer, *refs):
    parts, (forward, spec, signal, mid) = refs[:inner], refs[inner:]
    gather_lows(inner, outer, parts, 1, signal)
    outer_forward(signal, mid, 0)

    def body(k):
        spec[k] = jnp.dot(mid[k], forward[k], preferred_element_type=jnp.float32)

    each(mid.shape[0], body)


def conv_kernel(inner, outer, *refs):
    parts, (spec_taps, forward, inverse) = refs[:inner], refs[inner : inner + 3]
    outs, (spec, signal, mid, back) = refs[inner + 3 : inner + 3 + outer], refs[-4:]
    width = signal.shape[2]
    gather_lows(inner, outer, parts, 0, signal)
    outer_forward(signal, mid, 0)

    def body(k):
        value = jnp.dot(mid[k], forward[k], preferred_element_type=jnp.float32)
        spec[k] = value
        back[k] = jnp.dot(
            product(spec_taps[k], value, width, False),
            inverse[k],
            preferred_element_type=jnp.float32,
        )

    each(mid.shape[0], body)
    outer_inverse(back, 0, signal)
    plane, _ = place(inner)
    for far, out in enumerate(outs):
        for low in range(inner):
            out[0, low] = signal[ahead(plane, far, outer) * inner + low]


def grad_kernel(inner, outer, ndp, factor, *refs):
    parts, (spec_taps, spec_value, forward, inverse) = refs[:outer], refs[outer : outer + 4]
    outs, sums = refs[outer + 4 : outer + 4 + inner], refs[outer + 4 + inner : -4]
    signal, cross, mid, back = refs[-4:]
    blocks, group, width = signal.shape
    gather_planes(inner, outer, parts, signal)
    outer_forward(signal, mid, 0)

    def body(k):
        gated = jnp.dot(mid[k], forward[k], preferred_element_type=jnp.float32)
        both = jnp.concatenate(
            [
                product(spec_taps[k], gated, width, True),
                product(spec_value[k], gated, width, True),
            ],
            0,
        )
        back[k] = jnp.dot(both, inverse[k], preferred_element_type=jnp.float32)

    each(mid.shape[0], body)
    outer_inverse(back, 0, signal)
    scatter(inner, outer, signal, outs)
    outer_inverse(back, group, cross)
    share = blocks // ndp
    for step, total in enumerate(sums):
        first = lax.rem(lax.axis_index("dp") + step, ndp) * share
        for n in range(share):
            total[:, n * width : (n + 1) * width] = (cross[first + n] * factor).astype(total.dtype)


def final_kernel(inner, outer, ndp, *refs):
    grad_parts, conv_parts, refs = refs[:outer], refs[outer : outer + inner], refs[outer + inner :]
    sums, refs = refs[:ndp], refs[ndp:]
    grad_out, grad_gate, grad_value, grad_taps, product_of, total, sems, sum_sem = refs
    group = product_of.shape[2]
    plane, low = place(inner)
    copies = []

    def send(source, dest, sem):
        copies.append(pltpu.make_async_copy(source, dest, sem))
        copies[-1].start()

    def rows_of(there, where):
        return pl.ds(pl.multiple_of((there * inner + where) * group, ROWS), group)

    for far, part in enumerate(grad_parts):
        for where in range(inner):
            rows = rows_of(behind(plane, far, outer), where)
            send(part.at[0, where], grad_value.at[rows, :], sems.at[0, far, where])
    total[...] = sums[0][...]
    for other in sums[1:]:
        total[...] += other[...].astype(jnp.float32)
    send(total, grad_taps, sum_sem.at[0])
    for mask, part in enumerate(conv_parts):
        for there in range(outer):
            rows = rows_of(there, low ^ mask)
            product_of[there, mask] = (
                grad_out[rows, :].astype(jnp.float32) * part[0, there].astype(jnp.float32)
            ).astype(jnp.bfloat16)
            send(product_of.at[there, mask], grad_gate.at[rows, :], sems.at[1, there, mask])
    for copy in copies:
        copy.wait()


def vmem(count):
    return [pl.BlockSpec(memory_space=pltpu.VMEM)] * count


def anywhere(count):
    return [pl.BlockSpec(memory_space=pl.ANY)] * count


def call(kernel, outs, scratch, operands, ins=None, dests=None, mib=4, flops=10**9, after=()):
    count = len(operands)

    def ordered(*refs):
        kernel(*refs[len(after) :])

    return pl.pallas_call(
        ordered,
        out_shape=list(outs),
        in_specs=anywhere(len(after)) + (ins or vmem(count)),
        out_specs=dests or vmem(len(outs)),
        scratch_shapes=scratch,
        compiler_params=pltpu.CompilerParams(vmem_limit_bytes=mib * 1024 * 1024),
        cost_estimate=pl.CostEstimate(flops=flops, bytes_accessed=10**6, transcendentals=0),
        name=kernel.func.__name__,
    )(*after, *operands)


def permute(array, axis, target):
    count = lax.axis_size(axis)
    return lax.ppermute(array, axis, [(i, target(i)) for i in range(count)])


def on_device(grad_out, gate, value, filter_taps):
    nseq = lax.axis_size("seq")
    ndp = lax.axis_size("dp")
    chans = grad_out.shape[1]
    width = grad_out.shape[2]
    group = chans // nseq
    blocks = nseq
    inner = 1 << (nseq.bit_length() - 1) // 2
    outer = nseq // inner
    forward, inverse = (jnp.asarray(t) for t in inner_tables(blocks, width))
    factor = 1.0 / (ndp * math.sqrt(nseq * width))
    shape = jax.ShapeDtypeStruct
    bf16, f32 = jnp.bfloat16, jnp.float32

    def by_plane(count=1):
        return [shape((count, inner, group, width), bf16)] * outer

    def by_low(count=1):
        return [shape((count, outer, group, width), bf16)] * inner

    def arrivals(parts):
        return list(parts[1:])

    def in_plane(parts):
        return [
            permute(part, "seq", lambda i: i ^ mask) if mask else part
            for mask, part in enumerate(parts)
        ]

    def over_planes(parts):
        return [
            permute(part, "seq", lambda i: (i + far * inner) % nseq) if far else part
            for far, part in enumerate(parts)
        ]

    def turned(parts, after):
        kernel = functools.partial(turn_kernel, inner, outer)
        return call(kernel, by_plane(), [], parts, after=after)

    def turned_back(parts, count, after=()):
        kernel = functools.partial(turn_back_kernel, inner, outer)
        return call(kernel, by_low(count), [], parts, after=after)

    both_plane = over_planes(
        call(
            functools.partial(pack_kernel, inner, outer),
            by_plane(2),
            [pltpu.SemaphoreType.DMA((2, outer, inner))],
            [value[0], filter_taps],
            ins=anywhere(2),
            mib=56,
        )
    )
    gated_low = in_plane(
        call(
            functools.partial(gated_kernel, inner, outer),
            by_low(),
            [pltpu.VMEM((inner, outer, group, width), bf16)] * 2
            + [pltpu.SemaphoreType.DMA((2, inner, outer))],
            [grad_out[0], gate[0]],
            ins=anywhere(2),
            mib=16,
            after=both_plane[1:2],
        )
    )
    gated_turned = turned(gated_low, arrivals(both_plane))
    gated_plane = over_planes(gated_turned)
    both_low = in_plane(turned_back(both_plane, 2, gated_turned[:1]))

    spec = shape((blocks + 1, group, 2 * width), f32)
    signal = pltpu.VMEM((blocks, group, width), bf16)
    mid = pltpu.VMEM((blocks + 1, group, 2 * width), bf16)
    spec_taps = call(
        functools.partial(taps_kernel, inner, outer),
        [spec],
        [signal, mid],
        both_low + [forward],
        mib=16,
    )[0]
    outs = call(
        functools.partial(conv_kernel, inner, outer),
        by_plane() + [spec],
        [signal, mid, pltpu.VMEM((blocks + 1, group, 2 * width), f32)],
        both_low + [spec_taps, forward, inverse],
        mib=16,
    )
    conv_plane, spec_value = over_planes(outs[:outer]), outs[outer]
    wide = (group, blocks // ndp * width)
    outs = call(
        functools.partial(grad_kernel, inner, outer, ndp, factor),
        by_low() + [shape(wide, f32)] + [shape(wide, bf16)] * (ndp - 1),
        [
            signal,
            pltpu.VMEM((blocks, group, width), f32),
            mid,
            pltpu.VMEM((blocks + 1, 2 * group, 2 * width), f32),
        ],
        gated_plane + [spec_taps, spec_value, forward, inverse],
        mib=24,
        after=arrivals(gated_plane),
    )
    sums = list(outs[inner:])
    for step in range(1, ndp):
        sums[step] = permute(sums[step], "dp", lambda i: (i + step) % ndp)
    grad_turned = turned(in_plane(outs[:inner]), arrivals(conv_plane))
    grad_plane = over_planes(grad_turned)
    conv_low = in_plane(turned_back(conv_plane, 1))
    grad_gate, grad_value, grad_taps = call(
        functools.partial(final_kernel, inner, outer, ndp),
        [shape((chans, width), bf16)] * 2 + [shape(wide, f32)],
        [
            pltpu.VMEM((outer, inner, group, width), bf16),
            pltpu.VMEM(wide, f32),
            pltpu.SemaphoreType.DMA((2, outer, inner)),
            pltpu.SemaphoreType.DMA((1,)),
        ],
        grad_plane + conv_low + sums + [grad_out[0]],
        dests=anywhere(3),
        mib=8,
        after=arrivals(grad_plane),
    )
    return (grad_gate[None], grad_value[None], grad_taps)


def solution(mesh):
    return jax.shard_map(
        on_device,
        mesh=mesh,
        in_specs=(P("dp", None, "seq"), P("dp", None, "seq"), P("dp", None, "seq"), P(None, "seq")),
        out_specs=(P("dp", None, "seq"), P("dp", None, "seq"), P("seq", "dp")),
        check_vma=False,
    )
```

```python
import functools
import math

import jax
import jax.numpy as jnp
import numpy as np
from jax import lax
from jax.experimental import pallas as pl
from jax.experimental.pallas import tpu as pltpu
from jax.sharding import PartitionSpec as P

ROWS = 16


def inner_tables(blocks, width):
    total = 2 * blocks * width
    pos = np.arange(width)
    tables = []
    for outer in range(blocks + 1):
        turns = pos[:, None] * (outer + 2 * blocks * pos[None, :]) % total
        angle = 2.0 * np.pi / total * turns
        cos, sin = np.cos(angle), np.sin(angle)
        tables.append(np.block([[cos, -sin], [sin, cos]]))
    table = np.stack(tables)
    weight = np.full((blocks + 1, 1, 1), 2.0 / total)
    weight[0] = weight[blocks] = 1.0 / total
    return (
        table.astype(jnp.bfloat16),
        (table.transpose(0, 2, 1) * weight).astype(jnp.bfloat16),
    )


def turn(number, cos, sin):
    real, imag = number
    if abs(sin) < 1e-9:
        return (real, imag) if cos > 0 else (-real, -imag)
    if abs(cos) < 1e-9:
        return (imag, -real) if sin > 0 else (-imag, real)
    return (real * cos + imag * sin, imag * cos - real * sin)


def add(left, right):
    return (left[0] + right[0], left[1] + right[1])


def sub(left, right):
    return (left[0] - right[0], left[1] - right[1])


def complex_dft(items, sign):
    count = len(items)
    if count == 1:
        return items
    half = count // 2
    low, high = items[:half], items[half:]
    even = complex_dft([add(a, b) for a, b in zip(low, high)], sign)
    odd = []
    for n, (a, b) in enumerate(zip(low, high)):
        angle = 2.0 * math.pi * n / count
        odd.append(turn(sub(a, b), math.cos(angle), sign * math.sin(angle)))
    odd = complex_dft(odd, sign)
    return [item for pair in zip(even, odd) for item in pair]


def odd_outputs(items, period):
    quarter = len(items) // 2
    turned = []
    for n in range(quarter):
        angle = 2.0 * math.pi * n / period
        turned.append(turn((items[n], -items[n + quarter]), math.cos(angle), math.sin(angle)))
    found = {}
    for m, (real, imag) in enumerate(complex_dft(turned, 1)):
        freq = 4 * m + 1
        if freq > period // 2:
            freq, imag = period - freq, -imag
        found[freq] = (real, imag)
    return found


def real_dft(items):
    count = len(items)
    if count == 1:
        return {0: (items[0], None)}
    if count == 2:
        return {0: (items[0] + items[1], None), 1: (items[0] - items[1], None)}
    half = count // 2
    low, high = items[:half], items[half:]
    found = {2 * k: v for k, v in real_dft([a + b for a, b in zip(low, high)]).items()}
    found.update(odd_outputs([a - b for a, b in zip(low, high)], count))
    return found


def padded_dft(items):
    found = {2 * k: v for k, v in real_dft(items).items()}
    found.update(odd_outputs(items, 2 * len(items)))
    return found


def odd_inputs(freqs, period):
    quarter = period // 4
    items = []
    for m in range(quarter):
        freq = 4 * m + 1
        if freq > period // 2:
            real, imag = freqs[period - freq]
            items.append((real, -imag))
        else:
            items.append(freqs[freq])
    low, high = [], []
    for n, item in enumerate(complex_dft(items, -1)):
        angle = 2.0 * math.pi * n / period
        real, imag = turn(item, math.cos(angle), -math.sin(angle))
        low.append(real)
        high.append(-imag)
    return low + high


def real_inverse(freqs, count):
    if count == 1:
        return [freqs[0][0]]
    if count == 2:
        return [freqs[0][0] + freqs[1][0], freqs[0][0] - freqs[1][0]]
    even = real_inverse({k // 2: v for k, v in freqs.items() if k % 2 == 0}, count // 2)
    odd = odd_inputs(freqs, count)
    return [a + b for a, b in zip(even, odd)] + [a - b for a, b in zip(even, odd)]


def padded_inverse(freqs, count):
    even = real_inverse({k // 2: v for k, v in freqs.items() if k % 2 == 0}, count)
    return [a + b for a, b in zip(even, odd_inputs(freqs, 2 * count))]


def each(count, body):
    step = max(s for s in range(1, 18) if count % s == 0)

    def several(turn_no, carry):
        for k in range(step):
            body(turn_no * step + k)
        return carry

    if step == count:
        several(0, 0)
    else:
        lax.fori_loop(0, count // step, several, 0)


def outer_forward(source, mid, base):
    blocks, group, width = source.shape

    def body(step, carry):
        start = pl.multiple_of(step * ROWS, ROWS)
        rows = pl.ds(start, ROWS)
        found = padded_dft([source[n, rows, :].astype(jnp.float32) for n in range(blocks)])
        out_rows = pl.ds(pl.multiple_of(start + base, ROWS), ROWS)
        for freq, (real, imag) in found.items():
            if imag is None:
                imag = jnp.zeros_like(real)
            mid[freq, out_rows, 0:width] = real.astype(jnp.bfloat16)
            mid[freq, out_rows, width : 2 * width] = imag.astype(jnp.bfloat16)
        return carry

    lax.fori_loop(0, group // ROWS, body, 0)


def outer_inverse(mid, base, dest):
    blocks, group, width = dest.shape

    def body(step, carry):
        start = pl.multiple_of(step * ROWS, ROWS)
        rows = pl.ds(pl.multiple_of(start + base, ROWS), ROWS)
        freqs = {
            k: (mid[k, rows, 0:width], mid[k, rows, width : 2 * width]) for k in range(blocks + 1)
        }
        for n, item in enumerate(padded_inverse(freqs, blocks)):
            dest[n, pl.ds(start, ROWS), :] = item.astype(dest.dtype)
        return carry

    lax.fori_loop(0, group // ROWS, body, 0)


def product(left, right, width, conjugate):
    left_real, left_imag = left[:, :width], left[:, width:]
    right_real, right_imag = right[:, :width], right[:, width:]
    if conjugate:
        left_imag = -left_imag
    real = left_real * right_real - left_imag * right_imag
    imag = left_real * right_imag + left_imag * right_real
    return jnp.concatenate([real.astype(jnp.bfloat16), imag.astype(jnp.bfloat16)], 1)


def place(inner):
    here = lax.axis_index("seq")
    return here // inner, lax.rem(here, inner)


def pack_kernel(inner, outer, value, taps, *refs):
    value_parts, taps_parts = refs[:outer], refs[outer : outer + inner]
    value_sems, taps_sems = refs[outer + inner :]
    group = value_parts[0].shape[2]
    plane, low = place(inner)
    copies = []
    for far, part in enumerate(value_parts):
        for there in range(inner):
            start = pl.multiple_of(((plane ^ far) * inner + there) * group, ROWS)
            source = value.at[pl.ds(start, group), :]
            copies.append(
                pltpu.make_async_copy(source, part.at[0, there], value_sems.at[far, there])
            )
    for mask, part in enumerate(taps_parts):
        for there in range(outer):
            start = pl.multiple_of((there * inner + (low ^ mask)) * group, ROWS)
            source = taps.at[pl.ds(start, group), :]
            copies.append(
                pltpu.make_async_copy(source, part.at[0, there], taps_sems.at[mask, there])
            )
    for copy in copies:
        copy.start()
    for copy in copies:
        copy.wait()


def gated_kernel(inner, outer, grad_out, gate, *refs):
    parts, (left, right, sems) = refs[:inner], refs[inner:]
    group = left.shape[2]
    _, low = place(inner)
    copies = []
    for mask in range(inner):
        for plane in range(outer):
            start = pl.multiple_of((plane * inner + (low ^ mask)) * group, ROWS)
            rows = pl.ds(start, group)
            pair = [
                pltpu.make_async_copy(
                    source.at[rows, :], held.at[mask, plane], sems.at[which, mask, plane]
                )
                for which, (source, held) in enumerate(((grad_out, left), (gate, right)))
            ]
            for copy in pair:
                copy.start()
            copies.append(pair)
    for mask, part in enumerate(parts):
        for plane in range(outer):
            for copy in copies[mask * outer + plane]:
                copy.wait()
            part[0, plane] = (
                left[mask, plane].astype(jnp.float32) * right[mask, plane].astype(jnp.float32)
            ).astype(jnp.bfloat16)


def turn_kernel(inner, outer, *refs):
    parts, outs = refs[:inner], refs[inner:]
    plane, low = place(inner)
    for mask, part in enumerate(parts):
        for far, out in enumerate(outs):
            for which in range(part.shape[0]):
                out[which, low ^ mask] = part[which, plane ^ far]


def turn_back_kernel(inner, outer, *refs):
    parts, outs = refs[:outer], refs[outer:]
    plane, low = place(inner)
    for far, part in enumerate(parts):
        for mask, out in enumerate(outs):
            for which in range(part.shape[0]):
                out[which, plane ^ far] = part[which, low ^ mask]


def gather_planes(inner, outer, parts, signal):
    plane, _ = place(inner)
    for far, part in enumerate(parts):
        for low in range(inner):
            signal[(plane ^ far) * inner + low] = part[0, low]


def gather_lows(inner, outer, parts, signal):
    _, low = place(inner)
    for mask, part in enumerate(parts):
        for plane in range(outer):
            signal[plane * inner + (low ^ mask)] = part[0, plane]


def scatter(inner, outer, signal, outs):
    _, low = place(inner)
    for mask, out in enumerate(outs):
        for plane in range(outer):
            out[0, plane] = signal[plane * inner + (low ^ mask)]


def taps_kernel(inner, outer, *refs):
    parts, (forward, spec, signal, mid) = refs[:outer], refs[outer:]
    gather_planes(inner, outer, parts, signal)
    outer_forward(signal, mid, 0)

    def body(k):
        spec[k] = jnp.dot(mid[k], forward[k], preferred_element_type=jnp.float32)

    each(mid.shape[0], body)


def conv_kernel(inner, outer, *refs):
    parts, (spec_taps, forward, inverse) = refs[:inner], refs[inner : inner + 3]
    outs, (spec, signal, mid, back) = refs[inner + 3 : -4], refs[-4:]
    width = signal.shape[2]
    gather_lows(inner, outer, parts, signal)
    outer_forward(signal, mid, 0)

    def body(k):
        value = jnp.dot(mid[k], forward[k], preferred_element_type=jnp.float32)
        spec[k] = value
        back[k] = jnp.dot(
            product(spec_taps[k], value, width, False),
            inverse[k],
            preferred_element_type=jnp.float32,
        )

    each(mid.shape[0], body)
    outer_inverse(back, 0, signal)
    scatter(inner, outer, signal, outs)


def grad_kernel(inner, outer, ndp, factor, *refs):
    parts, (spec_taps, spec_value, forward, inverse) = refs[:outer], refs[outer : outer + 4]
    outs, sums = refs[outer + 4 : outer + 4 + inner], refs[outer + 4 + inner : -4]
    signal, cross, mid, back = refs[-4:]
    blocks, group, width = signal.shape
    gather_planes(inner, outer, parts, signal)
    outer_forward(signal, mid, 0)

    def body(k):
        gated = jnp.dot(mid[k], forward[k], preferred_element_type=jnp.float32)
        both = jnp.concatenate(
            [
                product(spec_taps[k], gated, width, True),
                product(spec_value[k], gated, width, True),
            ],
            0,
        )
        back[k] = jnp.dot(both, inverse[k], preferred_element_type=jnp.float32)

    each(mid.shape[0], body)
    outer_inverse(back, 0, signal)
    scatter(inner, outer, signal, outs)
    outer_inverse(back, group, cross)
    share = blocks // ndp
    for step, total in enumerate(sums):
        first = lax.rem(lax.axis_index("dp") + step, ndp) * share
        for n in range(share):
            total[:, n * width : (n + 1) * width] = (cross[first + n] * factor).astype(total.dtype)


def final_kernel(inner, outer, ndp, *refs):
    grad_parts, conv_parts, refs = refs[:outer], refs[outer : 2 * outer], refs[2 * outer :]
    sums, refs = refs[:ndp], refs[ndp:]
    grad_out, grad_gate, grad_value, grad_taps, product_of, total, sems, sum_sem = refs
    group = product_of.shape[2]
    plane, _ = place(inner)
    copies = []

    def send(source, dest, sem):
        copies.append(pltpu.make_async_copy(source, dest, sem))
        copies[-1].start()

    def rows_of(there, where):
        return pl.ds(pl.multiple_of((there * inner + where) * group, ROWS), group)

    for far, part in enumerate(grad_parts):
        for where in range(inner):
            rows = rows_of(plane ^ far, where)
            send(part.at[0, where], grad_value.at[rows, :], sems.at[0, far, where])
    total[...] = sums[0][...]
    for other in sums[1:]:
        total[...] += other[...].astype(jnp.float32)
    send(total, grad_taps, sum_sem.at[0])
    for far, part in enumerate(conv_parts):
        for where in range(inner):
            rows = rows_of(plane ^ far, where)
            product_of[far, where] = (
                grad_out[rows, :].astype(jnp.float32) * part[0, where].astype(jnp.float32)
            ).astype(jnp.bfloat16)
            send(product_of.at[far, where], grad_gate.at[rows, :], sems.at[1, far, where])
    for copy in copies:
        copy.wait()


def vmem(count):
    return [pl.BlockSpec(memory_space=pltpu.VMEM)] * count


def anywhere(count):
    return [pl.BlockSpec(memory_space=pl.ANY)] * count


def call(kernel, outs, scratch, operands, ins=None, dests=None, mib=4, flops=10**9, after=()):
    count = len(operands)

    def ordered(*refs):
        kernel(*refs[len(after) :])

    return pl.pallas_call(
        ordered,
        out_shape=list(outs),
        in_specs=anywhere(len(after)) + (ins or vmem(count)),
        out_specs=dests or vmem(len(outs)),
        scratch_shapes=scratch,
        compiler_params=pltpu.CompilerParams(vmem_limit_bytes=mib * 1024 * 1024),
        cost_estimate=pl.CostEstimate(flops=flops, bytes_accessed=10**6, transcendentals=0),
        name=kernel.func.__name__,
    )(*after, *operands)


def permute(array, axis, target):
    count = lax.axis_size(axis)
    return lax.ppermute(array, axis, [(i, target(i)) for i in range(count)])


def on_device(grad_out, gate, value, filter_taps):
    nseq = lax.axis_size("seq")
    ndp = lax.axis_size("dp")
    chans = grad_out.shape[1]
    width = grad_out.shape[2]
    group = chans // nseq
    blocks = nseq
    inner = 1 << (nseq.bit_length() - 1) // 2
    outer = nseq // inner
    forward, inverse = (jnp.asarray(t) for t in inner_tables(blocks, width))
    factor = 1.0 / (ndp * math.sqrt(nseq * width))
    shape = jax.ShapeDtypeStruct
    bf16, f32 = jnp.bfloat16, jnp.float32

    def by_plane(count=1):
        return [shape((count, inner, group, width), bf16)] * outer

    def by_low(count=1):
        return [shape((count, outer, group, width), bf16)] * inner

    def arrivals(parts, count=outer - 1):
        return [parts[far] for far in range(outer - 1, outer - 1 - count, -1)]

    def in_plane(parts):
        return [
            permute(part, "seq", lambda i: i ^ mask) if mask else part
            for mask, part in enumerate(parts)
        ]

    def over_planes(parts):
        return [
            permute(part, "seq", lambda i: i ^ (far * inner)) if far else part
            for far, part in enumerate(parts)
        ]

    def turned(parts, after):
        kernel = functools.partial(turn_kernel, inner, outer)
        return call(kernel, by_plane(), [], parts, after=after)

    packed = call(
        functools.partial(pack_kernel, inner, outer),
        by_plane() + by_low(),
        [pltpu.SemaphoreType.DMA((outer, inner)), pltpu.SemaphoreType.DMA((inner, outer))],
        [value[0], filter_taps],
        ins=anywhere(2),
        mib=56,
    )
    value_plane, taps_low = over_planes(packed[:outer]), in_plane(packed[outer:])
    gated_low = in_plane(
        call(
            functools.partial(gated_kernel, inner, outer),
            by_low(),
            [pltpu.VMEM((inner, outer, group, width), bf16)] * 2
            + [pltpu.SemaphoreType.DMA((2, inner, outer))],
            [grad_out[0], gate[0]],
            ins=anywhere(2),
            mib=16,
            after=taps_low[1:2],
        )
    )
    taps_turned = turned(taps_low, arrivals(value_plane, outer // 4))
    taps_plane = over_planes(taps_turned)
    gated_turned = turned(gated_low, arrivals(taps_plane, outer // 4))
    gated_plane = over_planes(gated_turned)
    value_low = in_plane(
        call(
            functools.partial(turn_back_kernel, inner, outer),
            by_low(),
            [],
            value_plane,
            after=list(taps_turned[:1]) + arrivals(value_plane),
        )
    )

    spec = shape((blocks + 1, group, 2 * width), f32)
    signal = pltpu.VMEM((blocks, group, width), bf16)
    mid = pltpu.VMEM((blocks + 1, group, 2 * width), bf16)
    spec_taps = call(
        functools.partial(taps_kernel, inner, outer),
        [spec],
        [signal, mid],
        taps_plane + [forward],
        mib=16,
        after=arrivals(taps_plane),
    )[0]
    outs = call(
        functools.partial(conv_kernel, inner, outer),
        by_low() + [spec],
        [signal, mid, pltpu.VMEM((blocks + 1, group, 2 * width), f32)],
        value_low + [spec_taps, forward, inverse],
        mib=16,
    )
    conv_low, spec_value = in_plane(outs[:inner]), outs[inner]
    conv_turned = turned(conv_low, arrivals(gated_plane, outer // 2))
    conv_plane = over_planes(conv_turned)
    wide = (group, blocks // ndp * width)
    outs = call(
        functools.partial(grad_kernel, inner, outer, ndp, factor),
        by_low() + [shape(wide, f32)] + [shape(wide, bf16)] * (ndp - 1),
        [
            signal,
            pltpu.VMEM((blocks, group, width), f32),
            mid,
            pltpu.VMEM((blocks + 1, 2 * group, 2 * width), f32),
        ],
        gated_plane + [spec_taps, spec_value, forward, inverse],
        mib=24,
        after=list(conv_turned[:1]) + arrivals(gated_plane),
    )
    sums = list(outs[inner:])
    for step in range(1, ndp):
        sums[step] = permute(sums[step], "dp", lambda i: (i + step) % ndp)
    grad_plane = over_planes(turned(in_plane(outs[:inner]), arrivals(conv_plane, outer // 2)))
    grad_gate, grad_value, grad_taps = call(
        functools.partial(final_kernel, inner, outer, ndp),
        [shape((chans, width), bf16)] * 2 + [shape(wide, f32)],
        [
            pltpu.VMEM((outer, inner, group, width), bf16),
            pltpu.VMEM(wide, f32),
            pltpu.SemaphoreType.DMA((2, outer, inner)),
            pltpu.SemaphoreType.DMA((1,)),
        ],
        grad_plane + conv_plane + sums + [grad_out[0]],
        dests=anywhere(3),
        mib=8,
        after=arrivals(conv_plane) + arrivals(grad_plane),
    )
    return (grad_gate[None], grad_value[None], grad_taps)


def solution(mesh):
    return jax.shard_map(
        on_device,
        mesh=mesh,
        in_specs=(P("dp", None, "seq"), P("dp", None, "seq"), P("dp", None, "seq"), P(None, "seq")),
        out_specs=(P("dp", None, "seq"), P("dp", None, "seq"), P("seq", "dp")),
        check_vma=False,
    )
```

```python
import functools
import math

import jax
import jax.numpy as jnp
import numpy as np
from jax import lax
from jax.experimental import pallas as pl
from jax.experimental.pallas import tpu as pltpu
from jax.sharding import PartitionSpec as P

ROWS = 16


def inner_tables(blocks, width):
    total = 2 * blocks * width
    pos = np.arange(width)
    tables = []
    for outer in range(blocks + 1):
        turns = pos[:, None] * (outer + 2 * blocks * pos[None, :]) % total
        angle = 2.0 * np.pi / total * turns
        cos, sin = np.cos(angle), np.sin(angle)
        tables.append(np.block([[cos, -sin], [sin, cos]]))
    table = np.stack(tables)
    weight = np.full((blocks + 1, 1, 1), 2.0 / total)
    weight[0] = weight[blocks] = 1.0 / total
    return (
        table.astype(jnp.bfloat16),
        (table.transpose(0, 2, 1) * weight).astype(jnp.bfloat16),
    )


def turn(number, cos, sin):
    real, imag = number
    if abs(sin) < 1e-9:
        return (real, imag) if cos > 0 else (-real, -imag)
    if abs(cos) < 1e-9:
        return (imag, -real) if sin > 0 else (-imag, real)
    return (real * cos + imag * sin, imag * cos - real * sin)


def add(left, right):
    return (left[0] + right[0], left[1] + right[1])


def sub(left, right):
    return (left[0] - right[0], left[1] - right[1])


def complex_dft(items, sign):
    count = len(items)
    if count == 1:
        return items
    half = count // 2
    low, high = items[:half], items[half:]
    even = complex_dft([add(a, b) for a, b in zip(low, high)], sign)
    odd = []
    for n, (a, b) in enumerate(zip(low, high)):
        angle = 2.0 * math.pi * n / count
        odd.append(turn(sub(a, b), math.cos(angle), sign * math.sin(angle)))
    odd = complex_dft(odd, sign)
    return [item for pair in zip(even, odd) for item in pair]


def odd_outputs(items, period):
    quarter = len(items) // 2
    turned = []
    for n in range(quarter):
        angle = 2.0 * math.pi * n / period
        turned.append(turn((items[n], -items[n + quarter]), math.cos(angle), math.sin(angle)))
    found = {}
    for m, (real, imag) in enumerate(complex_dft(turned, 1)):
        freq = 4 * m + 1
        if freq > period // 2:
            freq, imag = period - freq, -imag
        found[freq] = (real, imag)
    return found


def real_dft(items):
    count = len(items)
    if count == 1:
        return {0: (items[0], None)}
    if count == 2:
        return {0: (items[0] + items[1], None), 1: (items[0] - items[1], None)}
    half = count // 2
    low, high = items[:half], items[half:]
    found = {2 * k: v for k, v in real_dft([a + b for a, b in zip(low, high)]).items()}
    found.update(odd_outputs([a - b for a, b in zip(low, high)], count))
    return found


def padded_dft(items):
    found = {2 * k: v for k, v in real_dft(items).items()}
    found.update(odd_outputs(items, 2 * len(items)))
    return found


def odd_inputs(freqs, period):
    quarter = period // 4
    items = []
    for m in range(quarter):
        freq = 4 * m + 1
        if freq > period // 2:
            real, imag = freqs[period - freq]
            items.append((real, -imag))
        else:
            items.append(freqs[freq])
    low, high = [], []
    for n, item in enumerate(complex_dft(items, -1)):
        angle = 2.0 * math.pi * n / period
        real, imag = turn(item, math.cos(angle), -math.sin(angle))
        low.append(real)
        high.append(-imag)
    return low + high


def real_inverse(freqs, count):
    if count == 1:
        return [freqs[0][0]]
    if count == 2:
        return [freqs[0][0] + freqs[1][0], freqs[0][0] - freqs[1][0]]
    even = real_inverse({k // 2: v for k, v in freqs.items() if k % 2 == 0}, count // 2)
    odd = odd_inputs(freqs, count)
    return [a + b for a, b in zip(even, odd)] + [a - b for a, b in zip(even, odd)]


def padded_inverse(freqs, count):
    even = real_inverse({k // 2: v for k, v in freqs.items() if k % 2 == 0}, count)
    return [a + b for a, b in zip(even, odd_inputs(freqs, 2 * count))]


def each(count, body):
    step = max(s for s in range(1, 18) if count % s == 0)

    def several(turn_no, carry):
        for k in range(step):
            body(turn_no * step + k)
        return carry

    if step == count:
        several(0, 0)
    else:
        lax.fori_loop(0, count // step, several, 0)


def outer_forward(source, mid, base):
    blocks, group, width = source.shape

    def body(step, carry):
        start = pl.multiple_of(step * ROWS, ROWS)
        rows = pl.ds(start, ROWS)
        found = padded_dft([source[n, rows, :].astype(jnp.float32) for n in range(blocks)])
        out_rows = pl.ds(pl.multiple_of(start + base, ROWS), ROWS)
        for freq, (real, imag) in found.items():
            if imag is None:
                imag = jnp.zeros_like(real)
            mid[freq, out_rows, 0:width] = real.astype(jnp.bfloat16)
            mid[freq, out_rows, width : 2 * width] = imag.astype(jnp.bfloat16)
        return carry

    lax.fori_loop(0, group // ROWS, body, 0)


def outer_inverse(mid, base, dest):
    blocks, group, width = dest.shape

    def body(step, carry):
        start = pl.multiple_of(step * ROWS, ROWS)
        rows = pl.ds(pl.multiple_of(start + base, ROWS), ROWS)
        freqs = {
            k: (mid[k, rows, 0:width], mid[k, rows, width : 2 * width]) for k in range(blocks + 1)
        }
        for n, item in enumerate(padded_inverse(freqs, blocks)):
            dest[n, pl.ds(start, ROWS), :] = item.astype(dest.dtype)
        return carry

    lax.fori_loop(0, group // ROWS, body, 0)


def product(left, right, width, conjugate):
    left_real, left_imag = left[:, :width], left[:, width:]
    right_real, right_imag = right[:, :width], right[:, width:]
    if conjugate:
        left_imag = -left_imag
    real = left_real * right_real - left_imag * right_imag
    imag = left_real * right_imag + left_imag * right_real
    return jnp.concatenate([real.astype(jnp.bfloat16), imag.astype(jnp.bfloat16)], 1)


def place(inner):
    here = lax.axis_index("seq")
    return here // inner, lax.rem(here, inner)


def pack_planes_kernel(inner, outer, source, *refs):
    parts, sems = refs[:outer], refs[outer]
    group = parts[0].shape[2]
    plane, _ = place(inner)
    copies = []
    for far in range(outer - 1, -1, -1):
        for low in range(inner):
            start = pl.multiple_of(((plane ^ far) * inner + low) * group, ROWS)
            rows = source.at[pl.ds(start, group), :]
            copies.append(pltpu.make_async_copy(rows, parts[far].at[0, low], sems.at[far, low]))
            copies[-1].start()
    for copy in copies:
        copy.wait()


def pack_lows_kernel(inner, outer, source, *refs):
    parts, sems = refs[:inner], refs[inner]
    group = parts[0].shape[2]
    _, low = place(inner)
    copies = []
    for mask, part in enumerate(parts):
        for plane in range(outer):
            start = pl.multiple_of((plane * inner + (low ^ mask)) * group, ROWS)
            rows = source.at[pl.ds(start, group), :]
            copies.append(pltpu.make_async_copy(rows, part.at[0, plane], sems.at[mask, plane]))
            copies[-1].start()
    for copy in copies:
        copy.wait()


def gated_kernel(inner, outer, grad_out, gate, *refs):
    parts, (left, right, sems) = refs[:inner], refs[inner:]
    group = left.shape[2]
    _, low = place(inner)
    copies = []
    for mask in range(inner):
        for plane in range(outer):
            start = pl.multiple_of((plane * inner + (low ^ mask)) * group, ROWS)
            rows = pl.ds(start, group)
            pair = [
                pltpu.make_async_copy(
                    source.at[rows, :], held.at[mask, plane], sems.at[which, mask, plane]
                )
                for which, (source, held) in enumerate(((grad_out, left), (gate, right)))
            ]
            for copy in pair:
                copy.start()
            copies.append(pair)
    for mask, part in enumerate(parts):
        for plane in range(outer):
            for copy in copies[mask * outer + plane]:
                copy.wait()
            part[0, plane] = (
                left[mask, plane].astype(jnp.float32) * right[mask, plane].astype(jnp.float32)
            ).astype(jnp.bfloat16)


def turn_kernel(inner, fars, *refs):
    parts, outs = refs[:inner], refs[inner:]
    plane, low = place(inner)
    for mask, part in enumerate(parts):
        for far, out in zip(fars, outs):
            for which in range(part.shape[0]):
                out[which, low ^ mask] = part[which, plane ^ far]


def turn_back_kernel(inner, outer, *refs):
    parts, outs = refs[:outer], refs[outer:]
    plane, low = place(inner)
    for far, part in enumerate(parts):
        for mask, out in enumerate(outs):
            for which in range(part.shape[0]):
                out[which, plane ^ far] = part[which, low ^ mask]


def gather_planes(inner, outer, parts, signal):
    plane, _ = place(inner)
    for far, part in enumerate(parts):
        for low in range(inner):
            signal[(plane ^ far) * inner + low] = part[0, low]


def gather_lows(inner, outer, parts, signal):
    _, low = place(inner)
    for mask, part in enumerate(parts):
        for plane in range(outer):
            signal[plane * inner + (low ^ mask)] = part[0, plane]


def scatter(inner, outer, signal, outs):
    _, low = place(inner)
    for mask, out in enumerate(outs):
        for plane in range(outer):
            out[0, plane] = signal[plane * inner + (low ^ mask)]


def taps_kernel(inner, outer, *refs):
    parts, (forward, spec, signal, mid) = refs[:outer], refs[outer:]
    gather_planes(inner, outer, parts, signal)
    outer_forward(signal, mid, 0)

    def body(k):
        spec[k] = jnp.dot(mid[k], forward[k], preferred_element_type=jnp.float32)

    each(mid.shape[0], body)


def conv_kernel(inner, outer, *refs):
    parts, (spec_taps, forward, inverse) = refs[:inner], refs[inner : inner + 3]
    outs, (spec, signal, mid, back) = refs[inner + 3 : -4], refs[-4:]
    width = signal.shape[2]
    gather_lows(inner, outer, parts, signal)
    outer_forward(signal, mid, 0)

    def body(k):
        value = jnp.dot(mid[k], forward[k], preferred_element_type=jnp.float32)
        spec[k] = value
        back[k] = jnp.dot(
            product(spec_taps[k], value, width, False),
            inverse[k],
            preferred_element_type=jnp.float32,
        )

    each(mid.shape[0], body)
    outer_inverse(back, 0, signal)
    scatter(inner, outer, signal, outs)


def grad_kernel(inner, outer, ndp, factor, *refs):
    parts, (spec_taps, spec_value, forward, inverse) = refs[:outer], refs[outer : outer + 4]
    outs, sums = refs[outer + 4 : outer + 4 + inner], refs[outer + 4 + inner : -4]
    signal, cross, mid, back = refs[-4:]
    blocks, group, width = signal.shape
    gather_planes(inner, outer, parts, signal)
    outer_forward(signal, mid, 0)

    def body(k):
        gated = jnp.dot(mid[k], forward[k], preferred_element_type=jnp.float32)
        both = jnp.concatenate(
            [
                product(spec_taps[k], gated, width, True),
                product(spec_value[k], gated, width, True),
            ],
            0,
        )
        back[k] = jnp.dot(both, inverse[k], preferred_element_type=jnp.float32)

    each(mid.shape[0], body)
    outer_inverse(back, 0, signal)
    scatter(inner, outer, signal, outs)
    outer_inverse(back, group, cross)
    share = blocks // ndp
    for step, total in enumerate(sums):
        first = lax.rem(lax.axis_index("dp") + step, ndp) * share
        for n in range(share):
            total[:, n * width : (n + 1) * width] = (cross[first + n] * factor).astype(total.dtype)


def final_kernel(inner, outer, ndp, *refs):
    grad_parts, conv_parts, refs = refs[:outer], refs[outer : 2 * outer], refs[2 * outer :]
    sums, refs = refs[:ndp], refs[ndp:]
    grad_out, grad_gate, grad_value, grad_taps, product_of, total, sems, sum_sem = refs
    group = product_of.shape[2]
    plane, _ = place(inner)
    copies = []

    def send(source, dest, sem):
        copies.append(pltpu.make_async_copy(source, dest, sem))
        copies[-1].start()

    def rows_of(there, where):
        return pl.ds(pl.multiple_of((there * inner + where) * group, ROWS), group)

    for far, part in enumerate(grad_parts):
        for where in range(inner):
            rows = rows_of(plane ^ far, where)
            send(part.at[0, where], grad_value.at[rows, :], sems.at[0, far, where])
    total[...] = sums[0][...]
    for other in sums[1:]:
        total[...] += other[...].astype(jnp.float32)
    send(total, grad_taps, sum_sem.at[0])
    for far, part in enumerate(conv_parts):
        for where in range(inner):
            rows = rows_of(plane ^ far, where)
            product_of[far, where] = (
                grad_out[rows, :].astype(jnp.float32) * part[0, where].astype(jnp.float32)
            ).astype(jnp.bfloat16)
            send(product_of.at[far, where], grad_gate.at[rows, :], sems.at[1, far, where])
    for copy in copies:
        copy.wait()


def vmem(count):
    return [pl.BlockSpec(memory_space=pltpu.VMEM)] * count


def anywhere(count):
    return [pl.BlockSpec(memory_space=pl.ANY)] * count


def call(kernel, outs, scratch, operands, ins=None, dests=None, mib=4, flops=10**9, after=()):
    count = len(operands)

    def ordered(*refs):
        kernel(*refs[len(after) :])

    return pl.pallas_call(
        ordered,
        out_shape=list(outs),
        in_specs=anywhere(len(after)) + (ins or vmem(count)),
        out_specs=dests or vmem(len(outs)),
        scratch_shapes=scratch,
        compiler_params=pltpu.CompilerParams(vmem_limit_bytes=mib * 1024 * 1024),
        cost_estimate=pl.CostEstimate(flops=flops, bytes_accessed=10**6, transcendentals=0),
        name=kernel.func.__name__,
    )(*after, *operands)


def permute(array, axis, target):
    count = lax.axis_size(axis)
    return lax.ppermute(array, axis, [(i, target(i)) for i in range(count)])


def on_device(grad_out, gate, value, filter_taps):
    nseq = lax.axis_size("seq")
    ndp = lax.axis_size("dp")
    chans = grad_out.shape[1]
    width = grad_out.shape[2]
    group = chans // nseq
    blocks = nseq
    inner = 1 << (nseq.bit_length() - 1) // 2
    outer = nseq // inner
    forward, inverse = (jnp.asarray(t) for t in inner_tables(blocks, width))
    factor = 1.0 / (ndp * math.sqrt(nseq * width))
    shape = jax.ShapeDtypeStruct
    bf16, f32 = jnp.bfloat16, jnp.float32

    def by_plane(count=1):
        return [shape((count, inner, group, width), bf16)] * outer

    def by_low(count=1):
        return [shape((count, outer, group, width), bf16)] * inner

    def arrivals(parts, count=outer - 1):
        return [parts[far] for far in range(outer - 1, outer - 1 - count, -1)]

    def in_plane(parts):
        return [
            permute(part, "seq", lambda i: i ^ mask) if mask else part
            for mask, part in enumerate(parts)
        ]

    def over_planes(parts):
        return [
            permute(part, "seq", lambda i: i ^ (far * inner)) if far else part
            for far, part in enumerate(parts)
        ]

    def turned(parts, *steps):
        found = {}
        for fars, after in steps:
            kernel = functools.partial(turn_kernel, inner, fars)
            outs = call(kernel, by_plane()[: len(fars)], [], parts, after=list(after))
            found.update(zip(fars, outs))
        return [found[far] for far in range(outer)]

    everywhere = tuple(range(outer))
    lately = tuple(range(outer // 2, outer - 1))
    early = tuple(far for far in everywhere if far not in lately)

    value_packed = call(
        functools.partial(pack_planes_kernel, inner, outer),
        by_plane(),
        [pltpu.SemaphoreType.DMA((outer, inner))],
        [value[0]],
        ins=anywhere(1),
        mib=56,
    )
    taps_packed = call(
        functools.partial(pack_lows_kernel, inner, outer),
        by_low(),
        [pltpu.SemaphoreType.DMA((inner, outer))],
        [filter_taps],
        ins=anywhere(1),
        mib=56,
        after=value_packed[:1],
    )
    value_plane, taps_low = over_planes(value_packed), in_plane(taps_packed)
    gated_low = in_plane(
        call(
            functools.partial(gated_kernel, inner, outer),
            by_low(),
            [pltpu.VMEM((inner, outer, group, width), bf16)] * 2
            + [pltpu.SemaphoreType.DMA((2, inner, outer))],
            [grad_out[0], gate[0]],
            ins=anywhere(2),
            mib=48,
            after=taps_low[1:2],
        )
    )
    taps_turned = turned(taps_low, (everywhere, arrivals(value_plane, outer // 4)))
    taps_plane = over_planes(taps_turned)
    value_low = in_plane(
        call(
            functools.partial(turn_back_kernel, inner, outer),
            by_low(),
            [],
            value_plane,
            after=list(taps_turned[:1]) + arrivals(value_plane),
        )
    )

    spec = shape((blocks + 1, group, 2 * width), f32)
    signal = pltpu.VMEM((blocks, group, width), bf16)
    mid = pltpu.VMEM((blocks + 1, group, 2 * width), bf16)
    spec_taps = call(
        functools.partial(taps_kernel, inner, outer),
        [spec],
        [signal, mid],
        taps_plane + [forward],
        mib=16,
        after=arrivals(taps_plane),
    )[0]
    gated_turned = turned(gated_low, (early, arrivals(taps_plane, outer // 4)), (lately, [spec_taps]))
    gated_plane = over_planes(gated_turned)
    outs = call(
        functools.partial(conv_kernel, inner, outer),
        by_low() + [spec],
        [signal, mid, pltpu.VMEM((blocks + 1, group, 2 * width), f32)],
        value_low + [spec_taps, forward, inverse],
        mib=16,
    )
    conv_low, spec_value = in_plane(outs[:inner]), outs[inner]
    wide = (group, blocks // ndp * width)
    outs = call(
        functools.partial(grad_kernel, inner, outer, ndp, factor),
        by_low() + [shape(wide, f32)] + [shape(wide, bf16)] * (ndp - 1),
        [
            signal,
            pltpu.VMEM((blocks, group, width), f32),
            mid,
            pltpu.VMEM((blocks + 1, 2 * group, 2 * width), f32),
        ],
        gated_plane + [spec_taps, spec_value, forward, inverse],
        mib=24,
        after=arrivals(gated_plane),
    )
    sums = list(outs[inner:])
    for step in range(1, ndp):
        sums[step] = permute(sums[step], "dp", lambda i: (i + step) % ndp)
    conv_turned = turned(conv_low, (everywhere, outs[:1]))
    conv_plane = over_planes(conv_turned)
    grad_plane = over_planes(turned(in_plane(outs[:inner]), (everywhere, arrivals(conv_plane, outer // 2))))
    grad_gate, grad_value, grad_taps = call(
        functools.partial(final_kernel, inner, outer, ndp),
        [shape((chans, width), bf16)] * 2 + [shape(wide, f32)],
        [
            pltpu.VMEM((outer, inner, group, width), bf16),
            pltpu.VMEM(wide, f32),
            pltpu.SemaphoreType.DMA((2, outer, inner)),
            pltpu.SemaphoreType.DMA((1,)),
        ],
        grad_plane + conv_plane + sums + [grad_out[0]],
        dests=anywhere(3),
        mib=8,
        after=arrivals(conv_plane) + arrivals(grad_plane),
    )
    return (grad_gate[None], grad_value[None], grad_taps)


def solution(mesh):
    return jax.shard_map(
        on_device,
        mesh=mesh,
        in_specs=(P("dp", None, "seq"), P("dp", None, "seq"), P("dp", None, "seq"), P(None, "seq")),
        out_specs=(P("dp", None, "seq"), P("dp", None, "seq"), P("seq", "dp")),
        check_vma=False,
    )
```

```python
import functools
import math

import jax
import jax.numpy as jnp
import numpy as np
from jax import lax
from jax.experimental import pallas as pl
from jax.experimental.pallas import tpu as pltpu
from jax.sharding import PartitionSpec as P

ROWS = 16


def inner_tables(blocks, width):
    total = 2 * blocks * width
    pos = np.arange(width)
    tables = []
    for outer in range(blocks + 1):
        turns = pos[:, None] * (outer + 2 * blocks * pos[None, :]) % total
        angle = 2.0 * np.pi / total * turns
        cos, sin = np.cos(angle), np.sin(angle)
        tables.append(np.block([[cos, -sin], [sin, cos]]))
    table = np.stack(tables)
    weight = np.full((blocks + 1, 1, 1), 2.0 / total)
    weight[0] = weight[blocks] = 1.0 / total
    return (
        table.astype(jnp.bfloat16),
        (table.transpose(0, 2, 1) * weight).astype(jnp.bfloat16),
    )


def turn(number, cos, sin):
    real, imag = number
    if abs(sin) < 1e-9:
        return (real, imag) if cos > 0 else (-real, -imag)
    if abs(cos) < 1e-9:
        return (imag, -real) if sin > 0 else (-imag, real)
    return (real * cos + imag * sin, imag * cos - real * sin)


def add(left, right):
    return (left[0] + right[0], left[1] + right[1])


def sub(left, right):
    return (left[0] - right[0], left[1] - right[1])


def complex_dft(items, sign):
    count = len(items)
    if count == 1:
        return items
    half = count // 2
    low, high = items[:half], items[half:]
    even = complex_dft([add(a, b) for a, b in zip(low, high)], sign)
    odd = []
    for n, (a, b) in enumerate(zip(low, high)):
        angle = 2.0 * math.pi * n / count
        odd.append(turn(sub(a, b), math.cos(angle), sign * math.sin(angle)))
    odd = complex_dft(odd, sign)
    return [item for pair in zip(even, odd) for item in pair]


def odd_outputs(items, period):
    quarter = len(items) // 2
    turned = []
    for n in range(quarter):
        angle = 2.0 * math.pi * n / period
        turned.append(turn((items[n], -items[n + quarter]), math.cos(angle), math.sin(angle)))
    found = {}
    for m, (real, imag) in enumerate(complex_dft(turned, 1)):
        freq = 4 * m + 1
        if freq > period // 2:
            freq, imag = period - freq, -imag
        found[freq] = (real, imag)
    return found


def real_dft(items):
    count = len(items)
    if count == 1:
        return {0: (items[0], None)}
    if count == 2:
        return {0: (items[0] + items[1], None), 1: (items[0] - items[1], None)}
    half = count // 2
    low, high = items[:half], items[half:]
    found = {2 * k: v for k, v in real_dft([a + b for a, b in zip(low, high)]).items()}
    found.update(odd_outputs([a - b for a, b in zip(low, high)], count))
    return found


def padded_dft(items):
    found = {2 * k: v for k, v in real_dft(items).items()}
    found.update(odd_outputs(items, 2 * len(items)))
    return found


def odd_inputs(freqs, period):
    quarter = period // 4
    items = []
    for m in range(quarter):
        freq = 4 * m + 1
        if freq > period // 2:
            real, imag = freqs[period - freq]
            items.append((real, -imag))
        else:
            items.append(freqs[freq])
    low, high = [], []
    for n, item in enumerate(complex_dft(items, -1)):
        angle = 2.0 * math.pi * n / period
        real, imag = turn(item, math.cos(angle), -math.sin(angle))
        low.append(real)
        high.append(-imag)
    return low + high


def real_inverse(freqs, count):
    if count == 1:
        return [freqs[0][0]]
    if count == 2:
        return [freqs[0][0] + freqs[1][0], freqs[0][0] - freqs[1][0]]
    even = real_inverse({k // 2: v for k, v in freqs.items() if k % 2 == 0}, count // 2)
    odd = odd_inputs(freqs, count)
    return [a + b for a, b in zip(even, odd)] + [a - b for a, b in zip(even, odd)]


def padded_inverse(freqs, count):
    even = real_inverse({k // 2: v for k, v in freqs.items() if k % 2 == 0}, count)
    return [a + b for a, b in zip(even, odd_inputs(freqs, 2 * count))]


def each(count, body):
    step = max(s for s in range(1, 18) if count % s == 0)

    def several(turn_no, carry):
        for k in range(step):
            body(turn_no * step + k)
        return carry

    if step == count:
        several(0, 0)
    else:
        lax.fori_loop(0, count // step, several, 0)


def outer_forward(source, mid, base):
    blocks, group, width = source.shape

    def body(step, carry):
        start = pl.multiple_of(step * ROWS, ROWS)
        rows = pl.ds(start, ROWS)
        found = padded_dft([source[n, rows, :].astype(jnp.float32) for n in range(blocks)])
        out_rows = pl.ds(pl.multiple_of(start + base, ROWS), ROWS)
        for freq, (real, imag) in found.items():
            if imag is None:
                imag = jnp.zeros_like(real)
            mid[freq, out_rows, 0:width] = real.astype(jnp.bfloat16)
            mid[freq, out_rows, width : 2 * width] = imag.astype(jnp.bfloat16)
        return carry

    lax.fori_loop(0, group // ROWS, body, 0)


def outer_inverse(mid, base, dest):
    blocks, group, width = dest.shape

    def body(step, carry):
        start = pl.multiple_of(step * ROWS, ROWS)
        rows = pl.ds(pl.multiple_of(start + base, ROWS), ROWS)
        freqs = {
            k: (mid[k, rows, 0:width], mid[k, rows, width : 2 * width]) for k in range(blocks + 1)
        }
        for n, item in enumerate(padded_inverse(freqs, blocks)):
            dest[n, pl.ds(start, ROWS), :] = item.astype(dest.dtype)
        return carry

    lax.fori_loop(0, group // ROWS, body, 0)


def product(left, right, width, conjugate):
    left_real, left_imag = left[:, :width], left[:, width:]
    right_real, right_imag = right[:, :width], right[:, width:]
    if conjugate:
        left_imag = -left_imag
    real = left_real * right_real - left_imag * right_imag
    imag = left_real * right_imag + left_imag * right_real
    return jnp.concatenate([real.astype(jnp.bfloat16), imag.astype(jnp.bfloat16)], 1)


def place(inner):
    here = lax.axis_index("seq")
    return here // inner, lax.rem(here, inner)


def pack_planes_kernel(inner, outer, source, *refs):
    parts, sems = refs[:outer], refs[outer]
    group = parts[0].shape[2]
    plane, _ = place(inner)
    copies = []
    for far in range(outer - 1, -1, -1):
        for low in range(inner):
            start = pl.multiple_of(((plane ^ far) * inner + low) * group, ROWS)
            rows = source.at[pl.ds(start, group), :]
            copies.append(pltpu.make_async_copy(rows, parts[far].at[0, low], sems.at[far, low]))
            copies[-1].start()
    for copy in copies:
        copy.wait()


def pack_lows_kernel(inner, outer, source, *refs):
    parts, sems = refs[:inner], refs[inner]
    group = parts[0].shape[2]
    _, low = place(inner)
    copies = []
    for mask, part in enumerate(parts):
        for plane in range(outer):
            start = pl.multiple_of((plane * inner + (low ^ mask)) * group, ROWS)
            rows = source.at[pl.ds(start, group), :]
            copies.append(pltpu.make_async_copy(rows, part.at[0, plane], sems.at[mask, plane]))
            copies[-1].start()
    for copy in copies:
        copy.wait()


def gated_kernel(inner, outer, grad_out, gate, *refs):
    parts, (left, right, sems) = refs[:inner], refs[inner:]
    group = left.shape[2]
    _, low = place(inner)
    copies = []
    for mask in range(inner):
        for plane in range(outer):
            start = pl.multiple_of((plane * inner + (low ^ mask)) * group, ROWS)
            rows = pl.ds(start, group)
            pair = [
                pltpu.make_async_copy(
                    source.at[rows, :], held.at[mask, plane], sems.at[which, mask, plane]
                )
                for which, (source, held) in enumerate(((grad_out, left), (gate, right)))
            ]
            for copy in pair:
                copy.start()
            copies.append(pair)
    for mask, part in enumerate(parts):
        for plane in range(outer):
            for copy in copies[mask * outer + plane]:
                copy.wait()
            part[0, plane] = (
                left[mask, plane].astype(jnp.float32) * right[mask, plane].astype(jnp.float32)
            ).astype(jnp.bfloat16)


def turn_kernel(inner, fars, *refs):
    parts, outs = refs[:inner], refs[inner:]
    plane, low = place(inner)
    for mask, part in enumerate(parts):
        for far, out in zip(fars, outs):
            for which in range(part.shape[0]):
                out[which, low ^ mask] = part[which, plane ^ far]


def turn_back_kernel(inner, outer, *refs):
    parts, outs = refs[:outer], refs[outer:]
    plane, low = place(inner)
    for far, part in enumerate(parts):
        for mask, out in enumerate(outs):
            for which in range(part.shape[0]):
                out[which, plane ^ far] = part[which, low ^ mask]


def gather_planes(inner, outer, parts, signal):
    plane, _ = place(inner)
    for far, part in enumerate(parts):
        for low in range(inner):
            signal[(plane ^ far) * inner + low] = part[0, low]


def gather_lows(inner, outer, parts, signal):
    _, low = place(inner)
    for mask, part in enumerate(parts):
        for plane in range(outer):
            signal[plane * inner + (low ^ mask)] = part[0, plane]


def scatter(inner, outer, signal, outs):
    _, low = place(inner)
    for mask, out in enumerate(outs):
        for plane in range(outer):
            out[0, plane] = signal[plane * inner + (low ^ mask)]


def taps_kernel(inner, outer, *refs):
    parts, (forward, spec, signal, mid) = refs[:outer], refs[outer:]
    gather_planes(inner, outer, parts, signal)
    outer_forward(signal, mid, 0)

    def body(k):
        spec[k] = jnp.dot(mid[k], forward[k], preferred_element_type=jnp.float32)

    each(mid.shape[0], body)


def conv_kernel(inner, outer, *refs):
    parts, (spec_taps, forward, inverse) = refs[:inner], refs[inner : inner + 3]
    outs, (spec, signal, mid, back) = refs[inner + 3 : -4], refs[-4:]
    width = signal.shape[2]
    gather_lows(inner, outer, parts, signal)
    outer_forward(signal, mid, 0)

    def body(k):
        value = jnp.dot(mid[k], forward[k], preferred_element_type=jnp.float32)
        spec[k] = value
        back[k] = jnp.dot(
            product(spec_taps[k], value, width, False),
            inverse[k],
            preferred_element_type=jnp.float32,
        )

    each(mid.shape[0], body)
    outer_inverse(back, 0, signal)
    scatter(inner, outer, signal, outs)


def grad_kernel(inner, outer, ndp, factor, *refs):
    parts, (spec_taps, spec_value, forward, inverse) = refs[:outer], refs[outer : outer + 4]
    outs, sums = refs[outer + 4 : outer + 4 + inner], refs[outer + 4 + inner : -4]
    signal, cross, mid, back = refs[-4:]
    blocks, group, width = signal.shape
    gather_planes(inner, outer, parts, signal)
    outer_forward(signal, mid, 0)

    def body(k):
        gated = jnp.dot(mid[k], forward[k], preferred_element_type=jnp.float32)
        both = jnp.concatenate(
            [
                product(spec_taps[k], gated, width, True),
                product(spec_value[k], gated, width, True),
            ],
            0,
        )
        back[k] = jnp.dot(both, inverse[k], preferred_element_type=jnp.float32)

    each(mid.shape[0], body)
    outer_inverse(back, 0, signal)
    scatter(inner, outer, signal, outs)
    outer_inverse(back, group, cross)
    share = blocks // ndp
    for step, total in enumerate(sums):
        first = lax.rem(lax.axis_index("dp") + step, ndp) * share
        for n in range(share):
            total[:, n * width : (n + 1) * width] = (cross[first + n] * factor).astype(total.dtype)


def final_kernel(inner, outer, ndp, *refs):
    grad_parts, conv_parts, refs = refs[:outer], refs[outer : 2 * outer], refs[2 * outer :]
    sums, refs = refs[:ndp], refs[ndp:]
    grad_out, grad_gate, grad_value, grad_taps, product_of, total, sems, sum_sem = refs
    group = product_of.shape[2]
    plane, _ = place(inner)
    copies = []

    def send(source, dest, sem):
        copies.append(pltpu.make_async_copy(source, dest, sem))
        copies[-1].start()

    def rows_of(there, where):
        return pl.ds(pl.multiple_of((there * inner + where) * group, ROWS), group)

    for far, part in enumerate(grad_parts):
        for where in range(inner):
            rows = rows_of(plane ^ far, where)
            send(part.at[0, where], grad_value.at[rows, :], sems.at[0, far, where])
    total[...] = sums[0][...]
    for other in sums[1:]:
        total[...] += other[...].astype(jnp.float32)
    send(total, grad_taps, sum_sem.at[0])
    for far, part in enumerate(conv_parts):
        for where in range(inner):
            rows = rows_of(plane ^ far, where)
            product_of[far, where] = (
                grad_out[rows, :].astype(jnp.float32) * part[0, where].astype(jnp.float32)
            ).astype(jnp.bfloat16)
            send(product_of.at[far, where], grad_gate.at[rows, :], sems.at[1, far, where])
    for copy in copies:
        copy.wait()


def vmem(count):
    return [pl.BlockSpec(memory_space=pltpu.VMEM)] * count


def anywhere(count):
    return [pl.BlockSpec(memory_space=pl.ANY)] * count


def call(kernel, outs, scratch, operands, ins=None, dests=None, mib=4, flops=10**9, after=()):
    count = len(operands)

    def ordered(*refs):
        kernel(*refs[len(after) :])

    return pl.pallas_call(
        ordered,
        out_shape=list(outs),
        in_specs=anywhere(len(after)) + (ins or vmem(count)),
        out_specs=dests or vmem(len(outs)),
        scratch_shapes=scratch,
        compiler_params=pltpu.CompilerParams(vmem_limit_bytes=mib * 1024 * 1024),
        cost_estimate=pl.CostEstimate(flops=flops, bytes_accessed=10**6, transcendentals=0),
        name=kernel.func.__name__,
    )(*after, *operands)


def permute(array, axis, target):
    count = lax.axis_size(axis)
    return lax.ppermute(array, axis, [(i, target(i)) for i in range(count)])


def on_device(grad_out, gate, value, filter_taps):
    nseq = lax.axis_size("seq")
    ndp = lax.axis_size("dp")
    chans = grad_out.shape[1]
    width = grad_out.shape[2]
    group = chans // nseq
    blocks = nseq
    inner = 1 << (nseq.bit_length() - 1) // 2
    outer = nseq // inner
    forward, inverse = (jnp.asarray(t) for t in inner_tables(blocks, width))
    factor = 1.0 / (ndp * math.sqrt(nseq * width))
    shape = jax.ShapeDtypeStruct
    bf16, f32 = jnp.bfloat16, jnp.float32

    def by_plane(count=1):
        return [shape((count, inner, group, width), bf16)] * outer

    def by_low(count=1):
        return [shape((count, outer, group, width), bf16)] * inner

    def arrivals(parts, count=outer - 1):
        return [parts[far] for far in range(outer - 1, outer - 1 - count, -1)]

    def in_plane(parts):
        return [
            permute(part, "seq", lambda i: i ^ mask) if mask else part
            for mask, part in enumerate(parts)
        ]

    def over_planes(parts):
        return [
            permute(part, "seq", lambda i: i ^ (far * inner)) if far else part
            for far, part in enumerate(parts)
        ]

    def turned(parts, *steps):
        found = {}
        for fars, after in steps:
            kernel = functools.partial(turn_kernel, inner, fars)
            outs = call(kernel, by_plane()[: len(fars)], [], parts, after=list(after))
            found.update(zip(fars, outs))
        return [found[far] for far in range(outer)]

    everywhere = tuple(range(outer))
    lately = tuple(range(outer // 2, outer - 1))
    early = tuple(far for far in everywhere if far not in lately)

    value_packed = call(
        functools.partial(pack_planes_kernel, inner, outer),
        by_plane(),
        [pltpu.SemaphoreType.DMA((outer, inner))],
        [value[0]],
        ins=anywhere(1),
        mib=16,
    )
    taps_packed = call(
        functools.partial(pack_lows_kernel, inner, outer),
        by_low(),
        [pltpu.SemaphoreType.DMA((inner, outer))],
        [filter_taps],
        ins=anywhere(1),
        mib=16,
        after=value_packed[:1],
    )
    value_plane, taps_low = over_planes(value_packed), in_plane(taps_packed)
    gated_low = in_plane(
        call(
            functools.partial(gated_kernel, inner, outer),
            by_low(),
            [pltpu.VMEM((inner, outer, group, width), bf16)] * 2
            + [pltpu.SemaphoreType.DMA((2, inner, outer))],
            [grad_out[0], gate[0]],
            ins=anywhere(2),
            mib=16,
            after=taps_low[1:2],
        )
    )
    taps_turned = turned(taps_low, (everywhere, arrivals(value_plane, outer // 4)))
    taps_plane = over_planes(taps_turned)
    value_low = in_plane(
        call(
            functools.partial(turn_back_kernel, inner, outer),
            by_low(),
            [],
            value_plane,
            after=list(taps_turned[:1]) + arrivals(value_plane),
        )
    )

    spec = shape((blocks + 1, group, 2 * width), f32)
    signal = pltpu.VMEM((blocks, group, width), bf16)
    mid = pltpu.VMEM((blocks + 1, group, 2 * width), bf16)
    spec_taps = call(
        functools.partial(taps_kernel, inner, outer),
        [spec],
        [signal, mid],
        taps_plane + [forward],
        mib=16,
        after=arrivals(taps_plane),
    )[0]
    gated_turned = turned(gated_low, (early, arrivals(taps_plane, outer // 4)), (lately, [spec_taps]))
    gated_plane = over_planes(gated_turned)
    outs = call(
        functools.partial(conv_kernel, inner, outer),
        by_low() + [spec],
        [signal, mid, pltpu.VMEM((blocks + 1, group, 2 * width), f32)],
        value_low + [spec_taps, forward, inverse],
        mib=16,
    )
    conv_low, spec_value = in_plane(outs[:inner]), outs[inner]
    wide = (group, blocks // ndp * width)
    outs = call(
        functools.partial(grad_kernel, inner, outer, ndp, factor),
        by_low() + [shape(wide, f32)] + [shape(wide, bf16)] * (ndp - 1),
        [
            signal,
            pltpu.VMEM((blocks, group, width), f32),
            mid,
            pltpu.VMEM((blocks + 1, 2 * group, 2 * width), f32),
        ],
        gated_plane + [spec_taps, spec_value, forward, inverse],
        mib=24,
        after=arrivals(gated_plane),
    )
    sums = list(outs[inner:])
    for step in range(1, ndp):
        sums[step] = permute(sums[step], "dp", lambda i: (i + step) % ndp)
    conv_turned = turned(conv_low, (everywhere, outs[:1]))
    conv_plane = over_planes(conv_turned)
    grad_plane = over_planes(turned(in_plane(outs[:inner]), (everywhere, arrivals(conv_plane, outer // 2))))
    grad_gate, grad_value, grad_taps = call(
        functools.partial(final_kernel, inner, outer, ndp),
        [shape((chans, width), bf16)] * 2 + [shape(wide, f32)],
        [
            pltpu.VMEM((outer, inner, group, width), bf16),
            pltpu.VMEM(wide, f32),
            pltpu.SemaphoreType.DMA((2, outer, inner)),
            pltpu.SemaphoreType.DMA((1,)),
        ],
        grad_plane + conv_plane + sums + [grad_out[0]],
        dests=anywhere(3),
        mib=8,
        after=arrivals(conv_plane) + arrivals(grad_plane),
    )
    return (grad_gate[None], grad_value[None], grad_taps)


def solution(mesh):
    return jax.shard_map(
        on_device,
        mesh=mesh,
        in_specs=(P("dp", None, "seq"), P("dp", None, "seq"), P("dp", None, "seq"), P(None, "seq")),
        out_specs=(P("dp", None, "seq"), P("dp", None, "seq"), P("seq", "dp")),
        check_vma=False,
    )
```

```python
import functools
import math

import jax
import jax.numpy as jnp
import numpy as np
from jax import lax
from jax.experimental import pallas as pl
from jax.experimental.pallas import tpu as pltpu
from jax.sharding import PartitionSpec as P

ROWS = 16


def inner_tables(blocks, width):
    total = 2 * blocks * width
    pos = np.arange(width)
    tables = []
    for outer in range(blocks + 1):
        turns = pos[:, None] * (outer + 2 * blocks * pos[None, :]) % total
        angle = 2.0 * np.pi / total * turns
        cos, sin = np.cos(angle), np.sin(angle)
        tables.append(np.block([[cos, -sin], [sin, cos]]))
    table = np.stack(tables)
    weight = np.full((blocks + 1, 1, 1), 2.0 / total)
    weight[0] = weight[blocks] = 1.0 / total
    return (
        table.astype(jnp.bfloat16),
        (table.transpose(0, 2, 1) * weight).astype(jnp.bfloat16),
    )


def turn(number, cos, sin):
    real, imag = number
    if abs(sin) < 1e-9:
        return (real, imag) if cos > 0 else (-real, -imag)
    if abs(cos) < 1e-9:
        return (imag, -real) if sin > 0 else (-imag, real)
    return (real * cos + imag * sin, imag * cos - real * sin)


def add(left, right):
    return (left[0] + right[0], left[1] + right[1])


def sub(left, right):
    return (left[0] - right[0], left[1] - right[1])


def complex_dft(items, sign):
    count = len(items)
    if count == 1:
        return items
    half = count // 2
    low, high = items[:half], items[half:]
    even = complex_dft([add(a, b) for a, b in zip(low, high)], sign)
    odd = []
    for n, (a, b) in enumerate(zip(low, high)):
        angle = 2.0 * math.pi * n / count
        odd.append(turn(sub(a, b), math.cos(angle), sign * math.sin(angle)))
    odd = complex_dft(odd, sign)
    return [item for pair in zip(even, odd) for item in pair]


def odd_outputs(items, period):
    quarter = len(items) // 2
    turned = []
    for n in range(quarter):
        angle = 2.0 * math.pi * n / period
        turned.append(turn((items[n], -items[n + quarter]), math.cos(angle), math.sin(angle)))
    found = {}
    for m, (real, imag) in enumerate(complex_dft(turned, 1)):
        freq = 4 * m + 1
        if freq > period // 2:
            freq, imag = period - freq, -imag
        found[freq] = (real, imag)
    return found


def real_dft(items):
    count = len(items)
    if count == 1:
        return {0: (items[0], None)}
    if count == 2:
        return {0: (items[0] + items[1], None), 1: (items[0] - items[1], None)}
    half = count // 2
    low, high = items[:half], items[half:]
    found = {2 * k: v for k, v in real_dft([a + b for a, b in zip(low, high)]).items()}
    found.update(odd_outputs([a - b for a, b in zip(low, high)], count))
    return found


def padded_dft(items):
    found = {2 * k: v for k, v in real_dft(items).items()}
    found.update(odd_outputs(items, 2 * len(items)))
    return found


def odd_inputs(freqs, period):
    quarter = period // 4
    items = []
    for m in range(quarter):
        freq = 4 * m + 1
        if freq > period // 2:
            real, imag = freqs[period - freq]
            items.append((real, -imag))
        else:
            items.append(freqs[freq])
    low, high = [], []
    for n, item in enumerate(complex_dft(items, -1)):
        angle = 2.0 * math.pi * n / period
        real, imag = turn(item, math.cos(angle), -math.sin(angle))
        low.append(real)
        high.append(-imag)
    return low + high


def real_inverse(freqs, count):
    if count == 1:
        return [freqs[0][0]]
    if count == 2:
        return [freqs[0][0] + freqs[1][0], freqs[0][0] - freqs[1][0]]
    even = real_inverse({k // 2: v for k, v in freqs.items() if k % 2 == 0}, count // 2)
    odd = odd_inputs(freqs, count)
    return [a + b for a, b in zip(even, odd)] + [a - b for a, b in zip(even, odd)]


def padded_inverse(freqs, count):
    even = real_inverse({k // 2: v for k, v in freqs.items() if k % 2 == 0}, count)
    return [a + b for a, b in zip(even, odd_inputs(freqs, 2 * count))]


def each(count, body):
    step = max(s for s in range(1, 18) if count % s == 0)

    def several(turn_no, carry):
        for k in range(step):
            body(turn_no * step + k)
        return carry

    if step == count:
        several(0, 0)
    else:
        lax.fori_loop(0, count // step, several, 0)


def outer_forward(source, mid, base):
    blocks, group, width = source.shape

    def body(step, carry):
        start = pl.multiple_of(step * ROWS, ROWS)
        rows = pl.ds(start, ROWS)
        found = padded_dft([source[n, rows, :].astype(jnp.float32) for n in range(blocks)])
        out_rows = pl.ds(pl.multiple_of(start + base, ROWS), ROWS)
        for freq, (real, imag) in found.items():
            if imag is None:
                imag = jnp.zeros_like(real)
            mid[freq, out_rows, 0:width] = real.astype(jnp.bfloat16)
            mid[freq, out_rows, width : 2 * width] = imag.astype(jnp.bfloat16)
        return carry

    lax.fori_loop(0, group // ROWS, body, 0)


def outer_inverse(mid, base, dest):
    blocks, group, width = dest.shape

    def body(step, carry):
        start = pl.multiple_of(step * ROWS, ROWS)
        rows = pl.ds(pl.multiple_of(start + base, ROWS), ROWS)
        freqs = {
            k: (mid[k, rows, 0:width], mid[k, rows, width : 2 * width]) for k in range(blocks + 1)
        }
        for n, item in enumerate(padded_inverse(freqs, blocks)):
            dest[n, pl.ds(start, ROWS), :] = item.astype(dest.dtype)
        return carry

    lax.fori_loop(0, group // ROWS, body, 0)


def product(left, right, width, conjugate):
    left_real, left_imag = left[:, :width], left[:, width:]
    right_real, right_imag = right[:, :width], right[:, width:]
    if conjugate:
        left_imag = -left_imag
    real = left_real * right_real - left_imag * right_imag
    imag = left_real * right_imag + left_imag * right_real
    return jnp.concatenate([real.astype(jnp.bfloat16), imag.astype(jnp.bfloat16)], 1)


def place(inner):
    here = lax.axis_index("seq")
    return here // inner, lax.rem(here, inner)


def pack_planes_kernel(inner, outer, source, *refs):
    parts, sems = refs[:outer], refs[outer]
    group = parts[0].shape[2]
    plane, _ = place(inner)
    copies = []
    for far in range(outer - 1, -1, -1):
        for low in range(inner):
            start = pl.multiple_of(((plane ^ far) * inner + low) * group, ROWS)
            rows = source.at[pl.ds(start, group), :]
            copies.append(pltpu.make_async_copy(rows, parts[far].at[0, low], sems.at[far, low]))
            copies[-1].start()
    for copy in copies:
        copy.wait()


def pack_lows_kernel(inner, outer, source, *refs):
    parts, sems = refs[:inner], refs[inner]
    group = parts[0].shape[2]
    _, low = place(inner)
    copies = []
    for mask, part in enumerate(parts):
        for plane in range(outer):
            start = pl.multiple_of((plane * inner + (low ^ mask)) * group, ROWS)
            rows = source.at[pl.ds(start, group), :]
            copies.append(pltpu.make_async_copy(rows, part.at[0, plane], sems.at[mask, plane]))
            copies[-1].start()
    for copy in copies:
        copy.wait()


def gated_kernel(inner, outer, grad_out, gate, forward, inverse, *refs):
    parts, (left, right, sems) = refs[:inner], refs[inner:]
    group = left.shape[2]
    _, low = place(inner)
    copies = []
    for mask in range(inner):
        for plane in range(outer):
            start = pl.multiple_of((plane * inner + (low ^ mask)) * group, ROWS)
            rows = pl.ds(start, group)
            pair = [
                pltpu.make_async_copy(
                    source.at[rows, :], held.at[mask, plane], sems.at[which, mask, plane]
                )
                for which, (source, held) in enumerate(((grad_out, left), (gate, right)))
            ]
            for copy in pair:
                copy.start()
            copies.append(pair)
    for mask, part in enumerate(parts):
        for plane in range(outer):
            for copy in copies[mask * outer + plane]:
                copy.wait()
            part[0, plane] = (
                left[mask, plane].astype(jnp.float32) * right[mask, plane].astype(jnp.float32)
            ).astype(jnp.bfloat16)


def turn_kernel(inner, fars, *refs):
    parts, outs = refs[:inner], refs[inner:]
    plane, low = place(inner)
    for mask, part in enumerate(parts):
        for far, out in zip(fars, outs):
            for which in range(part.shape[0]):
                out[which, low ^ mask] = part[which, plane ^ far]


def turn_back_kernel(inner, outer, *refs):
    parts, outs = refs[:outer], refs[outer:]
    plane, low = place(inner)
    for far, part in enumerate(parts):
        for mask, out in enumerate(outs):
            for which in range(part.shape[0]):
                out[which, plane ^ far] = part[which, low ^ mask]


def gather_planes(inner, outer, parts, signal):
    plane, _ = place(inner)
    for far, part in enumerate(parts):
        for low in range(inner):
            signal[(plane ^ far) * inner + low] = part[0, low]


def gather_lows(inner, outer, parts, signal):
    _, low = place(inner)
    for mask, part in enumerate(parts):
        for plane in range(outer):
            signal[plane * inner + (low ^ mask)] = part[0, plane]


def scatter(inner, outer, signal, outs):
    _, low = place(inner)
    for mask, out in enumerate(outs):
        for plane in range(outer):
            out[0, plane] = signal[plane * inner + (low ^ mask)]


def taps_kernel(inner, outer, *refs):
    parts, (forward, spec, signal, mid) = refs[:outer], refs[outer:]
    gather_planes(inner, outer, parts, signal)
    outer_forward(signal, mid, 0)

    def body(k):
        spec[k] = jnp.dot(mid[k], forward[k], preferred_element_type=jnp.float32)

    each(mid.shape[0], body)


def conv_kernel(inner, outer, *refs):
    parts, (spec_taps, forward, inverse) = refs[:inner], refs[inner : inner + 3]
    outs, (spec, signal, mid, back) = refs[inner + 3 : -4], refs[-4:]
    width = signal.shape[2]
    gather_lows(inner, outer, parts, signal)
    outer_forward(signal, mid, 0)

    def body(k):
        value = jnp.dot(mid[k], forward[k], preferred_element_type=jnp.float32)
        spec[k] = value
        back[k] = jnp.dot(
            product(spec_taps[k], value, width, False),
            inverse[k],
            preferred_element_type=jnp.float32,
        )

    each(mid.shape[0], body)
    outer_inverse(back, 0, signal)
    scatter(inner, outer, signal, outs)


def grad_kernel(inner, outer, ndp, factor, *refs):
    parts, (spec_taps, spec_value, forward, inverse) = refs[:outer], refs[outer : outer + 4]
    outs, sums = refs[outer + 4 : outer + 4 + inner], refs[outer + 4 + inner : -4]
    signal, cross, mid, back = refs[-4:]
    blocks, group, width = signal.shape
    gather_planes(inner, outer, parts, signal)
    outer_forward(signal, mid, 0)

    def body(k):
        gated = jnp.dot(mid[k], forward[k], preferred_element_type=jnp.float32)
        both = jnp.concatenate(
            [
                product(spec_taps[k], gated, width, True),
                product(spec_value[k], gated, width, True),
            ],
            0,
        )
        back[k] = jnp.dot(both, inverse[k], preferred_element_type=jnp.float32)

    each(mid.shape[0], body)
    outer_inverse(back, 0, signal)
    scatter(inner, outer, signal, outs)
    outer_inverse(back, group, cross)
    share = blocks // ndp
    for step, total in enumerate(sums):
        first = lax.rem(lax.axis_index("dp") + step, ndp) * share
        for n in range(share):
            total[:, n * width : (n + 1) * width] = (cross[first + n] * factor).astype(total.dtype)


def final_kernel(inner, outer, ndp, *refs):
    grad_parts, conv_parts, refs = refs[:outer], refs[outer : 2 * outer], refs[2 * outer :]
    sums, refs = refs[:ndp], refs[ndp:]
    grad_out, grad_gate, grad_value, grad_taps, product_of, total, sems, sum_sem = refs
    group = product_of.shape[2]
    plane, _ = place(inner)
    copies = []

    def send(source, dest, sem):
        copies.append(pltpu.make_async_copy(source, dest, sem))
        copies[-1].start()

    def rows_of(there, where):
        return pl.ds(pl.multiple_of((there * inner + where) * group, ROWS), group)

    for far, part in enumerate(grad_parts):
        for where in range(inner):
            rows = rows_of(plane ^ far, where)
            send(part.at[0, where], grad_value.at[rows, :], sems.at[0, far, where])
    total[...] = sums[0][...]
    for other in sums[1:]:
        total[...] += other[...].astype(jnp.float32)
    send(total, grad_taps, sum_sem.at[0])
    for far, part in enumerate(conv_parts):
        for where in range(inner):
            rows = rows_of(plane ^ far, where)
            product_of[far, where] = (
                grad_out[rows, :].astype(jnp.float32) * part[0, where].astype(jnp.float32)
            ).astype(jnp.bfloat16)
            send(product_of.at[far, where], grad_gate.at[rows, :], sems.at[1, far, where])
    for copy in copies:
        copy.wait()


def vmem(count):
    return [pl.BlockSpec(memory_space=pltpu.VMEM)] * count


def anywhere(count):
    return [pl.BlockSpec(memory_space=pl.ANY)] * count


def call(kernel, outs, scratch, operands, ins=None, dests=None, mib=4, flops=10**9, after=()):
    count = len(operands)

    def ordered(*refs):
        kernel(*refs[len(after) :])

    return pl.pallas_call(
        ordered,
        out_shape=list(outs),
        in_specs=anywhere(len(after)) + (ins or vmem(count)),
        out_specs=dests or vmem(len(outs)),
        scratch_shapes=scratch,
        compiler_params=pltpu.CompilerParams(vmem_limit_bytes=mib * 1024 * 1024),
        cost_estimate=pl.CostEstimate(flops=flops, bytes_accessed=10**6, transcendentals=0),
        name=kernel.func.__name__,
    )(*after, *operands)


def permute(array, axis, target):
    count = lax.axis_size(axis)
    return lax.ppermute(array, axis, [(i, target(i)) for i in range(count)])


def on_device(grad_out, gate, value, filter_taps):
    nseq = lax.axis_size("seq")
    ndp = lax.axis_size("dp")
    chans = grad_out.shape[1]
    width = grad_out.shape[2]
    group = chans // nseq
    blocks = nseq
    inner = 1 << (nseq.bit_length() - 1) // 2
    outer = nseq // inner
    forward, inverse = (jnp.asarray(t) for t in inner_tables(blocks, width))
    factor = 1.0 / (ndp * math.sqrt(nseq * width))
    shape = jax.ShapeDtypeStruct
    bf16, f32 = jnp.bfloat16, jnp.float32

    def by_plane(count=1):
        return [shape((count, inner, group, width), bf16)] * outer

    def by_low(count=1):
        return [shape((count, outer, group, width), bf16)] * inner

    def arrivals(parts, count=outer - 1):
        return [parts[far] for far in range(outer - 1, outer - 1 - count, -1)]

    def in_plane(parts):
        return [
            permute(part, "seq", lambda i: i ^ mask) if mask else part
            for mask, part in enumerate(parts)
        ]

    def over_planes(found):
        return {
            far: permute(part, "seq", lambda i: i ^ (far * inner)) if far else part
            for far, part in found.items()
        }

    def turned(parts, fars, after=()):
        kernel = functools.partial(turn_kernel, inner, fars)
        outs = call(kernel, by_plane()[: len(fars)], [], parts, after=list(after))
        return dict(zip(fars, outs))

    def ordered(found):
        return [found[far] for far in range(outer)]

    everywhere = tuple(range(outer))
    early = (0, *everywhere[-outer // 4 :])
    lately = everywhere[1 : -outer // 4]

    value_packed = call(
        functools.partial(pack_planes_kernel, inner, outer),
        by_plane(),
        [pltpu.SemaphoreType.DMA((outer, inner))],
        [value[0]],
        ins=anywhere(1),
        mib=16,
    )
    taps_packed = call(
        functools.partial(pack_lows_kernel, inner, outer),
        by_low(),
        [pltpu.SemaphoreType.DMA((inner, outer))],
        [filter_taps],
        ins=anywhere(1),
        mib=16,
        after=value_packed[:1],
    )
    value_plane = ordered(over_planes(dict(enumerate(value_packed))))
    taps_low = in_plane(taps_packed)
    gated_low = in_plane(
        call(
            functools.partial(gated_kernel, inner, outer),
            by_low(),
            [pltpu.VMEM((inner, outer, group, width), bf16)] * 2
            + [pltpu.SemaphoreType.DMA((2, inner, outer))],
            [grad_out[0], gate[0], forward, inverse],
            ins=anywhere(2) + vmem(2),
            mib=16,
            after=taps_low[1:2],
        )
    )
    taps_turned = turned(taps_low, everywhere, arrivals(value_plane, outer // 4))
    taps_plane = ordered(over_planes(taps_turned))
    value_low = in_plane(
        call(
            functools.partial(turn_back_kernel, inner, outer),
            by_low(),
            [],
            value_plane,
            after=[taps_turned[0]] + arrivals(value_plane),
        )
    )

    spec = shape((blocks + 1, group, 2 * width), f32)
    signal = pltpu.VMEM((blocks, group, width), bf16)
    mid = pltpu.VMEM((blocks + 1, group, 2 * width), bf16)
    gated_early = turned(gated_low, early, arrivals(taps_plane, outer // 4))
    spec_taps = call(
        functools.partial(taps_kernel, inner, outer),
        [spec],
        [signal, mid],
        taps_plane + [forward],
        mib=16,
        after=[gated_early[outer - 1]] + arrivals(taps_plane),
    )[0]
    outs = call(
        functools.partial(conv_kernel, inner, outer),
        by_low() + [spec],
        [signal, mid, pltpu.VMEM((blocks + 1, group, 2 * width), f32)],
        value_low + [spec_taps, forward, inverse],
        mib=16,
    )
    conv_low, spec_value = in_plane(outs[:inner]), outs[inner]
    arrived = over_planes(gated_early)
    gated_late = turned(gated_low, lately, [outs[0], arrived[outer - 1]])
    gated_plane = ordered(arrived | over_planes(gated_late))
    conv_early = turned(conv_low, early)
    wide = (group, blocks // ndp * width)
    outs = call(
        functools.partial(grad_kernel, inner, outer, ndp, factor),
        by_low() + [shape(wide, f32)] + [shape(wide, bf16)] * (ndp - 1),
        [
            signal,
            pltpu.VMEM((blocks, group, width), f32),
            mid,
            pltpu.VMEM((blocks + 1, 2 * group, 2 * width), f32),
        ],
        gated_plane + [spec_taps, spec_value, forward, inverse],
        mib=24,
        after=[conv_early[outer - 1]] + arrivals(gated_plane),
    )
    sums = list(outs[inner:])
    for step in range(1, ndp):
        sums[step] = permute(sums[step], "dp", lambda i: (i + step) % ndp)
    conv_plane = ordered(over_planes(conv_early | turned(conv_low, lately, outs[:1])))
    grad_turned = turned(in_plane(outs[:inner]), everywhere, arrivals(conv_plane, outer // 2))
    grad_plane = ordered(over_planes(grad_turned))
    grad_gate, grad_value, grad_taps = call(
        functools.partial(final_kernel, inner, outer, ndp),
        [shape((chans, width), bf16)] * 2 + [shape(wide, f32)],
        [
            pltpu.VMEM((outer, inner, group, width), bf16),
            pltpu.VMEM(wide, f32),
            pltpu.SemaphoreType.DMA((2, outer, inner)),
            pltpu.SemaphoreType.DMA((1,)),
        ],
        grad_plane + conv_plane + sums + [grad_out[0]],
        dests=anywhere(3),
        mib=8,
        after=arrivals(conv_plane) + arrivals(grad_plane),
    )
    return (grad_gate[None], grad_value[None], grad_taps)


def solution(mesh):
    return jax.shard_map(
        on_device,
        mesh=mesh,
        in_specs=(P("dp", None, "seq"), P("dp", None, "seq"), P("dp", None, "seq"), P(None, "seq")),
        out_specs=(P("dp", None, "seq"), P("dp", None, "seq"), P("seq", "dp")),
        check_vma=False,
    )
```

```python
import functools
import math

import jax
import jax.numpy as jnp
import numpy as np
from jax import lax
from jax.experimental import pallas as pl
from jax.experimental.pallas import tpu as pltpu
from jax.sharding import PartitionSpec as P

ROWS = 16


def inner_tables(blocks, width):
    total = 2 * blocks * width
    pos = np.arange(width)
    tables = []
    for outer in range(blocks + 1):
        turns = pos[:, None] * (outer + 2 * blocks * pos[None, :]) % total
        angle = 2.0 * np.pi / total * turns
        cos, sin = np.cos(angle), np.sin(angle)
        tables.append(np.block([[cos, -sin], [sin, cos]]))
    table = np.stack(tables)
    weight = np.full((blocks + 1, 1, 1), 2.0 / total)
    weight[0] = weight[blocks] = 1.0 / total
    return (
        table.astype(jnp.bfloat16),
        (table.transpose(0, 2, 1) * weight).astype(jnp.bfloat16),
    )


def turn(number, cos, sin):
    real, imag = number
    if abs(sin) < 1e-9:
        return (real, imag) if cos > 0 else (-real, -imag)
    if abs(cos) < 1e-9:
        return (imag, -real) if sin > 0 else (-imag, real)
    return (real * cos + imag * sin, imag * cos - real * sin)


def add(left, right):
    return (left[0] + right[0], left[1] + right[1])


def sub(left, right):
    return (left[0] - right[0], left[1] - right[1])


def complex_dft(items, sign):
    count = len(items)
    if count == 1:
        return items
    half = count // 2
    low, high = items[:half], items[half:]
    even = complex_dft([add(a, b) for a, b in zip(low, high)], sign)
    odd = []
    for n, (a, b) in enumerate(zip(low, high)):
        angle = 2.0 * math.pi * n / count
        odd.append(turn(sub(a, b), math.cos(angle), sign * math.sin(angle)))
    odd = complex_dft(odd, sign)
    return [item for pair in zip(even, odd) for item in pair]


def odd_outputs(items, period):
    quarter = len(items) // 2
    turned = []
    for n in range(quarter):
        angle = 2.0 * math.pi * n / period
        turned.append(turn((items[n], -items[n + quarter]), math.cos(angle), math.sin(angle)))
    found = {}
    for m, (real, imag) in enumerate(complex_dft(turned, 1)):
        freq = 4 * m + 1
        if freq > period // 2:
            freq, imag = period - freq, -imag
        found[freq] = (real, imag)
    return found


def real_dft(items):
    count = len(items)
    if count == 1:
        return {0: (items[0], None)}
    if count == 2:
        return {0: (items[0] + items[1], None), 1: (items[0] - items[1], None)}
    half = count // 2
    low, high = items[:half], items[half:]
    found = {2 * k: v for k, v in real_dft([a + b for a, b in zip(low, high)]).items()}
    found.update(odd_outputs([a - b for a, b in zip(low, high)], count))
    return found


def padded_dft(items):
    found = {2 * k: v for k, v in real_dft(items).items()}
    found.update(odd_outputs(items, 2 * len(items)))
    return found


def odd_inputs(freqs, period):
    quarter = period // 4
    items = []
    for m in range(quarter):
        freq = 4 * m + 1
        if freq > period // 2:
            real, imag = freqs[period - freq]
            items.append((real, -imag))
        else:
            items.append(freqs[freq])
    low, high = [], []
    for n, item in enumerate(complex_dft(items, -1)):
        angle = 2.0 * math.pi * n / period
        real, imag = turn(item, math.cos(angle), -math.sin(angle))
        low.append(real)
        high.append(-imag)
    return low + high


def real_inverse(freqs, count):
    if count == 1:
        return [freqs[0][0]]
    if count == 2:
        return [freqs[0][0] + freqs[1][0], freqs[0][0] - freqs[1][0]]
    even = real_inverse({k // 2: v for k, v in freqs.items() if k % 2 == 0}, count // 2)
    odd = odd_inputs(freqs, count)
    return [a + b for a, b in zip(even, odd)] + [a - b for a, b in zip(even, odd)]


def padded_inverse(freqs, count):
    even = real_inverse({k // 2: v for k, v in freqs.items() if k % 2 == 0}, count)
    return [a + b for a, b in zip(even, odd_inputs(freqs, 2 * count))]


def each(count, body):
    step = max(s for s in range(1, 18) if count % s == 0)

    def several(turn_no, carry):
        for k in range(step):
            body(turn_no * step + k)
        return carry

    if step == count:
        several(0, 0)
    else:
        lax.fori_loop(0, count // step, several, 0)


def outer_forward(source, mid, base):
    blocks, group, width = source.shape

    def body(step, carry):
        start = pl.multiple_of(step * ROWS, ROWS)
        rows = pl.ds(start, ROWS)
        found = padded_dft([source[n, rows, :].astype(jnp.float32) for n in range(blocks)])
        out_rows = pl.ds(pl.multiple_of(start + base, ROWS), ROWS)
        for freq, (real, imag) in found.items():
            if imag is None:
                imag = jnp.zeros_like(real)
            mid[freq, out_rows, 0:width] = real.astype(jnp.bfloat16)
            mid[freq, out_rows, width : 2 * width] = imag.astype(jnp.bfloat16)
        return carry

    lax.fori_loop(0, group // ROWS, body, 0)


def outer_inverse(mid, base, dest):
    blocks, group, width = dest.shape

    def body(step, carry):
        start = pl.multiple_of(step * ROWS, ROWS)
        rows = pl.ds(pl.multiple_of(start + base, ROWS), ROWS)
        freqs = {
            k: (mid[k, rows, 0:width], mid[k, rows, width : 2 * width]) for k in range(blocks + 1)
        }
        for n, item in enumerate(padded_inverse(freqs, blocks)):
            dest[n, pl.ds(start, ROWS), :] = item.astype(dest.dtype)
        return carry

    lax.fori_loop(0, group // ROWS, body, 0)


def product(left, right, width, conjugate):
    left_real, left_imag = left[:, :width], left[:, width:]
    right_real, right_imag = right[:, :width], right[:, width:]
    if conjugate:
        left_imag = -left_imag
    real = left_real * right_real - left_imag * right_imag
    imag = left_real * right_imag + left_imag * right_real
    return jnp.concatenate([real.astype(jnp.bfloat16), imag.astype(jnp.bfloat16)], 1)


def place(inner):
    here = lax.axis_index("seq")
    return here // inner, lax.rem(here, inner)


def pack_planes_kernel(inner, outer, source, *refs):
    parts, sems = refs[:outer], refs[outer]
    group = parts[0].shape[2]
    plane, _ = place(inner)
    copies = []
    for far in range(outer - 1, -1, -1):
        for low in range(inner):
            start = pl.multiple_of(((plane ^ far) * inner + low) * group, ROWS)
            rows = source.at[pl.ds(start, group), :]
            copies.append(pltpu.make_async_copy(rows, parts[far].at[0, low], sems.at[far, low]))
            copies[-1].start()
    for copy in copies:
        copy.wait()


def pack_lows_kernel(inner, outer, source, *refs):
    parts, sems = refs[:inner], refs[inner]
    group = parts[0].shape[2]
    _, low = place(inner)
    copies = []
    for mask, part in enumerate(parts):
        for plane in range(outer):
            start = pl.multiple_of((plane * inner + (low ^ mask)) * group, ROWS)
            rows = source.at[pl.ds(start, group), :]
            copies.append(pltpu.make_async_copy(rows, part.at[0, plane], sems.at[mask, plane]))
            copies[-1].start()
    for copy in copies:
        copy.wait()


def gated_kernel(inner, outer, grad_out, gate, forward, inverse, *refs):
    parts, (left, right, sems) = refs[:inner], refs[inner:]
    group = left.shape[2]
    _, low = place(inner)
    copies = []
    for mask in range(inner):
        for plane in range(outer):
            start = pl.multiple_of((plane * inner + (low ^ mask)) * group, ROWS)
            rows = pl.ds(start, group)
            pair = [
                pltpu.make_async_copy(
                    source.at[rows, :], held.at[mask, plane], sems.at[which, mask, plane]
                )
                for which, (source, held) in enumerate(((grad_out, left), (gate, right)))
            ]
            for copy in pair:
                copy.start()
            copies.append(pair)
    for mask, part in enumerate(parts):
        for plane in range(outer):
            for copy in copies[mask * outer + plane]:
                copy.wait()
            part[0, plane] = (
                left[mask, plane].astype(jnp.float32) * right[mask, plane].astype(jnp.float32)
            ).astype(jnp.bfloat16)


def turn_kernel(inner, fars, *refs):
    parts, outs = refs[:inner], refs[inner:]
    plane, low = place(inner)
    for mask, part in enumerate(parts):
        for far, out in zip(fars, outs):
            for which in range(part.shape[0]):
                out[which, low ^ mask] = part[which, plane ^ far]


def turn_back_kernel(inner, outer, *refs):
    parts, outs = refs[:outer], refs[outer:]
    plane, low = place(inner)
    for far, part in enumerate(parts):
        for mask, out in enumerate(outs):
            for which in range(part.shape[0]):
                out[which, plane ^ far] = part[which, low ^ mask]


def gather_planes(inner, outer, parts, signal):
    plane, _ = place(inner)
    for far, part in enumerate(parts):
        for low in range(inner):
            signal[(plane ^ far) * inner + low] = part[0, low]


def gather_lows(inner, outer, parts, signal):
    _, low = place(inner)
    for mask, part in enumerate(parts):
        for plane in range(outer):
            signal[plane * inner + (low ^ mask)] = part[0, plane]


def scatter(inner, outer, signal, outs):
    _, low = place(inner)
    for mask, out in enumerate(outs):
        for plane in range(outer):
            out[0, plane] = signal[plane * inner + (low ^ mask)]


def taps_kernel(inner, outer, *refs):
    parts, (forward, spec, signal, mid) = refs[:outer], refs[outer:]
    gather_planes(inner, outer, parts, signal)
    outer_forward(signal, mid, 0)

    def body(k):
        spec[k] = jnp.dot(mid[k], forward[k], preferred_element_type=jnp.float32)

    each(mid.shape[0], body)


def conv_kernel(inner, outer, *refs):
    parts, (spec_taps, forward, inverse) = refs[:inner], refs[inner : inner + 3]
    outs, (spec, signal, mid, back) = refs[inner + 3 : -4], refs[-4:]
    width = signal.shape[2]
    gather_lows(inner, outer, parts, signal)
    outer_forward(signal, mid, 0)

    def body(k):
        value = jnp.dot(mid[k], forward[k], preferred_element_type=jnp.float32)
        spec[k] = value
        back[k] = jnp.dot(
            product(spec_taps[k], value, width, False),
            inverse[k],
            preferred_element_type=jnp.float32,
        )

    each(mid.shape[0], body)
    outer_inverse(back, 0, signal)
    scatter(inner, outer, signal, outs)


def grad_kernel(inner, outer, *refs):
    parts, (spec_taps, forward, inverse) = refs[:outer], refs[outer : outer + 3]
    outs, (spec, signal, mid, back) = refs[outer + 3 : -4], refs[-4:]
    width = signal.shape[2]
    gather_planes(inner, outer, parts, signal)
    outer_forward(signal, mid, 0)

    def body(k):
        gated = jnp.dot(mid[k], forward[k], preferred_element_type=jnp.float32)
        spec[k] = gated
        back[k] = jnp.dot(
            product(spec_taps[k], gated, width, True),
            inverse[k],
            preferred_element_type=jnp.float32,
        )

    each(mid.shape[0], body)
    outer_inverse(back, 0, signal)
    scatter(inner, outer, signal, outs)


def cross_kernel(ndp, factor, spec_value, spec_gated, inverse, *refs):
    sums, (cross, back) = refs[:ndp], refs[ndp:]
    blocks, _, width = cross.shape

    def body(k):
        back[k] = jnp.dot(
            product(spec_value[k], spec_gated[k], width, True),
            inverse[k],
            preferred_element_type=jnp.float32,
        )

    each(back.shape[0], body)
    outer_inverse(back, 0, cross)
    share = blocks // ndp
    for step, total in enumerate(sums):
        first = lax.rem(lax.axis_index("dp") + step, ndp) * share
        for n in range(share):
            total[:, n * width : (n + 1) * width] = (cross[first + n] * factor).astype(total.dtype)


def final_kernel(inner, outer, ndp, *refs):
    grad_parts, conv_parts, refs = refs[:outer], refs[outer : 2 * outer], refs[2 * outer :]
    sums, refs = refs[:ndp], refs[ndp:]
    grad_out, grad_gate, grad_value, grad_taps, product_of, total, sems, sum_sem = refs
    group = product_of.shape[2]
    plane, _ = place(inner)
    copies = []

    def send(source, dest, sem):
        copies.append(pltpu.make_async_copy(source, dest, sem))
        copies[-1].start()

    def rows_of(there, where):
        return pl.ds(pl.multiple_of((there * inner + where) * group, ROWS), group)

    for far, part in enumerate(grad_parts):
        for where in range(inner):
            rows = rows_of(plane ^ far, where)
            send(part.at[0, where], grad_value.at[rows, :], sems.at[0, far, where])
    total[...] = sums[0][...]
    for other in sums[1:]:
        total[...] += other[...].astype(jnp.float32)
    send(total, grad_taps, sum_sem.at[0])
    for far, part in enumerate(conv_parts):
        for where in range(inner):
            rows = rows_of(plane ^ far, where)
            product_of[far, where] = (
                grad_out[rows, :].astype(jnp.float32) * part[0, where].astype(jnp.float32)
            ).astype(jnp.bfloat16)
            send(product_of.at[far, where], grad_gate.at[rows, :], sems.at[1, far, where])
    for copy in copies:
        copy.wait()


def vmem(count):
    return [pl.BlockSpec(memory_space=pltpu.VMEM)] * count


def anywhere(count):
    return [pl.BlockSpec(memory_space=pl.ANY)] * count


def call(kernel, outs, scratch, operands, ins=None, dests=None, mib=4, flops=10**9, after=()):
    count = len(operands)

    def ordered(*refs):
        kernel(*refs[len(after) :])

    return pl.pallas_call(
        ordered,
        out_shape=list(outs),
        in_specs=anywhere(len(after)) + (ins or vmem(count)),
        out_specs=dests or vmem(len(outs)),
        scratch_shapes=scratch,
        compiler_params=pltpu.CompilerParams(vmem_limit_bytes=mib * 1024 * 1024),
        cost_estimate=pl.CostEstimate(flops=flops, bytes_accessed=10**6, transcendentals=0),
        name=kernel.func.__name__,
    )(*after, *operands)


def permute(array, axis, target):
    count = lax.axis_size(axis)
    return lax.ppermute(array, axis, [(i, target(i)) for i in range(count)])


def on_device(grad_out, gate, value, filter_taps):
    nseq = lax.axis_size("seq")
    ndp = lax.axis_size("dp")
    chans = grad_out.shape[1]
    width = grad_out.shape[2]
    group = chans // nseq
    blocks = nseq
    inner = 1 << (nseq.bit_length() - 1) // 2
    outer = nseq // inner
    forward, inverse = (jnp.asarray(t) for t in inner_tables(blocks, width))
    factor = 1.0 / (ndp * math.sqrt(nseq * width))
    shape = jax.ShapeDtypeStruct
    bf16, f32 = jnp.bfloat16, jnp.float32

    def by_plane(count=1):
        return [shape((count, inner, group, width), bf16)] * outer

    def by_low(count=1):
        return [shape((count, outer, group, width), bf16)] * inner

    def arrivals(parts, count=outer - 1):
        return [parts[far] for far in range(outer - 1, outer - 1 - count, -1)]

    def in_plane(parts):
        return [
            permute(part, "seq", lambda i: i ^ mask) if mask else part
            for mask, part in enumerate(parts)
        ]

    def over_planes(found):
        return {
            far: permute(part, "seq", lambda i: i ^ (far * inner)) if far else part
            for far, part in found.items()
        }

    def turned(parts, fars, after=()):
        kernel = functools.partial(turn_kernel, inner, fars)
        outs = call(kernel, by_plane()[: len(fars)], [], parts, after=list(after))
        return dict(zip(fars, outs))

    def ordered(found):
        return [found[far] for far in range(outer)]

    everywhere = tuple(range(outer))
    early = (0, *everywhere[-outer // 4 :])
    lately = everywhere[1 : -outer // 4]

    value_packed = call(
        functools.partial(pack_planes_kernel, inner, outer),
        by_plane(),
        [pltpu.SemaphoreType.DMA((outer, inner))],
        [value[0]],
        ins=anywhere(1),
        mib=16,
    )
    taps_packed = call(
        functools.partial(pack_lows_kernel, inner, outer),
        by_low(),
        [pltpu.SemaphoreType.DMA((inner, outer))],
        [filter_taps],
        ins=anywhere(1),
        mib=16,
        after=value_packed[:1],
    )
    value_plane = ordered(over_planes(dict(enumerate(value_packed))))
    taps_low = in_plane(taps_packed)
    gated_packed = call(
        functools.partial(gated_kernel, inner, outer),
        by_low(),
        [pltpu.VMEM((inner, outer, group, width), bf16)] * 2
        + [pltpu.SemaphoreType.DMA((2, inner, outer))],
        [grad_out[0], gate[0], forward, inverse],
        ins=anywhere(2) + vmem(2),
        mib=16,
        after=taps_low[1:2],
    )
    gated_low = in_plane(gated_packed)
    taps_turned = turned(taps_low, everywhere, list(gated_packed[:1]) + arrivals(value_plane, outer // 4))
    taps_plane = ordered(over_planes(taps_turned))
    value_low = in_plane(
        call(
            functools.partial(turn_back_kernel, inner, outer),
            by_low(),
            [],
            value_plane,
            after=[taps_turned[0]] + arrivals(value_plane),
        )
    )

    spec = shape((blocks + 1, group, 2 * width), f32)
    signal = pltpu.VMEM((blocks, group, width), bf16)
    mid = pltpu.VMEM((blocks + 1, group, 2 * width), bf16)
    back = pltpu.VMEM((blocks + 1, group, 2 * width), f32)
    gated_early = turned(gated_low, early, arrivals(taps_plane, outer // 4))
    spec_taps = call(
        functools.partial(taps_kernel, inner, outer),
        [spec],
        [signal, mid],
        taps_plane + [forward],
        mib=16,
        after=[gated_early[outer - 1]] + arrivals(taps_plane),
    )[0]
    outs = call(
        functools.partial(conv_kernel, inner, outer),
        by_low() + [spec],
        [signal, mid, back],
        value_low + [spec_taps, forward, inverse],
        mib=16,
    )
    conv_low, spec_value = in_plane(outs[:inner]), outs[inner]
    arrived = over_planes(gated_early)
    gated_late = turned(gated_low, lately, [outs[0], arrived[outer - 1]])
    gated_plane = ordered(arrived | over_planes(gated_late))
    conv_turned = turned(conv_low, everywhere)
    conv_plane = ordered(over_planes(conv_turned))
    wide = (group, blocks // ndp * width)
    outs = call(
        functools.partial(grad_kernel, inner, outer),
        by_low() + [spec],
        [signal, mid, back],
        gated_plane + [spec_taps, forward, inverse],
        mib=16,
        after=[conv_turned[0]] + arrivals(gated_plane),
    )
    grad_low, spec_gated = in_plane(outs[:inner]), outs[inner]
    sums = list(
        call(
            functools.partial(cross_kernel, ndp, factor),
            [shape(wide, f32)] + [shape(wide, bf16)] * (ndp - 1),
            [pltpu.VMEM((blocks, group, width), f32), back],
            [spec_value, spec_gated, inverse],
            mib=16,
        )
    )
    for step in range(1, ndp):
        sums[step] = permute(sums[step], "dp", lambda i: (i + step) % ndp)
    grad_turned = turned(grad_low, everywhere, arrivals(conv_plane, outer // 2))
    grad_plane = ordered(over_planes(grad_turned))
    grad_gate, grad_value, grad_taps = call(
        functools.partial(final_kernel, inner, outer, ndp),
        [shape((chans, width), bf16)] * 2 + [shape(wide, f32)],
        [
            pltpu.VMEM((outer, inner, group, width), bf16),
            pltpu.VMEM(wide, f32),
            pltpu.SemaphoreType.DMA((2, outer, inner)),
            pltpu.SemaphoreType.DMA((1,)),
        ],
        grad_plane + conv_plane + sums + [grad_out[0]],
        dests=anywhere(3),
        mib=8,
        after=arrivals(conv_plane) + arrivals(grad_plane),
    )
    return (grad_gate[None], grad_value[None], grad_taps)


def solution(mesh):
    return jax.shard_map(
        on_device,
        mesh=mesh,
        in_specs=(P("dp", None, "seq"), P("dp", None, "seq"), P("dp", None, "seq"), P(None, "seq")),
        out_specs=(P("dp", None, "seq"), P("dp", None, "seq"), P("seq", "dp")),
        check_vma=False,
    )
```

```python
import functools
import math

import jax
import jax.numpy as jnp
import numpy as np
from jax import lax
from jax.experimental import pallas as pl
from jax.experimental.pallas import tpu as pltpu
from jax.sharding import PartitionSpec as P

ROWS = 16


def inner_tables(blocks, width):
    total = 2 * blocks * width
    pos = np.arange(width)
    tables = []
    for outer in range(blocks + 1):
        turns = pos[:, None] * (outer + 2 * blocks * pos[None, :]) % total
        angle = 2.0 * np.pi / total * turns
        cos, sin = np.cos(angle), np.sin(angle)
        tables.append(np.block([[cos, -sin], [sin, cos]]))
    table = np.stack(tables)
    weight = np.full((blocks + 1, 1, 1), 2.0 / total)
    weight[0] = weight[blocks] = 1.0 / total
    return (
        table.astype(jnp.bfloat16),
        (table.transpose(0, 2, 1) * weight).astype(jnp.bfloat16),
    )


def turn(number, cos, sin):
    real, imag = number
    if abs(sin) < 1e-9:
        return (real, imag) if cos > 0 else (-real, -imag)
    if abs(cos) < 1e-9:
        return (imag, -real) if sin > 0 else (-imag, real)
    return (real * cos + imag * sin, imag * cos - real * sin)


def add(left, right):
    return (left[0] + right[0], left[1] + right[1])


def sub(left, right):
    return (left[0] - right[0], left[1] - right[1])


def complex_dft(items, sign):
    count = len(items)
    if count == 1:
        return items
    half = count // 2
    low, high = items[:half], items[half:]
    even = complex_dft([add(a, b) for a, b in zip(low, high)], sign)
    odd = []
    for n, (a, b) in enumerate(zip(low, high)):
        angle = 2.0 * math.pi * n / count
        odd.append(turn(sub(a, b), math.cos(angle), sign * math.sin(angle)))
    odd = complex_dft(odd, sign)
    return [item for pair in zip(even, odd) for item in pair]


def odd_outputs(items, period):
    quarter = len(items) // 2
    turned = []
    for n in range(quarter):
        angle = 2.0 * math.pi * n / period
        turned.append(turn((items[n], -items[n + quarter]), math.cos(angle), math.sin(angle)))
    found = {}
    for m, (real, imag) in enumerate(complex_dft(turned, 1)):
        freq = 4 * m + 1
        if freq > period // 2:
            freq, imag = period - freq, -imag
        found[freq] = (real, imag)
    return found


def real_dft(items):
    count = len(items)
    if count == 1:
        return {0: (items[0], None)}
    if count == 2:
        return {0: (items[0] + items[1], None), 1: (items[0] - items[1], None)}
    half = count // 2
    low, high = items[:half], items[half:]
    found = {2 * k: v for k, v in real_dft([a + b for a, b in zip(low, high)]).items()}
    found.update(odd_outputs([a - b for a, b in zip(low, high)], count))
    return found


def padded_dft(items):
    found = {2 * k: v for k, v in real_dft(items).items()}
    found.update(odd_outputs(items, 2 * len(items)))
    return found


def odd_inputs(freqs, period):
    quarter = period // 4
    items = []
    for m in range(quarter):
        freq = 4 * m + 1
        if freq > period // 2:
            real, imag = freqs[period - freq]
            items.append((real, -imag))
        else:
            items.append(freqs[freq])
    low, high = [], []
    for n, item in enumerate(complex_dft(items, -1)):
        angle = 2.0 * math.pi * n / period
        real, imag = turn(item, math.cos(angle), -math.sin(angle))
        low.append(real)
        high.append(-imag)
    return low + high


def real_inverse(freqs, count):
    if count == 1:
        return [freqs[0][0]]
    if count == 2:
        return [freqs[0][0] + freqs[1][0], freqs[0][0] - freqs[1][0]]
    even = real_inverse({k // 2: v for k, v in freqs.items() if k % 2 == 0}, count // 2)
    odd = odd_inputs(freqs, count)
    return [a + b for a, b in zip(even, odd)] + [a - b for a, b in zip(even, odd)]


def padded_inverse(freqs, count):
    even = real_inverse({k // 2: v for k, v in freqs.items() if k % 2 == 0}, count)
    return [a + b for a, b in zip(even, odd_inputs(freqs, 2 * count))]


def each(count, body):
    step = max(s for s in range(1, 18) if count % s == 0)

    def several(turn_no, carry):
        for k in range(step):
            body(turn_no * step + k)
        return carry

    if step == count:
        several(0, 0)
    else:
        lax.fori_loop(0, count // step, several, 0)


def outer_forward(source, mid, base):
    blocks, group, width = source.shape

    def body(step, carry):
        start = pl.multiple_of(step * ROWS, ROWS)
        rows = pl.ds(start, ROWS)
        found = padded_dft([source[n, rows, :].astype(jnp.float32) for n in range(blocks)])
        out_rows = pl.ds(pl.multiple_of(start + base, ROWS), ROWS)
        for freq, (real, imag) in found.items():
            if imag is None:
                imag = jnp.zeros_like(real)
            mid[freq, out_rows, 0:width] = real.astype(jnp.bfloat16)
            mid[freq, out_rows, width : 2 * width] = imag.astype(jnp.bfloat16)
        return carry

    lax.fori_loop(0, group // ROWS, body, 0)


def outer_inverse(mid, base, dest):
    blocks, group, width = dest.shape

    def body(step, carry):
        start = pl.multiple_of(step * ROWS, ROWS)
        rows = pl.ds(pl.multiple_of(start + base, ROWS), ROWS)
        freqs = {
            k: (mid[k, rows, 0:width], mid[k, rows, width : 2 * width]) for k in range(blocks + 1)
        }
        for n, item in enumerate(padded_inverse(freqs, blocks)):
            dest[n, pl.ds(start, ROWS), :] = item.astype(dest.dtype)
        return carry

    lax.fori_loop(0, group // ROWS, body, 0)


def product(left, right, width, conjugate):
    left_real, left_imag = left[:, :width], left[:, width:]
    right_real, right_imag = right[:, :width], right[:, width:]
    if conjugate:
        left_imag = -left_imag
    real = left_real * right_real - left_imag * right_imag
    imag = left_real * right_imag + left_imag * right_real
    return jnp.concatenate([real.astype(jnp.bfloat16), imag.astype(jnp.bfloat16)], 1)


def place(inner):
    here = lax.axis_index("seq")
    return here // inner, lax.rem(here, inner)


def pack_planes_kernel(inner, outer, source, *refs):
    parts, sems = refs[:outer], refs[outer]
    group = parts[0].shape[2]
    plane, _ = place(inner)
    copies = []
    for far in range(outer - 1, -1, -1):
        for low in range(inner):
            start = pl.multiple_of(((plane ^ far) * inner + low) * group, ROWS)
            rows = source.at[pl.ds(start, group), :]
            copies.append(pltpu.make_async_copy(rows, parts[far].at[0, low], sems.at[far, low]))
            copies[-1].start()
    for copy in copies:
        copy.wait()


def pack_lows_kernel(inner, outer, source, *refs):
    parts, sems = refs[:inner], refs[inner]
    group = parts[0].shape[2]
    _, low = place(inner)
    copies = []
    for mask, part in enumerate(parts):
        for plane in range(outer):
            start = pl.multiple_of((plane * inner + (low ^ mask)) * group, ROWS)
            rows = source.at[pl.ds(start, group), :]
            copies.append(pltpu.make_async_copy(rows, part.at[0, plane], sems.at[mask, plane]))
            copies[-1].start()
    for copy in copies:
        copy.wait()


def gated_kernel(inner, outer, grad_out, gate, forward, inverse, *refs):
    parts, (left, right, sems) = refs[:inner], refs[inner:]
    group = left.shape[2]
    _, low = place(inner)
    copies = []
    for mask in range(inner):
        for plane in range(outer):
            start = pl.multiple_of((plane * inner + (low ^ mask)) * group, ROWS)
            rows = pl.ds(start, group)
            pair = [
                pltpu.make_async_copy(
                    source.at[rows, :], held.at[mask, plane], sems.at[which, mask, plane]
                )
                for which, (source, held) in enumerate(((grad_out, left), (gate, right)))
            ]
            for copy in pair:
                copy.start()
            copies.append(pair)
    for mask, part in enumerate(parts):
        for plane in range(outer):
            for copy in copies[mask * outer + plane]:
                copy.wait()
            part[0, plane] = (
                left[mask, plane].astype(jnp.float32) * right[mask, plane].astype(jnp.float32)
            ).astype(jnp.bfloat16)


def turn_kernel(inner, fars, *refs):
    parts, outs = refs[:inner], refs[inner:]
    plane, low = place(inner)
    for mask, part in enumerate(parts):
        for far, out in zip(fars, outs):
            for which in range(part.shape[0]):
                out[which, low ^ mask] = part[which, plane ^ far]


def turn_back_kernel(inner, outer, *refs):
    parts, outs = refs[:outer], refs[outer:]
    plane, low = place(inner)
    for far, part in enumerate(parts):
        for mask, out in enumerate(outs):
            for which in range(part.shape[0]):
                out[which, plane ^ far] = part[which, low ^ mask]


def gather_planes(inner, outer, parts, signal):
    plane, _ = place(inner)
    for far, part in enumerate(parts):
        for low in range(inner):
            signal[(plane ^ far) * inner + low] = part[0, low]


def gather_lows(inner, outer, parts, signal):
    _, low = place(inner)
    for mask, part in enumerate(parts):
        for plane in range(outer):
            signal[plane * inner + (low ^ mask)] = part[0, plane]


def scatter(inner, outer, signal, outs):
    _, low = place(inner)
    for mask, out in enumerate(outs):
        for plane in range(outer):
            out[0, plane] = signal[plane * inner + (low ^ mask)]


def taps_kernel(inner, outer, *refs):
    parts, (forward, spec, signal, mid) = refs[:outer], refs[outer:]
    gather_planes(inner, outer, parts, signal)
    outer_forward(signal, mid, 0)

    def body(k):
        spec[k] = jnp.dot(mid[k], forward[k], preferred_element_type=jnp.float32)

    each(mid.shape[0], body)


def conv_kernel(inner, outer, *refs):
    parts, (spec_taps, forward, inverse) = refs[:inner], refs[inner : inner + 3]
    outs, (spec, signal, mid, back) = refs[inner + 3 : -4], refs[-4:]
    width = signal.shape[2]
    gather_lows(inner, outer, parts, signal)
    outer_forward(signal, mid, 0)

    def body(k):
        value = jnp.dot(mid[k], forward[k], preferred_element_type=jnp.float32)
        spec[k] = value
        back[k] = jnp.dot(
            product(spec_taps[k], value, width, False),
            inverse[k],
            preferred_element_type=jnp.float32,
        )

    each(mid.shape[0], body)
    outer_inverse(back, 0, signal)
    plane, _ = place(inner)
    for far, out in enumerate(outs):
        for low in range(inner):
            out[0, low] = signal[(plane ^ far) * inner + low]


def grad_kernel(inner, outer, *refs):
    parts, (spec_taps, forward, inverse) = refs[:outer], refs[outer : outer + 3]
    outs, (spec, signal, mid, back) = refs[outer + 3 : -4], refs[-4:]
    width = signal.shape[2]
    gather_planes(inner, outer, parts, signal)
    outer_forward(signal, mid, 0)

    def body(k):
        gated = jnp.dot(mid[k], forward[k], preferred_element_type=jnp.float32)
        spec[k] = gated
        back[k] = jnp.dot(
            product(spec_taps[k], gated, width, True),
            inverse[k],
            preferred_element_type=jnp.float32,
        )

    each(mid.shape[0], body)
    outer_inverse(back, 0, signal)
    scatter(inner, outer, signal, outs)


def cross_kernel(ndp, factor, spec_value, spec_gated, inverse, *refs):
    sums, (cross, back) = refs[:ndp], refs[ndp:]
    blocks, _, width = cross.shape

    def body(k):
        back[k] = jnp.dot(
            product(spec_value[k], spec_gated[k], width, True),
            inverse[k],
            preferred_element_type=jnp.float32,
        )

    each(back.shape[0], body)
    outer_inverse(back, 0, cross)
    share = blocks // ndp
    for step, total in enumerate(sums):
        first = lax.rem(lax.axis_index("dp") + step, ndp) * share
        for n in range(share):
            total[:, n * width : (n + 1) * width] = (cross[first + n] * factor).astype(total.dtype)


def final_kernel(inner, outer, ndp, *refs):
    grad_parts, conv_parts, refs = refs[:outer], refs[outer : outer + inner], refs[outer + inner :]
    sums, refs = refs[:ndp], refs[ndp:]
    grad_out, grad_gate, grad_value, grad_taps, product_of, total, sems, sum_sem = refs
    group = product_of.shape[2]
    plane, low = place(inner)
    copies = []

    def send(source, dest, sem):
        copies.append(pltpu.make_async_copy(source, dest, sem))
        copies[-1].start()

    def rows_of(there, where):
        return pl.ds(pl.multiple_of((there * inner + where) * group, ROWS), group)

    for far, part in enumerate(grad_parts):
        for where in range(inner):
            rows = rows_of(plane ^ far, where)
            send(part.at[0, where], grad_value.at[rows, :], sems.at[0, far, where])
    total[...] = sums[0][...]
    for other in sums[1:]:
        total[...] += other[...].astype(jnp.float32)
    send(total, grad_taps, sum_sem.at[0])
    for mask, part in enumerate(conv_parts):
        for there in range(outer):
            rows = rows_of(there, low ^ mask)
            product_of[there, mask] = (
                grad_out[rows, :].astype(jnp.float32) * part[0, there].astype(jnp.float32)
            ).astype(jnp.bfloat16)
            send(product_of.at[there, mask], grad_gate.at[rows, :], sems.at[1, there, mask])
    for copy in copies:
        copy.wait()


def vmem(count):
    return [pl.BlockSpec(memory_space=pltpu.VMEM)] * count


def anywhere(count):
    return [pl.BlockSpec(memory_space=pl.ANY)] * count


def call(kernel, outs, scratch, operands, ins=None, dests=None, mib=4, flops=10**9, after=()):
    count = len(operands)

    def ordered(*refs):
        kernel(*refs[len(after) :])

    return pl.pallas_call(
        ordered,
        out_shape=list(outs),
        in_specs=anywhere(len(after)) + (ins or vmem(count)),
        out_specs=dests or vmem(len(outs)),
        scratch_shapes=scratch,
        compiler_params=pltpu.CompilerParams(vmem_limit_bytes=mib * 1024 * 1024),
        cost_estimate=pl.CostEstimate(flops=flops, bytes_accessed=10**6, transcendentals=0),
        name=kernel.func.__name__,
    )(*after, *operands)


def permute(array, axis, target):
    count = lax.axis_size(axis)
    return lax.ppermute(array, axis, [(i, target(i)) for i in range(count)])


def on_device(grad_out, gate, value, filter_taps):
    nseq = lax.axis_size("seq")
    ndp = lax.axis_size("dp")
    chans = grad_out.shape[1]
    width = grad_out.shape[2]
    group = chans // nseq
    blocks = nseq
    inner = 1 << (nseq.bit_length() - 1) // 2
    outer = nseq // inner
    forward, inverse = (jnp.asarray(t) for t in inner_tables(blocks, width))
    factor = 1.0 / (ndp * math.sqrt(nseq * width))
    shape = jax.ShapeDtypeStruct
    bf16, f32 = jnp.bfloat16, jnp.float32

    def by_plane(count=1):
        return [shape((count, inner, group, width), bf16)] * outer

    def by_low(count=1):
        return [shape((count, outer, group, width), bf16)] * inner

    def arrivals(parts, count=outer - 1):
        return [parts[far] for far in range(outer - 1, outer - 1 - count, -1)]

    def in_plane(parts):
        return [
            permute(part, "seq", lambda i: i ^ mask) if mask else part
            for mask, part in enumerate(parts)
        ]

    def over_planes(found):
        return {
            far: permute(part, "seq", lambda i: i ^ (far * inner)) if far else part
            for far, part in found.items()
        }

    def turned(parts, fars, after=()):
        kernel = functools.partial(turn_kernel, inner, fars)
        outs = call(kernel, by_plane()[: len(fars)], [], parts, after=list(after))
        return dict(zip(fars, outs))

    def ordered(found):
        return [found[far] for far in range(outer)]

    everywhere = tuple(range(outer))

    value_packed = call(
        functools.partial(pack_planes_kernel, inner, outer),
        by_plane(),
        [pltpu.SemaphoreType.DMA((outer, inner))],
        [value[0]],
        ins=anywhere(1),
        mib=16,
    )
    taps_packed = call(
        functools.partial(pack_lows_kernel, inner, outer),
        by_low(),
        [pltpu.SemaphoreType.DMA((inner, outer))],
        [filter_taps],
        ins=anywhere(1),
        mib=16,
        after=value_packed[:1],
    )
    value_plane = ordered(over_planes(dict(enumerate(value_packed))))
    taps_low = in_plane(taps_packed)
    gated_packed = call(
        functools.partial(gated_kernel, inner, outer),
        by_low(),
        [pltpu.VMEM((inner, outer, group, width), bf16)] * 2
        + [pltpu.SemaphoreType.DMA((2, inner, outer))],
        [grad_out[0], gate[0], forward, inverse],
        ins=anywhere(2) + vmem(2),
        mib=16,
        after=taps_low[1:2],
    )
    gated_low = in_plane(gated_packed)
    taps_turned = turned(taps_low, everywhere, list(gated_packed[:1]) + arrivals(value_plane, outer // 4))
    taps_plane = ordered(over_planes(taps_turned))
    value_low = in_plane(
        call(
            functools.partial(turn_back_kernel, inner, outer),
            by_low(),
            [],
            value_plane,
            after=[taps_turned[0]] + arrivals(value_plane),
        )
    )

    spec = shape((blocks + 1, group, 2 * width), f32)
    signal = pltpu.VMEM((blocks, group, width), bf16)
    mid = pltpu.VMEM((blocks + 1, group, 2 * width), bf16)
    back = pltpu.VMEM((blocks + 1, group, 2 * width), f32)
    gated_turned = turned(gated_low, everywhere, arrivals(taps_plane, outer // 4))
    gated_plane = ordered(over_planes(gated_turned))
    spec_taps = call(
        functools.partial(taps_kernel, inner, outer),
        [spec],
        [signal, mid],
        taps_plane + [forward],
        mib=16,
        after=[gated_turned[0]] + arrivals(taps_plane),
    )[0]
    outs = call(
        functools.partial(conv_kernel, inner, outer),
        by_plane() + [spec],
        [signal, mid, back],
        value_low + [spec_taps, forward, inverse],
        mib=16,
    )
    conv_plane = ordered(over_planes(dict(enumerate(outs[:outer]))))
    spec_value = outs[outer]
    wide = (group, blocks // ndp * width)
    outs = call(
        functools.partial(grad_kernel, inner, outer),
        by_low() + [spec],
        [signal, mid, back],
        gated_plane + [spec_taps, forward, inverse],
        mib=16,
        after=arrivals(gated_plane),
    )
    grad_low, spec_gated = in_plane(outs[:inner]), outs[inner]
    sums = list(
        call(
            functools.partial(cross_kernel, ndp, factor),
            [shape(wide, f32)] + [shape(wide, bf16)] * (ndp - 1),
            [pltpu.VMEM((blocks, group, width), f32), back],
            [spec_value, spec_gated, inverse],
            mib=16,
        )
    )
    mine = sums[0]
    for step in range(1, ndp):
        sums[step] = permute(sums[step], "dp", lambda i: (i + step) % ndp)
    grad_turned = turned(grad_low, everywhere, arrivals(conv_plane, outer // 2) + [mine])
    grad_plane = ordered(over_planes(grad_turned))
    conv_low = in_plane(
        call(
            functools.partial(turn_back_kernel, inner, outer),
            by_low(),
            [],
            conv_plane,
            after=[grad_turned[0]],
        )
    )
    grad_gate, grad_value, grad_taps = call(
        functools.partial(final_kernel, inner, outer, ndp),
        [shape((chans, width), bf16)] * 2 + [shape(wide, f32)],
        [
            pltpu.VMEM((outer, inner, group, width), bf16),
            pltpu.VMEM(wide, f32),
            pltpu.SemaphoreType.DMA((2, outer, inner)),
            pltpu.SemaphoreType.DMA((1,)),
        ],
        grad_plane + conv_low + sums + [grad_out[0]],
        dests=anywhere(3),
        mib=8,
        after=arrivals(grad_plane),
    )
    return (grad_gate[None], grad_value[None], grad_taps)


def solution(mesh):
    return jax.shard_map(
        on_device,
        mesh=mesh,
        in_specs=(P("dp", None, "seq"), P("dp", None, "seq"), P("dp", None, "seq"), P(None, "seq")),
        out_specs=(P("dp", None, "seq"), P("dp", None, "seq"), P("seq", "dp")),
        check_vma=False,
    )
```

```python
import functools
import math

import jax
import jax.numpy as jnp
import numpy as np
from jax import lax
from jax.experimental import pallas as pl
from jax.experimental.pallas import tpu as pltpu
from jax.sharding import PartitionSpec as P

ROWS = 16


def inner_tables(blocks, width):
    total = 2 * blocks * width
    pos = np.arange(width)
    tables = []
    for outer in range(blocks + 1):
        turns = pos[:, None] * (outer + 2 * blocks * pos[None, :]) % total
        angle = 2.0 * np.pi / total * turns
        cos, sin = np.cos(angle), np.sin(angle)
        tables.append(np.block([[cos, -sin], [sin, cos]]))
    table = np.stack(tables)
    weight = np.full((blocks + 1, 1, 1), 2.0 / total)
    weight[0] = weight[blocks] = 1.0 / total
    return (
        table.astype(jnp.bfloat16),
        (table.transpose(0, 2, 1) * weight).astype(jnp.bfloat16),
    )


def turn(number, cos, sin):
    real, imag = number
    if abs(sin) < 1e-9:
        return (real, imag) if cos > 0 else (-real, -imag)
    if abs(cos) < 1e-9:
        return (imag, -real) if sin > 0 else (-imag, real)
    return (real * cos + imag * sin, imag * cos - real * sin)


def add(left, right):
    return (left[0] + right[0], left[1] + right[1])


def sub(left, right):
    return (left[0] - right[0], left[1] - right[1])


def complex_dft(items, sign):
    count = len(items)
    if count == 1:
        return items
    half = count // 2
    low, high = items[:half], items[half:]
    even = complex_dft([add(a, b) for a, b in zip(low, high)], sign)
    odd = []
    for n, (a, b) in enumerate(zip(low, high)):
        angle = 2.0 * math.pi * n / count
        odd.append(turn(sub(a, b), math.cos(angle), sign * math.sin(angle)))
    odd = complex_dft(odd, sign)
    return [item for pair in zip(even, odd) for item in pair]


def odd_outputs(items, period):
    quarter = len(items) // 2
    turned = []
    for n in range(quarter):
        angle = 2.0 * math.pi * n / period
        turned.append(turn((items[n], -items[n + quarter]), math.cos(angle), math.sin(angle)))
    found = {}
    for m, (real, imag) in enumerate(complex_dft(turned, 1)):
        freq = 4 * m + 1
        if freq > period // 2:
            freq, imag = period - freq, -imag
        found[freq] = (real, imag)
    return found


def real_dft(items):
    count = len(items)
    if count == 1:
        return {0: (items[0], None)}
    if count == 2:
        return {0: (items[0] + items[1], None), 1: (items[0] - items[1], None)}
    half = count // 2
    low, high = items[:half], items[half:]
    found = {2 * k: v for k, v in real_dft([a + b for a, b in zip(low, high)]).items()}
    found.update(odd_outputs([a - b for a, b in zip(low, high)], count))
    return found


def padded_dft(items):
    found = {2 * k: v for k, v in real_dft(items).items()}
    found.update(odd_outputs(items, 2 * len(items)))
    return found


def odd_inputs(freqs, period):
    quarter = period // 4
    items = []
    for m in range(quarter):
        freq = 4 * m + 1
        if freq > period // 2:
            real, imag = freqs[period - freq]
            items.append((real, -imag))
        else:
            items.append(freqs[freq])
    low, high = [], []
    for n, item in enumerate(complex_dft(items, -1)):
        angle = 2.0 * math.pi * n / period
        real, imag = turn(item, math.cos(angle), -math.sin(angle))
        low.append(real)
        high.append(-imag)
    return low + high


def real_inverse(freqs, count):
    if count == 1:
        return [freqs[0][0]]
    if count == 2:
        return [freqs[0][0] + freqs[1][0], freqs[0][0] - freqs[1][0]]
    even = real_inverse({k // 2: v for k, v in freqs.items() if k % 2 == 0}, count // 2)
    odd = odd_inputs(freqs, count)
    return [a + b for a, b in zip(even, odd)] + [a - b for a, b in zip(even, odd)]


def padded_inverse(freqs, count):
    even = real_inverse({k // 2: v for k, v in freqs.items() if k % 2 == 0}, count)
    return [a + b for a, b in zip(even, odd_inputs(freqs, 2 * count))]


def each(count, body):
    step = max(s for s in range(1, 18) if count % s == 0)

    def several(turn_no, carry):
        for k in range(step):
            body(turn_no * step + k)
        return carry

    if step == count:
        several(0, 0)
    else:
        lax.fori_loop(0, count // step, several, 0)


def outer_forward(source, mid, base):
    blocks, group, width = source.shape

    def body(step, carry):
        start = pl.multiple_of(step * ROWS, ROWS)
        rows = pl.ds(start, ROWS)
        found = padded_dft([source[n, rows, :].astype(jnp.float32) for n in range(blocks)])
        out_rows = pl.ds(pl.multiple_of(start + base, ROWS), ROWS)
        for freq, (real, imag) in found.items():
            if imag is None:
                imag = jnp.zeros_like(real)
            mid[freq, out_rows, 0:width] = real.astype(jnp.bfloat16)
            mid[freq, out_rows, width : 2 * width] = imag.astype(jnp.bfloat16)
        return carry

    lax.fori_loop(0, group // ROWS, body, 0)


def outer_inverse(mid, base, dest):
    blocks, group, width = dest.shape

    def body(step, carry):
        start = pl.multiple_of(step * ROWS, ROWS)
        rows = pl.ds(pl.multiple_of(start + base, ROWS), ROWS)
        freqs = {
            k: (mid[k, rows, 0:width], mid[k, rows, width : 2 * width]) for k in range(blocks + 1)
        }
        for n, item in enumerate(padded_inverse(freqs, blocks)):
            dest[n, pl.ds(start, ROWS), :] = item.astype(dest.dtype)
        return carry

    lax.fori_loop(0, group // ROWS, body, 0)


def product(left, right, width, conjugate):
    left_real, left_imag = left[:, :width], left[:, width:]
    right_real, right_imag = right[:, :width], right[:, width:]
    if conjugate:
        left_imag = -left_imag
    real = left_real * right_real - left_imag * right_imag
    imag = left_real * right_imag + left_imag * right_real
    return jnp.concatenate([real.astype(jnp.bfloat16), imag.astype(jnp.bfloat16)], 1)


def place(inner):
    here = lax.axis_index("seq")
    return here // inner, lax.rem(here, inner)


def pack_planes_kernel(inner, outer, source, *refs):
    parts, sems = refs[:outer], refs[outer]
    group = parts[0].shape[2]
    plane, _ = place(inner)
    copies = []
    for far in range(outer - 1, -1, -1):
        for low in range(inner):
            start = pl.multiple_of(((plane ^ far) * inner + low) * group, ROWS)
            rows = source.at[pl.ds(start, group), :]
            copies.append(pltpu.make_async_copy(rows, parts[far].at[0, low], sems.at[far, low]))
            copies[-1].start()
    for copy in copies:
        copy.wait()


def pack_lows_kernel(inner, outer, source, *refs):
    parts, sems = refs[:inner], refs[inner]
    group = parts[0].shape[2]
    _, low = place(inner)
    copies = []
    for mask, part in enumerate(parts):
        for plane in range(outer):
            start = pl.multiple_of((plane * inner + (low ^ mask)) * group, ROWS)
            rows = source.at[pl.ds(start, group), :]
            copies.append(pltpu.make_async_copy(rows, part.at[0, plane], sems.at[mask, plane]))
            copies[-1].start()
    for copy in copies:
        copy.wait()


def gated_kernel(inner, outer, grad_out, gate, forward, inverse, *refs):
    parts, (left, right, sems) = refs[:inner], refs[inner:]
    group = left.shape[2]
    _, low = place(inner)
    copies = []
    for mask in range(inner):
        for plane in range(outer):
            start = pl.multiple_of((plane * inner + (low ^ mask)) * group, ROWS)
            rows = pl.ds(start, group)
            pair = [
                pltpu.make_async_copy(
                    source.at[rows, :], held.at[mask, plane], sems.at[which, mask, plane]
                )
                for which, (source, held) in enumerate(((grad_out, left), (gate, right)))
            ]
            for copy in pair:
                copy.start()
            copies.append(pair)
    for mask, part in enumerate(parts):
        for plane in range(outer):
            for copy in copies[mask * outer + plane]:
                copy.wait()
            part[0, plane] = (
                left[mask, plane].astype(jnp.float32) * right[mask, plane].astype(jnp.float32)
            ).astype(jnp.bfloat16)


def turn_kernel(inner, fars, *refs):
    parts, outs = refs[:inner], refs[inner:]
    plane, low = place(inner)
    for mask, part in enumerate(parts):
        for far, out in zip(fars, outs):
            for which in range(part.shape[0]):
                out[which, low ^ mask] = part[which, plane ^ far]


def turn_back_kernel(inner, outer, *refs):
    parts, outs = refs[:outer], refs[outer:]
    plane, low = place(inner)
    for far, part in enumerate(parts):
        for mask, out in enumerate(outs):
            for which in range(part.shape[0]):
                out[which, plane ^ far] = part[which, low ^ mask]


def hold_kernel(*refs):
    half = len(refs) // 2
    for source, dest in zip(refs[:half], refs[half:]):
        dest[...] = source[...]


def gather_planes(inner, outer, parts, signal):
    plane, _ = place(inner)
    for far, part in enumerate(parts):
        for low in range(inner):
            signal[(plane ^ far) * inner + low] = part[0, low]


def gather_lows(inner, outer, parts, signal):
    _, low = place(inner)
    for mask, part in enumerate(parts):
        for plane in range(outer):
            signal[plane * inner + (low ^ mask)] = part[0, plane]


def scatter(inner, outer, signal, outs):
    _, low = place(inner)
    for mask, out in enumerate(outs):
        for plane in range(outer):
            out[0, plane] = signal[plane * inner + (low ^ mask)]


def taps_kernel(inner, outer, *refs):
    parts, (forward, spec, signal, mid) = refs[:outer], refs[outer:]
    gather_planes(inner, outer, parts, signal)
    outer_forward(signal, mid, 0)

    def body(k):
        spec[k] = jnp.dot(mid[k], forward[k], preferred_element_type=jnp.float32)

    each(mid.shape[0], body)


def conv_kernel(inner, outer, *refs):
    parts, (spec_taps, forward, inverse) = refs[:inner], refs[inner : inner + 3]
    outs, (spec, signal, mid, back) = refs[inner + 3 : -4], refs[-4:]
    width = signal.shape[2]
    gather_lows(inner, outer, parts, signal)
    outer_forward(signal, mid, 0)

    def body(k):
        value = jnp.dot(mid[k], forward[k], preferred_element_type=jnp.float32)
        spec[k] = value
        back[k] = jnp.dot(
            product(spec_taps[k], value, width, False),
            inverse[k],
            preferred_element_type=jnp.float32,
        )

    each(mid.shape[0], body)
    outer_inverse(back, 0, signal)
    plane, _ = place(inner)
    for far, out in enumerate(outs):
        for low in range(inner):
            out[0, low] = signal[(plane ^ far) * inner + low]


def grad_kernel(inner, outer, *refs):
    parts, (spec_taps, forward, inverse) = refs[:outer], refs[outer : outer + 3]
    outs, (spec, signal, mid, back) = refs[outer + 3 : -4], refs[-4:]
    width = signal.shape[2]
    gather_planes(inner, outer, parts, signal)
    outer_forward(signal, mid, 0)

    def body(k):
        gated = jnp.dot(mid[k], forward[k], preferred_element_type=jnp.float32)
        spec[k] = gated
        back[k] = jnp.dot(
            product(spec_taps[k], gated, width, True),
            inverse[k],
            preferred_element_type=jnp.float32,
        )

    each(mid.shape[0], body)
    outer_inverse(back, 0, signal)
    scatter(inner, outer, signal, outs)


def cross_kernel(ndp, factor, spec_value, spec_gated, inverse, *refs):
    sums, (cross, back) = refs[:ndp], refs[ndp:]
    blocks, _, width = cross.shape

    def body(k):
        back[k] = jnp.dot(
            product(spec_value[k], spec_gated[k], width, True),
            inverse[k],
            preferred_element_type=jnp.float32,
        )

    each(back.shape[0], body)
    outer_inverse(back, 0, cross)
    share = blocks // ndp
    for step, total in enumerate(sums):
        first = lax.rem(lax.axis_index("dp") + step, ndp) * share
        for n in range(share):
            total[:, n * width : (n + 1) * width] = (cross[first + n] * factor).astype(total.dtype)


def final_kernel(inner, outer, ndp, *refs):
    grad_parts, conv_parts, refs = refs[:outer], refs[outer : outer + inner], refs[outer + inner :]
    sums, refs = refs[:ndp], refs[ndp:]
    grad_out, grad_gate, grad_value, grad_taps, product_of, total, sems, sum_sem = refs
    group = product_of.shape[2]
    plane, low = place(inner)
    copies = []

    def send(source, dest, sem):
        copies.append(pltpu.make_async_copy(source, dest, sem))
        copies[-1].start()

    def rows_of(there, where):
        return pl.ds(pl.multiple_of((there * inner + where) * group, ROWS), group)

    for far, part in enumerate(grad_parts):
        for where in range(inner):
            rows = rows_of(plane ^ far, where)
            send(part.at[0, where], grad_value.at[rows, :], sems.at[0, far, where])
    total[...] = sums[0][...]
    for other in sums[1:]:
        total[...] += other[...].astype(jnp.float32)
    send(total, grad_taps, sum_sem.at[0])
    for mask, part in enumerate(conv_parts):
        for there in range(outer):
            rows = rows_of(there, low ^ mask)
            product_of[there, mask] = (
                grad_out[rows, :].astype(jnp.float32) * part[0, there].astype(jnp.float32)
            ).astype(jnp.bfloat16)
            send(product_of.at[there, mask], grad_gate.at[rows, :], sems.at[1, there, mask])
    for copy in copies:
        copy.wait()


def vmem(count):
    return [pl.BlockSpec(memory_space=pltpu.VMEM)] * count


def anywhere(count):
    return [pl.BlockSpec(memory_space=pl.ANY)] * count


def call(kernel, outs, scratch, operands, ins=None, dests=None, mib=4, flops=10**9, after=()):
    count = len(operands)

    def ordered(*refs):
        kernel(*refs[len(after) :])

    return pl.pallas_call(
        ordered,
        out_shape=list(outs),
        in_specs=anywhere(len(after)) + (ins or vmem(count)),
        out_specs=dests or vmem(len(outs)),
        scratch_shapes=scratch,
        compiler_params=pltpu.CompilerParams(vmem_limit_bytes=mib * 1024 * 1024),
        cost_estimate=pl.CostEstimate(flops=flops, bytes_accessed=10**6, transcendentals=0),
        name=kernel.func.__name__,
    )(*after, *operands)


def permute(array, axis, target):
    count = lax.axis_size(axis)
    return lax.ppermute(array, axis, [(i, target(i)) for i in range(count)])


def on_device(grad_out, gate, value, filter_taps):
    nseq = lax.axis_size("seq")
    ndp = lax.axis_size("dp")
    chans = grad_out.shape[1]
    width = grad_out.shape[2]
    group = chans // nseq
    blocks = nseq
    inner = 1 << (nseq.bit_length() - 1) // 2
    outer = nseq // inner
    forward, inverse = (jnp.asarray(t) for t in inner_tables(blocks, width))
    factor = 1.0 / (ndp * math.sqrt(nseq * width))
    shape = jax.ShapeDtypeStruct
    bf16, f32 = jnp.bfloat16, jnp.float32

    def by_plane(count=1):
        return [shape((count, inner, group, width), bf16)] * outer

    def by_low(count=1):
        return [shape((count, outer, group, width), bf16)] * inner

    def arrivals(parts, count=outer - 1):
        return [parts[far] for far in range(outer - 1, outer - 1 - count, -1)]

    def in_plane(parts):
        return [
            permute(part, "seq", lambda i: i ^ mask) if mask else part
            for mask, part in enumerate(parts)
        ]

    def over_planes(found):
        return {
            far: permute(part, "seq", lambda i: i ^ (far * inner)) if far else part
            for far, part in found.items()
        }

    def turned(parts, fars, after=()):
        kernel = functools.partial(turn_kernel, inner, fars)
        outs = call(kernel, by_plane()[: len(fars)], [], parts, after=list(after))
        return dict(zip(fars, outs))

    def ordered(found):
        return [found[far] for far in range(outer)]

    everywhere = tuple(range(outer))

    value_packed = call(
        functools.partial(pack_planes_kernel, inner, outer),
        by_plane(),
        [pltpu.SemaphoreType.DMA((outer, inner))],
        [value[0]],
        ins=anywhere(1),
        mib=16,
    )
    taps_packed = call(
        functools.partial(pack_lows_kernel, inner, outer),
        by_low(),
        [pltpu.SemaphoreType.DMA((inner, outer))],
        [filter_taps],
        ins=anywhere(1),
        mib=16,
        after=value_packed[:1],
    )
    value_plane = ordered(over_planes(dict(enumerate(value_packed))))
    taps_low = in_plane(taps_packed)
    gated_packed = call(
        functools.partial(gated_kernel, inner, outer),
        by_low(),
        [pltpu.VMEM((inner, outer, group, width), bf16)] * 2
        + [pltpu.SemaphoreType.DMA((2, inner, outer))],
        [grad_out[0], gate[0], forward, inverse],
        ins=anywhere(2) + vmem(2),
        mib=16,
        after=taps_low[1:2],
    )
    gated_low = in_plane(gated_packed)
    taps_turned = turned(taps_low, everywhere, list(gated_packed[:1]) + arrivals(value_plane, outer // 4))
    taps_plane = ordered(over_planes(taps_turned))
    value_low = in_plane(
        call(
            functools.partial(turn_back_kernel, inner, outer),
            by_low(),
            [],
            value_plane,
            after=[taps_turned[0]] + arrivals(value_plane),
        )
    )

    spec = shape((blocks + 1, group, 2 * width), f32)
    signal = pltpu.VMEM((blocks, group, width), bf16)
    mid = pltpu.VMEM((blocks + 1, group, 2 * width), bf16)
    back = pltpu.VMEM((blocks + 1, group, 2 * width), f32)
    gated_turned = turned(gated_low, everywhere, arrivals(taps_plane, outer // 4))
    gated_plane = ordered(over_planes(gated_turned))
    spec_taps = call(
        functools.partial(taps_kernel, inner, outer),
        [spec],
        [signal, mid],
        taps_plane + [forward],
        mib=16,
        after=[gated_turned[0]] + arrivals(taps_plane),
    )[0]
    outs = call(
        functools.partial(conv_kernel, inner, outer),
        by_plane() + [spec],
        [signal, mid, back],
        value_low + [spec_taps, forward, inverse],
        mib=16,
    )
    held = call(
        functools.partial(hold_kernel), by_plane(), [], outs[:outer], after=arrivals(gated_plane, outer // 2)
    )
    conv_plane = ordered(over_planes(dict(enumerate(held))))
    spec_value = outs[outer]
    wide = (group, blocks // ndp * width)
    outs = call(
        functools.partial(grad_kernel, inner, outer),
        by_low() + [spec],
        [signal, mid, back],
        gated_plane + [spec_taps, forward, inverse],
        mib=16,
        after=[held[0]] + arrivals(gated_plane),
    )
    grad_low, spec_gated = in_plane(outs[:inner]), outs[inner]
    sums = list(
        call(
            functools.partial(cross_kernel, ndp, factor),
            [shape(wide, f32)] + [shape(wide, bf16)] * (ndp - 1),
            [pltpu.VMEM((blocks, group, width), f32), back],
            [spec_value, spec_gated, inverse],
            mib=16,
        )
    )
    mine = sums[0]
    for step in range(1, ndp):
        sums[step] = permute(sums[step], "dp", lambda i: (i + step) % ndp)
    grad_turned = turned(grad_low, everywhere, arrivals(conv_plane, outer // 2) + [mine])
    grad_plane = ordered(over_planes(grad_turned))
    conv_low = in_plane(
        call(
            functools.partial(turn_back_kernel, inner, outer),
            by_low(),
            [],
            conv_plane,
            after=[grad_turned[0]] + sums[1:],
        )
    )
    grad_gate, grad_value, grad_taps = call(
        functools.partial(final_kernel, inner, outer, ndp),
        [shape((chans, width), bf16)] * 2 + [shape(wide, f32)],
        [
            pltpu.VMEM((outer, inner, group, width), bf16),
            pltpu.VMEM(wide, f32),
            pltpu.SemaphoreType.DMA((2, outer, inner)),
            pltpu.SemaphoreType.DMA((1,)),
        ],
        grad_plane + conv_low + sums + [grad_out[0]],
        dests=anywhere(3),
        mib=8,
        after=arrivals(grad_plane),
    )
    return (grad_gate[None], grad_value[None], grad_taps)


def solution(mesh):
    return jax.shard_map(
        on_device,
        mesh=mesh,
        in_specs=(P("dp", None, "seq"), P("dp", None, "seq"), P("dp", None, "seq"), P(None, "seq")),
        out_specs=(P("dp", None, "seq"), P("dp", None, "seq"), P("seq", "dp")),
        check_vma=False,
    )
```

```python
import functools
import math

import jax
import jax.numpy as jnp
import numpy as np
from jax import lax
from jax.experimental import pallas as pl
from jax.experimental.pallas import tpu as pltpu
from jax.sharding import PartitionSpec as P

ROWS = 16


def inner_tables(blocks, width):
    total = 2 * blocks * width
    pos = np.arange(width)
    tables = []
    for outer in range(blocks + 1):
        turns = pos[:, None] * (outer + 2 * blocks * pos[None, :]) % total
        angle = 2.0 * np.pi / total * turns
        cos, sin = np.cos(angle), np.sin(angle)
        tables.append(np.block([[cos, -sin], [sin, cos]]))
    table = np.stack(tables)
    weight = np.full((blocks + 1, 1, 1), 2.0 / total)
    weight[0] = weight[blocks] = 1.0 / total
    return (
        table.astype(jnp.bfloat16),
        (table.transpose(0, 2, 1) * weight).astype(jnp.bfloat16),
    )


def turn(number, cos, sin):
    real, imag = number
    if abs(sin) < 1e-9:
        return (real, imag) if cos > 0 else (-real, -imag)
    if abs(cos) < 1e-9:
        return (imag, -real) if sin > 0 else (-imag, real)
    return (real * cos + imag * sin, imag * cos - real * sin)


def add(left, right):
    return (left[0] + right[0], left[1] + right[1])


def sub(left, right):
    return (left[0] - right[0], left[1] - right[1])


def complex_dft(items, sign):
    count = len(items)
    if count == 1:
        return items
    half = count // 2
    low, high = items[:half], items[half:]
    even = complex_dft([add(a, b) for a, b in zip(low, high)], sign)
    odd = []
    for n, (a, b) in enumerate(zip(low, high)):
        angle = 2.0 * math.pi * n / count
        odd.append(turn(sub(a, b), math.cos(angle), sign * math.sin(angle)))
    odd = complex_dft(odd, sign)
    return [item for pair in zip(even, odd) for item in pair]


def odd_outputs(items, period):
    quarter = len(items) // 2
    turned = []
    for n in range(quarter):
        angle = 2.0 * math.pi * n / period
        turned.append(turn((items[n], -items[n + quarter]), math.cos(angle), math.sin(angle)))
    found = {}
    for m, (real, imag) in enumerate(complex_dft(turned, 1)):
        freq = 4 * m + 1
        if freq > period // 2:
            freq, imag = period - freq, -imag
        found[freq] = (real, imag)
    return found


def real_dft(items):
    count = len(items)
    if count == 1:
        return {0: (items[0], None)}
    if count == 2:
        return {0: (items[0] + items[1], None), 1: (items[0] - items[1], None)}
    half = count // 2
    low, high = items[:half], items[half:]
    found = {2 * k: v for k, v in real_dft([a + b for a, b in zip(low, high)]).items()}
    found.update(odd_outputs([a - b for a, b in zip(low, high)], count))
    return found


def padded_dft(items):
    found = {2 * k: v for k, v in real_dft(items).items()}
    found.update(odd_outputs(items, 2 * len(items)))
    return found


def odd_inputs(freqs, period):
    quarter = period // 4
    items = []
    for m in range(quarter):
        freq = 4 * m + 1
        if freq > period // 2:
            real, imag = freqs[period - freq]
            items.append((real, -imag))
        else:
            items.append(freqs[freq])
    low, high = [], []
    for n, item in enumerate(complex_dft(items, -1)):
        angle = 2.0 * math.pi * n / period
        real, imag = turn(item, math.cos(angle), -math.sin(angle))
        low.append(real)
        high.append(-imag)
    return low + high


def real_inverse(freqs, count):
    if count == 1:
        return [freqs[0][0]]
    if count == 2:
        return [freqs[0][0] + freqs[1][0], freqs[0][0] - freqs[1][0]]
    even = real_inverse({k // 2: v for k, v in freqs.items() if k % 2 == 0}, count // 2)
    odd = odd_inputs(freqs, count)
    return [a + b for a, b in zip(even, odd)] + [a - b for a, b in zip(even, odd)]


def padded_inverse(freqs, count):
    even = real_inverse({k // 2: v for k, v in freqs.items() if k % 2 == 0}, count)
    return [a + b for a, b in zip(even, odd_inputs(freqs, 2 * count))]


def each(count, body):
    step = max(s for s in range(1, 18) if count % s == 0)

    def several(turn_no, carry):
        for k in range(step):
            body(turn_no * step + k)
        return carry

    if step == count:
        several(0, 0)
    else:
        lax.fori_loop(0, count // step, several, 0)


def outer_forward(source, mid, base):
    blocks, group, width = source.shape

    def body(step, carry):
        start = pl.multiple_of(step * ROWS, ROWS)
        rows = pl.ds(start, ROWS)
        found = padded_dft([source[n, rows, :].astype(jnp.float32) for n in range(blocks)])
        out_rows = pl.ds(pl.multiple_of(start + base, ROWS), ROWS)
        for freq, (real, imag) in found.items():
            if imag is None:
                imag = jnp.zeros_like(real)
            mid[freq, out_rows, 0:width] = real.astype(jnp.bfloat16)
            mid[freq, out_rows, width : 2 * width] = imag.astype(jnp.bfloat16)
        return carry

    lax.fori_loop(0, group // ROWS, body, 0)


def outer_inverse(mid, base, dest):
    blocks, group, width = dest.shape

    def body(step, carry):
        start = pl.multiple_of(step * ROWS, ROWS)
        rows = pl.ds(pl.multiple_of(start + base, ROWS), ROWS)
        freqs = {
            k: (mid[k, rows, 0:width], mid[k, rows, width : 2 * width]) for k in range(blocks + 1)
        }
        for n, item in enumerate(padded_inverse(freqs, blocks)):
            dest[n, pl.ds(start, ROWS), :] = item.astype(dest.dtype)
        return carry

    lax.fori_loop(0, group // ROWS, body, 0)


def product(left, right, width, conjugate):
    left_real, left_imag = left[:, :width], left[:, width:]
    right_real, right_imag = right[:, :width], right[:, width:]
    if conjugate:
        left_imag = -left_imag
    real = left_real * right_real - left_imag * right_imag
    imag = left_real * right_imag + left_imag * right_real
    return jnp.concatenate([real.astype(jnp.bfloat16), imag.astype(jnp.bfloat16)], 1)


def place(inner):
    here = lax.axis_index("seq")
    return here // inner, lax.rem(here, inner)


def pack_planes_kernel(inner, outer, source, *refs):
    parts, sems = refs[:outer], refs[outer]
    group = parts[0].shape[2]
    plane, _ = place(inner)
    copies = []
    for far in range(outer - 1, -1, -1):
        for low in range(inner):
            start = pl.multiple_of(((plane ^ far) * inner + low) * group, ROWS)
            rows = source.at[pl.ds(start, group), :]
            copies.append(pltpu.make_async_copy(rows, parts[far].at[0, low], sems.at[far, low]))
            copies[-1].start()
    for copy in copies:
        copy.wait()


def pack_lows_kernel(inner, outer, source, *refs):
    parts, sems = refs[:inner], refs[inner]
    group = parts[0].shape[2]
    _, low = place(inner)
    copies = []
    for mask, part in enumerate(parts):
        for plane in range(outer):
            start = pl.multiple_of((plane * inner + (low ^ mask)) * group, ROWS)
            rows = source.at[pl.ds(start, group), :]
            copies.append(pltpu.make_async_copy(rows, part.at[0, plane], sems.at[mask, plane]))
            copies[-1].start()
    for copy in copies:
        copy.wait()


def gated_kernel(inner, outer, grad_out, gate, forward, inverse, *refs):
    parts, (left, right, sems) = refs[:inner], refs[inner:]
    group = left.shape[2]
    _, low = place(inner)
    copies = []
    for mask in range(inner):
        for plane in range(outer):
            start = pl.multiple_of((plane * inner + (low ^ mask)) * group, ROWS)
            rows = pl.ds(start, group)
            pair = [
                pltpu.make_async_copy(
                    source.at[rows, :], held.at[mask, plane], sems.at[which, mask, plane]
                )
                for which, (source, held) in enumerate(((grad_out, left), (gate, right)))
            ]
            for copy in pair:
                copy.start()
            copies.append(pair)
    for mask, part in enumerate(parts):
        for plane in range(outer):
            for copy in copies[mask * outer + plane]:
                copy.wait()
            part[0, plane] = (
                left[mask, plane].astype(jnp.float32) * right[mask, plane].astype(jnp.float32)
            ).astype(jnp.bfloat16)


def turn_kernel(inner, fars, *refs):
    parts, outs = refs[:inner], refs[inner:]
    plane, low = place(inner)
    for mask, part in enumerate(parts):
        for far, out in zip(fars, outs):
            for which in range(part.shape[0]):
                out[which, low ^ mask] = part[which, plane ^ far]


def turn_back_kernel(inner, outer, *refs):
    parts, outs = refs[:outer], refs[outer:]
    plane, low = place(inner)
    for far, part in enumerate(parts):
        for mask, out in enumerate(outs):
            for which in range(part.shape[0]):
                out[which, plane ^ far] = part[which, low ^ mask]


def hold_kernel(*refs):
    half = len(refs) // 2
    for source, dest in zip(refs[:half], refs[half:]):
        dest[...] = source[...]


def gather_planes(inner, outer, parts, signal):
    plane, _ = place(inner)
    for far, part in enumerate(parts):
        for low in range(inner):
            signal[(plane ^ far) * inner + low] = part[0, low]


def gather_lows(inner, outer, parts, signal):
    _, low = place(inner)
    for mask, part in enumerate(parts):
        for plane in range(outer):
            signal[plane * inner + (low ^ mask)] = part[0, plane]


def scatter(inner, outer, signal, outs):
    _, low = place(inner)
    for mask, out in enumerate(outs):
        for plane in range(outer):
            out[0, plane] = signal[plane * inner + (low ^ mask)]


def taps_kernel(inner, outer, *refs):
    parts, (forward, spec, signal, mid) = refs[:outer], refs[outer:]
    gather_planes(inner, outer, parts, signal)
    outer_forward(signal, mid, 0)

    def body(k):
        spec[k] = jnp.dot(mid[k], forward[k], preferred_element_type=jnp.float32)

    each(mid.shape[0], body)


def conv_kernel(inner, outer, *refs):
    parts, (spec_taps, forward, inverse) = refs[:inner], refs[inner : inner + 3]
    outs, (spec, signal, mid, back) = refs[inner + 3 : -4], refs[-4:]
    width = signal.shape[2]
    gather_lows(inner, outer, parts, signal)
    outer_forward(signal, mid, 0)

    def body(k):
        value = jnp.dot(mid[k], forward[k], preferred_element_type=jnp.float32)
        spec[k] = value
        back[k] = jnp.dot(
            product(spec_taps[k], value, width, False),
            inverse[k],
            preferred_element_type=jnp.float32,
        )

    each(mid.shape[0], body)
    outer_inverse(back, 0, signal)
    plane, _ = place(inner)
    for far, out in enumerate(outs):
        for low in range(inner):
            out[0, low] = signal[(plane ^ far) * inner + low]


def grad_kernel(inner, outer, *refs):
    parts, (spec_taps, forward, inverse) = refs[:outer], refs[outer : outer + 3]
    outs, (spec, signal, mid, back) = refs[outer + 3 : -4], refs[-4:]
    width = signal.shape[2]
    gather_planes(inner, outer, parts, signal)
    outer_forward(signal, mid, 0)

    def body(k):
        gated = jnp.dot(mid[k], forward[k], preferred_element_type=jnp.float32)
        spec[k] = gated
        back[k] = jnp.dot(
            product(spec_taps[k], gated, width, True),
            inverse[k],
            preferred_element_type=jnp.float32,
        )

    each(mid.shape[0], body)
    outer_inverse(back, 0, signal)
    scatter(inner, outer, signal, outs)


def cross_kernel(ndp, factor, spec_value, spec_gated, inverse, *refs):
    sums, (cross, back) = refs[:ndp], refs[ndp:]
    blocks, _, width = cross.shape

    def body(k):
        back[k] = jnp.dot(
            product(spec_value[k], spec_gated[k], width, True),
            inverse[k],
            preferred_element_type=jnp.float32,
        )

    each(back.shape[0], body)
    outer_inverse(back, 0, cross)
    share = blocks // ndp
    for step, total in enumerate(sums):
        first = lax.rem(lax.axis_index("dp") + step, ndp) * share
        for n in range(share):
            total[:, n * width : (n + 1) * width] = (cross[first + n] * factor).astype(total.dtype)


def final_kernel(inner, outer, ndp, *refs):
    grad_parts, conv_parts, refs = refs[:outer], refs[outer : outer + inner], refs[outer + inner :]
    sums, refs = refs[:ndp], refs[ndp:]
    grad_out, grad_gate, grad_value, grad_taps, product_of, total, sems, sum_sem = refs
    group = product_of.shape[2]
    plane, low = place(inner)
    copies = []

    def send(source, dest, sem):
        copies.append(pltpu.make_async_copy(source, dest, sem))
        copies[-1].start()

    def rows_of(there, where):
        return pl.ds(pl.multiple_of((there * inner + where) * group, ROWS), group)

    for far, part in enumerate(grad_parts):
        for where in range(inner):
            rows = rows_of(plane ^ far, where)
            send(part.at[0, where], grad_value.at[rows, :], sems.at[0, far, where])
    total[...] = sums[0][...]
    for other in sums[1:]:
        total[...] += other[...].astype(jnp.float32)
    send(total, grad_taps, sum_sem.at[0])
    for mask, part in enumerate(conv_parts):
        for there in range(outer):
            rows = rows_of(there, low ^ mask)
            product_of[there, mask] = (
                grad_out[rows, :].astype(jnp.float32) * part[0, there].astype(jnp.float32)
            ).astype(jnp.bfloat16)
            send(product_of.at[there, mask], grad_gate.at[rows, :], sems.at[1, there, mask])
    for copy in copies:
        copy.wait()


def vmem(count):
    return [pl.BlockSpec(memory_space=pltpu.VMEM)] * count


def anywhere(count):
    return [pl.BlockSpec(memory_space=pl.ANY)] * count


def call(kernel, outs, scratch, operands, ins=None, dests=None, mib=4, flops=10**9, after=()):
    count = len(operands)

    def ordered(*refs):
        kernel(*refs[len(after) :])

    return pl.pallas_call(
        ordered,
        out_shape=list(outs),
        in_specs=anywhere(len(after)) + (ins or vmem(count)),
        out_specs=dests or vmem(len(outs)),
        scratch_shapes=scratch,
        compiler_params=pltpu.CompilerParams(vmem_limit_bytes=mib * 1024 * 1024),
        cost_estimate=pl.CostEstimate(flops=flops, bytes_accessed=10**6, transcendentals=0),
        name=kernel.func.__name__,
    )(*after, *operands)


def permute(array, axis, target):
    count = lax.axis_size(axis)
    return lax.ppermute(array, axis, [(i, target(i)) for i in range(count)])


def on_device(grad_out, gate, value, filter_taps):
    nseq = lax.axis_size("seq")
    ndp = lax.axis_size("dp")
    chans = grad_out.shape[1]
    width = grad_out.shape[2]
    group = chans // nseq
    blocks = nseq
    inner = 1 << (nseq.bit_length() - 1) // 2
    outer = nseq // inner
    forward, inverse = (jnp.asarray(t) for t in inner_tables(blocks, width))
    factor = 1.0 / (ndp * math.sqrt(nseq * width))
    shape = jax.ShapeDtypeStruct
    bf16, f32 = jnp.bfloat16, jnp.float32

    def by_plane(count=1):
        return [shape((count, inner, group, width), bf16)] * outer

    def by_low(count=1):
        return [shape((count, outer, group, width), bf16)] * inner

    def arrivals(parts, count=outer - 1):
        return [parts[far] for far in range(outer - 1, outer - 1 - count, -1)]

    def in_plane(parts):
        return [
            permute(part, "seq", lambda i: i ^ mask) if mask else part
            for mask, part in enumerate(parts)
        ]

    def over_planes(found):
        return {
            far: permute(part, "seq", lambda i: i ^ (far * inner)) if far else part
            for far, part in found.items()
        }

    def turned(parts, fars, after=()):
        kernel = functools.partial(turn_kernel, inner, fars)
        outs = call(kernel, by_plane()[: len(fars)], [], parts, after=list(after))
        return dict(zip(fars, outs))

    def ordered(found):
        return [found[far] for far in range(outer)]

    everywhere = tuple(range(outer))

    value_packed = call(
        functools.partial(pack_planes_kernel, inner, outer),
        by_plane(),
        [pltpu.SemaphoreType.DMA((outer, inner))],
        [value[0]],
        ins=anywhere(1),
        mib=16,
    )
    taps_packed = call(
        functools.partial(pack_lows_kernel, inner, outer),
        by_low(),
        [pltpu.SemaphoreType.DMA((inner, outer))],
        [filter_taps],
        ins=anywhere(1),
        mib=16,
        after=value_packed[:1],
    )
    value_plane = ordered(over_planes(dict(enumerate(value_packed))))
    taps_low = in_plane(taps_packed)
    gated_packed = call(
        functools.partial(gated_kernel, inner, outer),
        by_low(),
        [pltpu.VMEM((inner, outer, group, width), bf16)] * 2
        + [pltpu.SemaphoreType.DMA((2, inner, outer))],
        [grad_out[0], gate[0], forward, inverse],
        ins=anywhere(2) + vmem(2),
        mib=16,
        after=taps_low[1:2],
    )
    gated_low = in_plane(gated_packed)
    taps_turned = turned(taps_low, everywhere, list(gated_packed[:1]) + arrivals(value_plane, outer // 4))
    taps_plane = ordered(over_planes(taps_turned))
    value_low = in_plane(
        call(
            functools.partial(turn_back_kernel, inner, outer),
            by_low(),
            [],
            value_plane,
            after=[taps_turned[0]] + arrivals(value_plane),
        )
    )

    spec = shape((blocks + 1, group, 2 * width), f32)
    signal = pltpu.VMEM((blocks, group, width), bf16)
    mid = pltpu.VMEM((blocks + 1, group, 2 * width), bf16)
    back = pltpu.VMEM((blocks + 1, group, 2 * width), f32)
    gated_turned = turned(gated_low, everywhere, arrivals(taps_plane, outer // 4))
    gated_plane = ordered(over_planes(gated_turned))
    spec_taps = call(
        functools.partial(taps_kernel, inner, outer),
        [spec],
        [signal, mid],
        taps_plane + [forward],
        mib=16,
        after=[gated_turned[0]] + arrivals(taps_plane),
    )[0]
    outs = call(
        functools.partial(conv_kernel, inner, outer),
        by_plane() + [spec],
        [signal, mid, back],
        value_low + [spec_taps, forward, inverse],
        mib=16,
    )
    held = call(
        functools.partial(hold_kernel), by_plane(), [], outs[:outer], after=arrivals(gated_plane, outer // 2)
    )
    conv_plane = ordered(over_planes(dict(enumerate(held))))
    spec_value = outs[outer]
    wide = (group, blocks // ndp * width)
    outs = call(
        functools.partial(grad_kernel, inner, outer),
        by_low() + [spec],
        [signal, mid, back],
        gated_plane + [spec_taps, forward, inverse],
        mib=16,
        after=[held[0]] + arrivals(gated_plane),
    )
    grad_low, spec_gated = in_plane(outs[:inner]), outs[inner]
    sums = list(
        call(
            functools.partial(cross_kernel, ndp, factor),
            [shape(wide, f32)] + [shape(wide, bf16)] * (ndp - 1),
            [pltpu.VMEM((blocks, group, width), f32), back],
            [spec_value, spec_gated, inverse],
            mib=16,
        )
    )
    mine = sums[0]
    for step in range(1, ndp):
        sums[step] = permute(sums[step], "dp", lambda i: (i + step) % ndp)
    grad_turned = turned(grad_low, everywhere, arrivals(conv_plane, outer // 2) + [mine])
    grad_plane = ordered(over_planes(grad_turned))
    conv_low = in_plane(
        call(
            functools.partial(turn_back_kernel, inner, outer),
            by_low(),
            [],
            conv_plane,
            after=grad_plane[1:2] + sums[1:],
        )
    )
    grad_gate, grad_value, grad_taps = call(
        functools.partial(final_kernel, inner, outer, ndp),
        [shape((chans, width), bf16)] * 2 + [shape(wide, f32)],
        [
            pltpu.VMEM((outer, inner, group, width), bf16),
            pltpu.VMEM(wide, f32),
            pltpu.SemaphoreType.DMA((2, outer, inner)),
            pltpu.SemaphoreType.DMA((1,)),
        ],
        grad_plane + conv_low + sums + [grad_out[0]],
        dests=anywhere(3),
        mib=8,
        after=grad_plane[1:2] + arrivals(grad_plane),
    )
    return (grad_gate[None], grad_value[None], grad_taps)


def solution(mesh):
    return jax.shard_map(
        on_device,
        mesh=mesh,
        in_specs=(P("dp", None, "seq"), P("dp", None, "seq"), P("dp", None, "seq"), P(None, "seq")),
        out_specs=(P("dp", None, "seq"), P("dp", None, "seq"), P("seq", "dp")),
        check_vma=False,
    )
```

```python
import functools
import math

import jax
import jax.numpy as jnp
import numpy as np
from jax import lax
from jax.experimental import pallas as pl
from jax.experimental.pallas import tpu as pltpu
from jax.sharding import PartitionSpec as P

ROWS = 16


def inner_tables(blocks, width):
    total = 2 * blocks * width
    pos = np.arange(width)
    tables = []
    for outer in range(blocks + 1):
        turns = pos[:, None] * (outer + 2 * blocks * pos[None, :]) % total
        angle = 2.0 * np.pi / total * turns
        cos, sin = np.cos(angle), np.sin(angle)
        tables.append(np.block([[cos, -sin], [sin, cos]]))
    table = np.stack(tables)
    weight = np.full((blocks + 1, 1, 1), 2.0 / total)
    weight[0] = weight[blocks] = 1.0 / total
    return (
        table.astype(jnp.bfloat16),
        (table.transpose(0, 2, 1) * weight).astype(jnp.bfloat16),
    )


def turn(number, cos, sin):
    real, imag = number
    if abs(sin) < 1e-9:
        return (real, imag) if cos > 0 else (-real, -imag)
    if abs(cos) < 1e-9:
        return (imag, -real) if sin > 0 else (-imag, real)
    return (real * cos + imag * sin, imag * cos - real * sin)


def add(left, right):
    return (left[0] + right[0], left[1] + right[1])


def sub(left, right):
    return (left[0] - right[0], left[1] - right[1])


def complex_dft(items, sign):
    count = len(items)
    if count == 1:
        return items
    half = count // 2
    low, high = items[:half], items[half:]
    even = complex_dft([add(a, b) for a, b in zip(low, high)], sign)
    odd = []
    for n, (a, b) in enumerate(zip(low, high)):
        angle = 2.0 * math.pi * n / count
        odd.append(turn(sub(a, b), math.cos(angle), sign * math.sin(angle)))
    odd = complex_dft(odd, sign)
    return [item for pair in zip(even, odd) for item in pair]


def odd_outputs(items, period):
    quarter = len(items) // 2
    turned = []
    for n in range(quarter):
        angle = 2.0 * math.pi * n / period
        turned.append(turn((items[n], -items[n + quarter]), math.cos(angle), math.sin(angle)))
    found = {}
    for m, (real, imag) in enumerate(complex_dft(turned, 1)):
        freq = 4 * m + 1
        if freq > period // 2:
            freq, imag = period - freq, -imag
        found[freq] = (real, imag)
    return found


def real_dft(items):
    count = len(items)
    if count == 1:
        return {0: (items[0], None)}
    if count == 2:
        return {0: (items[0] + items[1], None), 1: (items[0] - items[1], None)}
    half = count // 2
    low, high = items[:half], items[half:]
    found = {2 * k: v for k, v in real_dft([a + b for a, b in zip(low, high)]).items()}
    found.update(odd_outputs([a - b for a, b in zip(low, high)], count))
    return found


def padded_dft(items):
    found = {2 * k: v for k, v in real_dft(items).items()}
    found.update(odd_outputs(items, 2 * len(items)))
    return found


def odd_inputs(freqs, period):
    quarter = period // 4
    items = []
    for m in range(quarter):
        freq = 4 * m + 1
        if freq > period // 2:
            real, imag = freqs[period - freq]
            items.append((real, -imag))
        else:
            items.append(freqs[freq])
    low, high = [], []
    for n, item in enumerate(complex_dft(items, -1)):
        angle = 2.0 * math.pi * n / period
        real, imag = turn(item, math.cos(angle), -math.sin(angle))
        low.append(real)
        high.append(-imag)
    return low + high


def real_inverse(freqs, count):
    if count == 1:
        return [freqs[0][0]]
    if count == 2:
        return [freqs[0][0] + freqs[1][0], freqs[0][0] - freqs[1][0]]
    even = real_inverse({k // 2: v for k, v in freqs.items() if k % 2 == 0}, count // 2)
    odd = odd_inputs(freqs, count)
    return [a + b for a, b in zip(even, odd)] + [a - b for a, b in zip(even, odd)]


def padded_inverse(freqs, count):
    even = real_inverse({k // 2: v for k, v in freqs.items() if k % 2 == 0}, count)
    return [a + b for a, b in zip(even, odd_inputs(freqs, 2 * count))]


def each(count, body):
    step = max(s for s in range(1, 18) if count % s == 0)

    def several(turn_no, carry):
        for k in range(step):
            body(turn_no * step + k)
        return carry

    if step == count:
        several(0, 0)
    else:
        lax.fori_loop(0, count // step, several, 0)


def outer_forward(source, mid, base):
    blocks, group, width = source.shape

    def body(step, carry):
        start = pl.multiple_of(step * ROWS, ROWS)
        rows = pl.ds(start, ROWS)
        found = padded_dft([source[n, rows, :].astype(jnp.float32) for n in range(blocks)])
        out_rows = pl.ds(pl.multiple_of(start + base, ROWS), ROWS)
        for freq, (real, imag) in found.items():
            if imag is None:
                imag = jnp.zeros_like(real)
            mid[freq, out_rows, 0:width] = real.astype(jnp.bfloat16)
            mid[freq, out_rows, width : 2 * width] = imag.astype(jnp.bfloat16)
        return carry

    lax.fori_loop(0, group // ROWS, body, 0)


def outer_inverse(mid, base, dest):
    blocks, group, width = dest.shape

    def body(step, carry):
        start = pl.multiple_of(step * ROWS, ROWS)
        rows = pl.ds(pl.multiple_of(start + base, ROWS), ROWS)
        freqs = {
            k: (mid[k, rows, 0:width], mid[k, rows, width : 2 * width]) for k in range(blocks + 1)
        }
        for n, item in enumerate(padded_inverse(freqs, blocks)):
            dest[n, pl.ds(start, ROWS), :] = item.astype(dest.dtype)
        return carry

    lax.fori_loop(0, group // ROWS, body, 0)


def product(left, right, width, conjugate):
    left_real, left_imag = left[:, :width], left[:, width:]
    right_real, right_imag = right[:, :width], right[:, width:]
    if conjugate:
        left_imag = -left_imag
    real = left_real * right_real - left_imag * right_imag
    imag = left_real * right_imag + left_imag * right_real
    return jnp.concatenate([real.astype(jnp.bfloat16), imag.astype(jnp.bfloat16)], 1)


def place(inner):
    here = lax.axis_index("seq")
    return here // inner, lax.rem(here, inner)


def pack_planes_kernel(inner, outer, source, *refs):
    parts, sems = refs[:outer], refs[outer]
    group = parts[0].shape[2]
    plane, _ = place(inner)
    copies = []
    for far in range(outer - 1, -1, -1):
        for low in range(inner):
            start = pl.multiple_of(((plane ^ far) * inner + low) * group, ROWS)
            rows = source.at[pl.ds(start, group), :]
            copies.append(pltpu.make_async_copy(rows, parts[far].at[0, low], sems.at[far, low]))
            copies[-1].start()
    for copy in copies:
        copy.wait()


def pack_lows_kernel(inner, outer, source, *refs):
    parts, sems = refs[:inner], refs[inner]
    group = parts[0].shape[2]
    _, low = place(inner)
    copies = []
    for mask, part in enumerate(parts):
        for plane in range(outer):
            start = pl.multiple_of((plane * inner + (low ^ mask)) * group, ROWS)
            rows = source.at[pl.ds(start, group), :]
            copies.append(pltpu.make_async_copy(rows, part.at[0, plane], sems.at[mask, plane]))
            copies[-1].start()
    for copy in copies:
        copy.wait()


def gated_kernel(inner, outer, grad_out, gate, forward, inverse, *refs):
    parts, (left, right, sems) = refs[:inner], refs[inner:]
    group = left.shape[2]
    _, low = place(inner)
    copies = []
    for mask in range(inner):
        for plane in range(outer):
            start = pl.multiple_of((plane * inner + (low ^ mask)) * group, ROWS)
            rows = pl.ds(start, group)
            pair = [
                pltpu.make_async_copy(
                    source.at[rows, :], held.at[mask, plane], sems.at[which, mask, plane]
                )
                for which, (source, held) in enumerate(((grad_out, left), (gate, right)))
            ]
            for copy in pair:
                copy.start()
            copies.append(pair)
    for mask, part in enumerate(parts):
        for plane in range(outer):
            for copy in copies[mask * outer + plane]:
                copy.wait()
            part[0, plane] = (
                left[mask, plane].astype(jnp.float32) * right[mask, plane].astype(jnp.float32)
            ).astype(jnp.bfloat16)


def turn_kernel(inner, fars, *refs):
    parts, outs = refs[:inner], refs[inner:]
    plane, low = place(inner)
    for mask, part in enumerate(parts):
        for far, out in zip(fars, outs):
            for which in range(part.shape[0]):
                out[which, low ^ mask] = part[which, plane ^ far]


def turn_back_kernel(inner, outer, *refs):
    parts, outs = refs[:outer], refs[outer:]
    plane, low = place(inner)
    for far, part in enumerate(parts):
        for mask, out in enumerate(outs):
            for which in range(part.shape[0]):
                out[which, plane ^ far] = part[which, low ^ mask]


def hold_kernel(*refs):
    half = len(refs) // 2
    for source, dest in zip(refs[:half], refs[half:]):
        dest[...] = source[...]


def gather_planes(inner, outer, parts, signal):
    plane, _ = place(inner)
    for far, part in enumerate(parts):
        for low in range(inner):
            signal[(plane ^ far) * inner + low] = part[0, low]


def gather_lows(inner, outer, parts, signal):
    _, low = place(inner)
    for mask, part in enumerate(parts):
        for plane in range(outer):
            signal[plane * inner + (low ^ mask)] = part[0, plane]


def scatter(inner, outer, signal, outs):
    _, low = place(inner)
    for mask, out in enumerate(outs):
        for plane in range(outer):
            out[0, plane] = signal[plane * inner + (low ^ mask)]


def taps_kernel(inner, outer, *refs):
    parts, (forward, spec, signal, mid) = refs[:outer], refs[outer:]
    gather_planes(inner, outer, parts, signal)
    outer_forward(signal, mid, 0)

    def body(k):
        spec[k] = jnp.dot(mid[k], forward[k], preferred_element_type=jnp.float32)

    each(mid.shape[0], body)


def conv_kernel(inner, outer, *refs):
    parts, (spec_taps, forward, inverse) = refs[:inner], refs[inner : inner + 3]
    outs, (spec, signal, mid, back) = refs[inner + 3 : -4], refs[-4:]
    width = signal.shape[2]
    gather_lows(inner, outer, parts, signal)
    outer_forward(signal, mid, 0)

    def body(k):
        value = jnp.dot(mid[k], forward[k], preferred_element_type=jnp.float32)
        spec[k] = value
        back[k] = jnp.dot(
            product(spec_taps[k], value, width, False),
            inverse[k],
            preferred_element_type=jnp.float32,
        )

    each(mid.shape[0], body)
    outer_inverse(back, 0, signal)
    plane, _ = place(inner)
    for far, out in enumerate(outs):
        for low in range(inner):
            out[0, low] = signal[(plane ^ far) * inner + low]


def grad_kernel(inner, outer, *refs):
    parts, (spec_taps, forward, inverse) = refs[:outer], refs[outer : outer + 3]
    outs, (spec, signal, mid, back) = refs[outer + 3 : -4], refs[-4:]
    width = signal.shape[2]
    gather_planes(inner, outer, parts, signal)
    outer_forward(signal, mid, 0)

    def body(k):
        gated = jnp.dot(mid[k], forward[k], preferred_element_type=jnp.float32)
        spec[k] = gated
        back[k] = jnp.dot(
            product(spec_taps[k], gated, width, True),
            inverse[k],
            preferred_element_type=jnp.float32,
        )

    each(mid.shape[0], body)
    outer_inverse(back, 0, signal)
    scatter(inner, outer, signal, outs)


def cross_kernel(ndp, factor, spec_value, spec_gated, inverse, *refs):
    sums, (cross, back) = refs[:ndp], refs[ndp:]
    blocks, _, width = cross.shape

    def body(k):
        back[k] = jnp.dot(
            product(spec_value[k], spec_gated[k], width, True),
            inverse[k],
            preferred_element_type=jnp.float32,
        )

    each(back.shape[0], body)
    outer_inverse(back, 0, cross)
    share = blocks // ndp
    for step, total in enumerate(sums):
        first = lax.rem(lax.axis_index("dp") + step, ndp) * share
        for n in range(share):
            total[:, n * width : (n + 1) * width] = (cross[first + n] * factor).astype(total.dtype)


def final_kernel(inner, outer, ndp, *refs):
    grad_parts, conv_parts, refs = refs[:outer], refs[outer : outer + inner], refs[outer + inner :]
    sums, refs = refs[:ndp], refs[ndp:]
    grad_out, grad_gate, grad_value, grad_taps, product_of, total, sems, sum_sem = refs
    group = product_of.shape[2]
    plane, low = place(inner)
    copies = []

    def send(source, dest, sem):
        copies.append(pltpu.make_async_copy(source, dest, sem))
        copies[-1].start()

    def rows_of(there, where):
        return pl.ds(pl.multiple_of((there * inner + where) * group, ROWS), group)

    for far, part in enumerate(grad_parts):
        for where in range(inner):
            rows = rows_of(plane ^ far, where)
            send(part.at[0, where], grad_value.at[rows, :], sems.at[0, far, where])
    total[...] = sums[0][...]
    for other in sums[1:]:
        total[...] += other[...].astype(jnp.float32)
    send(total, grad_taps, sum_sem.at[0])
    for mask, part in enumerate(conv_parts):
        for there in range(outer):
            rows = rows_of(there, low ^ mask)
            product_of[there, mask] = (
                grad_out[rows, :].astype(jnp.float32) * part[0, there].astype(jnp.float32)
            ).astype(jnp.bfloat16)
            send(product_of.at[there, mask], grad_gate.at[rows, :], sems.at[1, there, mask])
    for copy in copies:
        copy.wait()


def vmem(count):
    return [pl.BlockSpec(memory_space=pltpu.VMEM)] * count


def anywhere(count):
    return [pl.BlockSpec(memory_space=pl.ANY)] * count


def call(kernel, outs, scratch, operands, ins=None, dests=None, mib=4, flops=10**9, after=()):
    count = len(operands)

    def ordered(*refs):
        kernel(*refs[len(after) :])

    return pl.pallas_call(
        ordered,
        out_shape=list(outs),
        in_specs=anywhere(len(after)) + (ins or vmem(count)),
        out_specs=dests or vmem(len(outs)),
        scratch_shapes=scratch,
        compiler_params=pltpu.CompilerParams(vmem_limit_bytes=mib * 1024 * 1024),
        cost_estimate=pl.CostEstimate(flops=flops, bytes_accessed=10**6, transcendentals=0),
        name=kernel.func.__name__,
    )(*after, *operands)


def permute(array, axis, target):
    count = lax.axis_size(axis)
    return lax.ppermute(array, axis, [(i, target(i)) for i in range(count)])


def on_device(grad_out, gate, value, filter_taps):
    nseq = lax.axis_size("seq")
    ndp = lax.axis_size("dp")
    chans = grad_out.shape[1]
    width = grad_out.shape[2]
    group = chans // nseq
    blocks = nseq
    inner = 1 << (nseq.bit_length() - 1) // 2
    outer = nseq // inner
    forward, inverse = (jnp.asarray(t) for t in inner_tables(blocks, width))
    factor = 1.0 / (ndp * math.sqrt(nseq * width))
    shape = jax.ShapeDtypeStruct
    bf16, f32 = jnp.bfloat16, jnp.float32

    def by_plane(count=1):
        return [shape((count, inner, group, width), bf16)] * outer

    def by_low(count=1):
        return [shape((count, outer, group, width), bf16)] * inner

    def arrivals(parts, count=outer - 1):
        return [parts[far] for far in range(outer - 1, outer - 1 - count, -1)]

    def in_plane(parts):
        return [
            permute(part, "seq", lambda i: i ^ mask) if mask else part
            for mask, part in enumerate(parts)
        ]

    def over_planes(found):
        return {
            far: permute(part, "seq", lambda i: i ^ (far * inner)) if far else part
            for far, part in found.items()
        }

    def turned(parts, fars, after=()):
        kernel = functools.partial(turn_kernel, inner, fars)
        outs = call(kernel, by_plane()[: len(fars)], [], parts, after=list(after))
        return dict(zip(fars, outs))

    def ordered(found):
        return [found[far] for far in range(outer)]

    everywhere = tuple(range(outer))

    value_packed = call(
        functools.partial(pack_planes_kernel, inner, outer),
        by_plane(),
        [pltpu.SemaphoreType.DMA((outer, inner))],
        [value[0]],
        ins=anywhere(1),
        mib=16,
    )
    taps_packed = call(
        functools.partial(pack_lows_kernel, inner, outer),
        by_low(),
        [pltpu.SemaphoreType.DMA((inner, outer))],
        [filter_taps],
        ins=anywhere(1),
        mib=16,
        after=value_packed[:1],
    )
    value_plane = ordered(over_planes(dict(enumerate(value_packed))))
    taps_low = in_plane(taps_packed)
    gated_packed = call(
        functools.partial(gated_kernel, inner, outer),
        by_low(),
        [pltpu.VMEM((inner, outer, group, width), bf16)] * 2
        + [pltpu.SemaphoreType.DMA((2, inner, outer))],
        [grad_out[0], gate[0], forward, inverse],
        ins=anywhere(2) + vmem(2),
        mib=16,
        after=taps_packed[:1],
    )
    gated_low = in_plane(gated_packed)
    taps_turned = turned(taps_low, everywhere, arrivals(value_plane, outer // 4) + list(gated_packed[:1]))
    taps_plane = ordered(over_planes(taps_turned))
    value_low = in_plane(
        call(
            functools.partial(turn_back_kernel, inner, outer),
            by_low(),
            [],
            value_plane,
            after=[taps_turned[0]] + arrivals(value_plane),
        )
    )

    spec = shape((blocks + 1, group, 2 * width), f32)
    signal = pltpu.VMEM((blocks, group, width), bf16)
    mid = pltpu.VMEM((blocks + 1, group, 2 * width), bf16)
    back = pltpu.VMEM((blocks + 1, group, 2 * width), f32)
    gated_turned = turned(gated_low, everywhere, arrivals(taps_plane, outer // 4))
    gated_plane = ordered(over_planes(gated_turned))
    spec_taps = call(
        functools.partial(taps_kernel, inner, outer),
        [spec],
        [signal, mid],
        taps_plane + [forward],
        mib=16,
        after=[gated_turned[0]] + arrivals(taps_plane),
    )[0]
    outs = call(
        functools.partial(conv_kernel, inner, outer),
        by_plane() + [spec],
        [signal, mid, back],
        value_low + [spec_taps, forward, inverse],
        mib=16,
    )
    held = call(
        functools.partial(hold_kernel), by_plane(), [], outs[:outer], after=arrivals(gated_plane, outer // 2)
    )
    conv_plane = ordered(over_planes(dict(enumerate(held))))
    spec_value = outs[outer]
    wide = (group, blocks // ndp * width)
    outs = call(
        functools.partial(grad_kernel, inner, outer),
        by_low() + [spec],
        [signal, mid, back],
        gated_plane + [spec_taps, forward, inverse],
        mib=16,
        after=[held[0]] + arrivals(gated_plane),
    )
    grad_low, spec_gated = in_plane(outs[:inner]), outs[inner]
    sums = list(
        call(
            functools.partial(cross_kernel, ndp, factor),
            [shape(wide, f32)] + [shape(wide, bf16)] * (ndp - 1),
            [pltpu.VMEM((blocks, group, width), f32), back],
            [spec_value, spec_gated, inverse],
            mib=16,
        )
    )
    mine = sums[0]
    for step in range(1, ndp):
        sums[step] = permute(sums[step], "dp", lambda i: (i + step) % ndp)
    grad_turned = turned(grad_low, everywhere, arrivals(conv_plane, outer // 2) + [mine])
    grad_plane = ordered(over_planes(grad_turned))
    conv_low = in_plane(
        call(
            functools.partial(turn_back_kernel, inner, outer),
            by_low(),
            [],
            conv_plane,
            after=[grad_turned[0]] + sums[1:],
        )
    )
    grad_gate, grad_value, grad_taps = call(
        functools.partial(final_kernel, inner, outer, ndp),
        [shape((chans, width), bf16)] * 2 + [shape(wide, f32)],
        [
            pltpu.VMEM((outer, inner, group, width), bf16),
            pltpu.VMEM(wide, f32),
            pltpu.SemaphoreType.DMA((2, outer, inner)),
            pltpu.SemaphoreType.DMA((1,)),
        ],
        grad_plane + conv_low + sums + [grad_out[0]],
        dests=anywhere(3),
        mib=8,
        after=arrivals(grad_plane),
    )
    return (grad_gate[None], grad_value[None], grad_taps)


def solution(mesh):
    return jax.shard_map(
        on_device,
        mesh=mesh,
        in_specs=(P("dp", None, "seq"), P("dp", None, "seq"), P("dp", None, "seq"), P(None, "seq")),
        out_specs=(P("dp", None, "seq"), P("dp", None, "seq"), P("seq", "dp")),
        check_vma=False,
    )
```

```python
import functools
import math

import jax
import jax.numpy as jnp
import numpy as np
from jax import lax
from jax.experimental import pallas as pl
from jax.experimental.pallas import tpu as pltpu
from jax.sharding import PartitionSpec as P

ROWS = 16


def inner_tables(blocks, width):
    total = 2 * blocks * width
    pos = np.arange(width)
    tables = []
    for outer in range(blocks + 1):
        turns = pos[:, None] * (outer + 2 * blocks * pos[None, :]) % total
        angle = 2.0 * np.pi / total * turns
        cos, sin = np.cos(angle), np.sin(angle)
        tables.append(np.block([[cos, -sin], [sin, cos]]))
    table = np.stack(tables)
    weight = np.full((blocks + 1, 1, 1), 2.0 / total)
    weight[0] = weight[blocks] = 1.0 / total
    return (
        table.astype(jnp.bfloat16),
        (table.transpose(0, 2, 1) * weight).astype(jnp.bfloat16),
    )


def turn(number, cos, sin):
    real, imag = number
    if abs(sin) < 1e-9:
        return (real, imag) if cos > 0 else (-real, -imag)
    if abs(cos) < 1e-9:
        return (imag, -real) if sin > 0 else (-imag, real)
    return (real * cos + imag * sin, imag * cos - real * sin)


def add(left, right):
    return (left[0] + right[0], left[1] + right[1])


def sub(left, right):
    return (left[0] - right[0], left[1] - right[1])


def complex_dft(items, sign):
    count = len(items)
    if count == 1:
        return items
    half = count // 2
    low, high = items[:half], items[half:]
    even = complex_dft([add(a, b) for a, b in zip(low, high)], sign)
    odd = []
    for n, (a, b) in enumerate(zip(low, high)):
        angle = 2.0 * math.pi * n / count
        odd.append(turn(sub(a, b), math.cos(angle), sign * math.sin(angle)))
    odd = complex_dft(odd, sign)
    return [item for pair in zip(even, odd) for item in pair]


def odd_outputs(items, period):
    quarter = len(items) // 2
    turned = []
    for n in range(quarter):
        angle = 2.0 * math.pi * n / period
        turned.append(turn((items[n], -items[n + quarter]), math.cos(angle), math.sin(angle)))
    found = {}
    for m, (real, imag) in enumerate(complex_dft(turned, 1)):
        freq = 4 * m + 1
        if freq > period // 2:
            freq, imag = period - freq, -imag
        found[freq] = (real, imag)
    return found


def real_dft(items):
    count = len(items)
    if count == 1:
        return {0: (items[0], None)}
    if count == 2:
        return {0: (items[0] + items[1], None), 1: (items[0] - items[1], None)}
    half = count // 2
    low, high = items[:half], items[half:]
    found = {2 * k: v for k, v in real_dft([a + b for a, b in zip(low, high)]).items()}
    found.update(odd_outputs([a - b for a, b in zip(low, high)], count))
    return found


def padded_dft(items):
    found = {2 * k: v for k, v in real_dft(items).items()}
    found.update(odd_outputs(items, 2 * len(items)))
    return found


def odd_inputs(freqs, period):
    quarter = period // 4
    items = []
    for m in range(quarter):
        freq = 4 * m + 1
        if freq > period // 2:
            real, imag = freqs[period - freq]
            items.append((real, -imag))
        else:
            items.append(freqs[freq])
    low, high = [], []
    for n, item in enumerate(complex_dft(items, -1)):
        angle = 2.0 * math.pi * n / period
        real, imag = turn(item, math.cos(angle), -math.sin(angle))
        low.append(real)
        high.append(-imag)
    return low + high


def real_inverse(freqs, count):
    if count == 1:
        return [freqs[0][0]]
    if count == 2:
        return [freqs[0][0] + freqs[1][0], freqs[0][0] - freqs[1][0]]
    even = real_inverse({k // 2: v for k, v in freqs.items() if k % 2 == 0}, count // 2)
    odd = odd_inputs(freqs, count)
    return [a + b for a, b in zip(even, odd)] + [a - b for a, b in zip(even, odd)]


def padded_inverse(freqs, count):
    even = real_inverse({k // 2: v for k, v in freqs.items() if k % 2 == 0}, count)
    return [a + b for a, b in zip(even, odd_inputs(freqs, 2 * count))]


def each(count, body):
    step = max(s for s in range(1, 18) if count % s == 0)

    def several(turn_no, carry):
        for k in range(step):
            body(turn_no * step + k)
        return carry

    if step == count:
        several(0, 0)
    else:
        lax.fori_loop(0, count // step, several, 0)


def outer_forward(source, mid, base):
    blocks, group, width = source.shape

    def body(step, carry):
        start = pl.multiple_of(step * ROWS, ROWS)
        rows = pl.ds(start, ROWS)
        found = padded_dft([source[n, rows, :].astype(jnp.float32) for n in range(blocks)])
        out_rows = pl.ds(pl.multiple_of(start + base, ROWS), ROWS)
        for freq, (real, imag) in found.items():
            if imag is None:
                imag = jnp.zeros_like(real)
            mid[freq, out_rows, 0:width] = real.astype(jnp.bfloat16)
            mid[freq, out_rows, width : 2 * width] = imag.astype(jnp.bfloat16)
        return carry

    lax.fori_loop(0, group // ROWS, body, 0)


def outer_inverse(mid, base, dest):
    blocks, group, width = dest.shape

    def body(step, carry):
        start = pl.multiple_of(step * ROWS, ROWS)
        rows = pl.ds(pl.multiple_of(start + base, ROWS), ROWS)
        freqs = {
            k: (mid[k, rows, 0:width], mid[k, rows, width : 2 * width]) for k in range(blocks + 1)
        }
        for n, item in enumerate(padded_inverse(freqs, blocks)):
            dest[n, pl.ds(start, ROWS), :] = item.astype(dest.dtype)
        return carry

    lax.fori_loop(0, group // ROWS, body, 0)


def product(left, right, width, conjugate):
    left_real, left_imag = left[:, :width], left[:, width:]
    right_real, right_imag = right[:, :width], right[:, width:]
    if conjugate:
        left_imag = -left_imag
    real = left_real * right_real - left_imag * right_imag
    imag = left_real * right_imag + left_imag * right_real
    return jnp.concatenate([real.astype(jnp.bfloat16), imag.astype(jnp.bfloat16)], 1)


def place(inner):
    here = lax.axis_index("seq")
    return here // inner, lax.rem(here, inner)


def pack_planes_kernel(inner, outer, source, *refs):
    parts, sems = refs[:outer], refs[outer]
    group = parts[0].shape[2]
    plane, _ = place(inner)
    copies = []
    for far in range(outer - 1, -1, -1):
        for low in range(inner):
            start = pl.multiple_of(((plane ^ far) * inner + low) * group, ROWS)
            rows = source.at[pl.ds(start, group), :]
            copies.append(pltpu.make_async_copy(rows, parts[far].at[0, low], sems.at[far, low]))
            copies[-1].start()
    for copy in copies:
        copy.wait()


def pack_lows_kernel(inner, outer, source, *refs):
    parts, sems = refs[:inner], refs[inner]
    group = parts[0].shape[2]
    _, low = place(inner)
    copies = []
    for mask, part in enumerate(parts):
        for plane in range(outer):
            start = pl.multiple_of((plane * inner + (low ^ mask)) * group, ROWS)
            rows = source.at[pl.ds(start, group), :]
            copies.append(pltpu.make_async_copy(rows, part.at[0, plane], sems.at[mask, plane]))
            copies[-1].start()
    for copy in copies:
        copy.wait()


def gated_kernel(inner, outer, grad_out, gate, forward, inverse, *refs):
    parts, (left, right, sems) = refs[:inner], refs[inner:]
    group = left.shape[2]
    _, low = place(inner)
    copies = []
    for mask in range(inner):
        for plane in range(outer):
            start = pl.multiple_of((plane * inner + (low ^ mask)) * group, ROWS)
            rows = pl.ds(start, group)
            pair = [
                pltpu.make_async_copy(
                    source.at[rows, :], held.at[mask, plane], sems.at[which, mask, plane]
                )
                for which, (source, held) in enumerate(((grad_out, left), (gate, right)))
            ]
            for copy in pair:
                copy.start()
            copies.append(pair)
    for mask, part in enumerate(parts):
        for plane in range(outer):
            for copy in copies[mask * outer + plane]:
                copy.wait()
            part[0, plane] = (
                left[mask, plane].astype(jnp.float32) * right[mask, plane].astype(jnp.float32)
            ).astype(jnp.bfloat16)


def turn_kernel(inner, fars, *refs):
    parts, outs = refs[:inner], refs[inner:]
    plane, low = place(inner)
    for mask, part in enumerate(parts):
        for far, out in zip(fars, outs):
            for which in range(part.shape[0]):
                out[which, low ^ mask] = part[which, plane ^ far]


def turn_back_kernel(inner, outer, *refs):
    parts, outs = refs[:outer], refs[outer:]
    plane, low = place(inner)
    for far, part in enumerate(parts):
        for mask, out in enumerate(outs):
            for which in range(part.shape[0]):
                out[which, plane ^ far] = part[which, low ^ mask]


def hold_kernel(*refs):
    half = len(refs) // 2
    for source, dest in zip(refs[:half], refs[half:]):
        dest[...] = source[...]


def gather_planes(inner, outer, parts, signal):
    plane, _ = place(inner)
    for far, part in enumerate(parts):
        for low in range(inner):
            signal[(plane ^ far) * inner + low] = part[0, low]


def gather_lows(inner, outer, parts, signal):
    _, low = place(inner)
    for mask, part in enumerate(parts):
        for plane in range(outer):
            signal[plane * inner + (low ^ mask)] = part[0, plane]


def scatter(inner, outer, signal, outs):
    _, low = place(inner)
    for mask, out in enumerate(outs):
        for plane in range(outer):
            out[0, plane] = signal[plane * inner + (low ^ mask)]


def taps_kernel(inner, outer, *refs):
    parts, (forward, spec, signal, mid) = refs[:outer], refs[outer:]
    gather_planes(inner, outer, parts, signal)
    outer_forward(signal, mid, 0)

    def body(k):
        spec[k] = jnp.dot(mid[k], forward[k], preferred_element_type=jnp.float32)

    each(mid.shape[0], body)


def conv_kernel(inner, outer, *refs):
    parts, (spec_taps, forward, inverse) = refs[:inner], refs[inner : inner + 3]
    outs, (spec, signal, mid, back) = refs[inner + 3 : -4], refs[-4:]
    width = signal.shape[2]
    gather_lows(inner, outer, parts, signal)
    outer_forward(signal, mid, 0)

    def body(k):
        value = jnp.dot(mid[k], forward[k], preferred_element_type=jnp.float32)
        spec[k] = value
        back[k] = jnp.dot(
            product(spec_taps[k], value, width, False),
            inverse[k],
            preferred_element_type=jnp.float32,
        )

    each(mid.shape[0], body)
    outer_inverse(back, 0, signal)
    plane, _ = place(inner)
    for far, out in enumerate(outs):
        for low in range(inner):
            out[0, low] = signal[(plane ^ far) * inner + low]


def grad_kernel(inner, outer, *refs):
    parts, (spec_taps, forward, inverse) = refs[:outer], refs[outer : outer + 3]
    outs, (spec, signal, mid, back) = refs[outer + 3 : -4], refs[-4:]
    width = signal.shape[2]
    gather_planes(inner, outer, parts, signal)
    outer_forward(signal, mid, 0)

    def body(k):
        gated = jnp.dot(mid[k], forward[k], preferred_element_type=jnp.float32)
        spec[k] = gated
        back[k] = jnp.dot(
            product(spec_taps[k], gated, width, True),
            inverse[k],
            preferred_element_type=jnp.float32,
        )

    each(mid.shape[0], body)
    outer_inverse(back, 0, signal)
    scatter(inner, outer, signal, outs)


def cross_kernel(ndp, factor, spec_value, spec_gated, inverse, *refs):
    sums, (cross, back) = refs[:ndp], refs[ndp:]
    blocks, _, width = cross.shape

    def body(k):
        back[k] = jnp.dot(
            product(spec_value[k], spec_gated[k], width, True),
            inverse[k],
            preferred_element_type=jnp.float32,
        )

    each(back.shape[0], body)
    outer_inverse(back, 0, cross)
    share = blocks // ndp
    for step, total in enumerate(sums):
        first = lax.rem(lax.axis_index("dp") + step, ndp) * share
        for n in range(share):
            total[:, n * width : (n + 1) * width] = (cross[first + n] * factor).astype(total.dtype)


def final_kernel(inner, outer, ndp, *refs):
    grad_parts, conv_parts, refs = refs[:outer], refs[outer : outer + inner], refs[outer + inner :]
    sums, refs = refs[:ndp], refs[ndp:]
    grad_out, grad_gate, grad_value, grad_taps, product_of, total, sems, sum_sem = refs
    group = product_of.shape[2]
    plane, low = place(inner)
    copies = []

    def send(source, dest, sem):
        copies.append(pltpu.make_async_copy(source, dest, sem))
        copies[-1].start()

    def rows_of(there, where):
        return pl.ds(pl.multiple_of((there * inner + where) * group, ROWS), group)

    for far, part in enumerate(grad_parts):
        for where in range(inner):
            rows = rows_of(plane ^ far, where)
            send(part.at[0, where], grad_value.at[rows, :], sems.at[0, far, where])
    total[...] = sums[0][...]
    for other in sums[1:]:
        total[...] += other[...].astype(jnp.float32)
    send(total, grad_taps, sum_sem.at[0])
    for mask, part in enumerate(conv_parts):
        for there in range(outer):
            rows = rows_of(there, low ^ mask)
            product_of[there, mask] = (
                grad_out[rows, :].astype(jnp.float32) * part[0, there].astype(jnp.float32)
            ).astype(jnp.bfloat16)
            send(product_of.at[there, mask], grad_gate.at[rows, :], sems.at[1, there, mask])
    for copy in copies:
        copy.wait()


def vmem(count):
    return [pl.BlockSpec(memory_space=pltpu.VMEM)] * count


def anywhere(count):
    return [pl.BlockSpec(memory_space=pl.ANY)] * count


def call(kernel, outs, scratch, operands, ins=None, dests=None, mib=4, flops=10**9, after=()):
    count = len(operands)

    def ordered(*refs):
        kernel(*refs[len(after) :])

    return pl.pallas_call(
        ordered,
        out_shape=list(outs),
        in_specs=anywhere(len(after)) + (ins or vmem(count)),
        out_specs=dests or vmem(len(outs)),
        scratch_shapes=scratch,
        compiler_params=pltpu.CompilerParams(vmem_limit_bytes=mib * 1024 * 1024),
        cost_estimate=pl.CostEstimate(flops=flops, bytes_accessed=10**6, transcendentals=0),
        name=kernel.func.__name__,
    )(*after, *operands)


def permute(array, axis, target):
    count = lax.axis_size(axis)
    return lax.ppermute(array, axis, [(i, target(i)) for i in range(count)])


def on_device(grad_out, gate, value, filter_taps):
    nseq = lax.axis_size("seq")
    ndp = lax.axis_size("dp")
    chans = grad_out.shape[1]
    width = grad_out.shape[2]
    group = chans // nseq
    blocks = nseq
    inner = 1 << (nseq.bit_length() - 1) // 2
    outer = nseq // inner
    forward, inverse = (jnp.asarray(t) for t in inner_tables(blocks, width))
    factor = 1.0 / (ndp * math.sqrt(nseq * width))
    shape = jax.ShapeDtypeStruct
    bf16, f32 = jnp.bfloat16, jnp.float32

    def by_plane(count=1):
        return [shape((count, inner, group, width), bf16)] * outer

    def by_low(count=1):
        return [shape((count, outer, group, width), bf16)] * inner

    def arrivals(parts, count=outer - 1):
        return [parts[far] for far in range(outer - 1, outer - 1 - count, -1)]

    def in_plane(parts):
        return [
            permute(part, "seq", lambda i: i ^ mask) if mask else part
            for mask, part in enumerate(parts)
        ]

    def over_planes(found):
        return {
            far: permute(part, "seq", lambda i: i ^ (far * inner)) if far else part
            for far, part in found.items()
        }

    def turned(parts, fars, after=()):
        kernel = functools.partial(turn_kernel, inner, fars)
        outs = call(kernel, by_plane()[: len(fars)], [], parts, after=list(after))
        return dict(zip(fars, outs))

    def ordered(found):
        return [found[far] for far in range(outer)]

    everywhere = tuple(range(outer))

    value_packed = call(
        functools.partial(pack_planes_kernel, inner, outer),
        by_plane(),
        [pltpu.SemaphoreType.DMA((outer, inner))],
        [value[0]],
        ins=anywhere(1),
        mib=16,
    )
    taps_packed = call(
        functools.partial(pack_lows_kernel, inner, outer),
        by_low(),
        [pltpu.SemaphoreType.DMA((inner, outer))],
        [filter_taps],
        ins=anywhere(1),
        mib=16,
        after=value_packed[:1],
    )
    value_plane = ordered(over_planes(dict(enumerate(value_packed))))
    taps_low = in_plane(taps_packed)
    gated_packed = call(
        functools.partial(gated_kernel, inner, outer),
        by_low(),
        [pltpu.VMEM((inner, outer, group, width), bf16)] * 2
        + [pltpu.SemaphoreType.DMA((2, inner, outer))],
        [grad_out[0], gate[0], forward, inverse],
        ins=anywhere(2) + vmem(2),
        mib=16,
        after=taps_packed[:1],
    )
    gated_low = in_plane(gated_packed)
    taps_turned = turned(taps_low, everywhere, arrivals(value_plane, outer // 4) + list(gated_packed[:1]))
    taps_plane = ordered(over_planes(taps_turned))
    value_low = in_plane(
        call(
            functools.partial(turn_back_kernel, inner, outer),
            by_low(),
            [],
            value_plane,
            after=[taps_turned[0]] + arrivals(value_plane),
        )
    )

    spec = shape((blocks + 1, group, 2 * width), f32)
    signal = pltpu.VMEM((blocks, group, width), bf16)
    mid = pltpu.VMEM((blocks + 1, group, 2 * width), bf16)
    back = pltpu.VMEM((blocks + 1, group, 2 * width), f32)
    gated_turned = turned(gated_low, everywhere, arrivals(taps_plane, outer // 4))
    gated_plane = ordered(over_planes(gated_turned))
    spec_taps = call(
        functools.partial(taps_kernel, inner, outer),
        [spec],
        [signal, mid],
        taps_plane + [forward],
        mib=16,
        after=[gated_turned[0]] + arrivals(taps_plane),
    )[0]
    outs = call(
        functools.partial(conv_kernel, inner, outer),
        by_plane() + [spec],
        [signal, mid, back],
        value_low + [spec_taps, forward, inverse],
        mib=16,
    )
    held = call(
        functools.partial(hold_kernel), by_plane(), [], outs[:outer], after=arrivals(gated_plane, outer // 2)
    )
    conv_plane = ordered(over_planes(dict(enumerate(held))))
    spec_value = outs[outer]
    wide = (group, blocks // ndp * width)
    outs = call(
        functools.partial(grad_kernel, inner, outer),
        by_low() + [spec],
        [signal, mid, back],
        gated_plane + [spec_taps, forward, inverse],
        mib=16,
        after=[held[0]] + arrivals(gated_plane),
    )
    grad_low, spec_gated = in_plane(outs[:inner]), outs[inner]
    sums = list(
        call(
            functools.partial(cross_kernel, ndp, factor),
            [shape(wide, f32)] + [shape(wide, bf16)] * (ndp - 1),
            [pltpu.VMEM((blocks, group, width), f32), back],
            [spec_value, spec_gated, inverse],
            mib=16,
        )
    )
    mine = sums[0]
    for step in range(1, ndp):
        sums[step] = permute(sums[step], "dp", lambda i: (i + step) % ndp)
    grad_turned = turned(grad_low, everywhere, arrivals(conv_plane, outer // 2) + [mine])
    grad_plane = ordered(over_planes(grad_turned))
    conv_low = in_plane(
        call(
            functools.partial(turn_back_kernel, inner, outer),
            by_low(),
            [],
            conv_plane,
            after=[grad_turned[0]],
        )
    )
    grad_gate, grad_value, grad_taps = call(
        functools.partial(final_kernel, inner, outer, ndp),
        [shape((chans, width), bf16)] * 2 + [shape(wide, f32)],
        [
            pltpu.VMEM((outer, inner, group, width), bf16),
            pltpu.VMEM(wide, f32),
            pltpu.SemaphoreType.DMA((2, outer, inner)),
            pltpu.SemaphoreType.DMA((1,)),
        ],
        grad_plane + conv_low + sums + [grad_out[0]],
        dests=anywhere(3),
        mib=8,
        after=arrivals(grad_plane),
    )
    return (grad_gate[None], grad_value[None], grad_taps)


def solution(mesh):
    return jax.shard_map(
        on_device,
        mesh=mesh,
        in_specs=(P("dp", None, "seq"), P("dp", None, "seq"), P("dp", None, "seq"), P(None, "seq")),
        out_specs=(P("dp", None, "seq"), P("dp", None, "seq"), P("seq", "dp")),
        check_vma=False,
    )
```

```python
import functools
import math

import jax
import jax.numpy as jnp
import numpy as np
from jax import lax
from jax.experimental import pallas as pl
from jax.experimental.pallas import tpu as pltpu
from jax.sharding import PartitionSpec as P

ROWS = 16


def inner_tables(blocks, width):
    total = 2 * blocks * width
    pos = np.arange(width)
    tables = []
    for outer in range(blocks + 1):
        turns = pos[:, None] * (outer + 2 * blocks * pos[None, :]) % total
        angle = 2.0 * np.pi / total * turns
        cos, sin = np.cos(angle), np.sin(angle)
        tables.append(np.block([[cos, -sin], [sin, cos]]))
    table = np.stack(tables)
    weight = np.full((blocks + 1, 1, 1), 2.0 / total)
    weight[0] = weight[blocks] = 1.0 / total
    return (
        table.astype(jnp.bfloat16),
        (table.transpose(0, 2, 1) * weight).astype(jnp.bfloat16),
    )


def turn(number, cos, sin):
    real, imag = number
    if abs(sin) < 1e-9:
        return (real, imag) if cos > 0 else (-real, -imag)
    if abs(cos) < 1e-9:
        return (imag, -real) if sin > 0 else (-imag, real)
    return (real * cos + imag * sin, imag * cos - real * sin)


def add(left, right):
    return (left[0] + right[0], left[1] + right[1])


def sub(left, right):
    return (left[0] - right[0], left[1] - right[1])


def complex_dft(items, sign):
    count = len(items)
    if count == 1:
        return items
    half = count // 2
    low, high = items[:half], items[half:]
    even = complex_dft([add(a, b) for a, b in zip(low, high)], sign)
    odd = []
    for n, (a, b) in enumerate(zip(low, high)):
        angle = 2.0 * math.pi * n / count
        odd.append(turn(sub(a, b), math.cos(angle), sign * math.sin(angle)))
    odd = complex_dft(odd, sign)
    return [item for pair in zip(even, odd) for item in pair]


def odd_outputs(items, period):
    quarter = len(items) // 2
    turned = []
    for n in range(quarter):
        angle = 2.0 * math.pi * n / period
        turned.append(turn((items[n], -items[n + quarter]), math.cos(angle), math.sin(angle)))
    found = {}
    for m, (real, imag) in enumerate(complex_dft(turned, 1)):
        freq = 4 * m + 1
        if freq > period // 2:
            freq, imag = period - freq, -imag
        found[freq] = (real, imag)
    return found


def real_dft(items):
    count = len(items)
    if count == 1:
        return {0: (items[0], None)}
    if count == 2:
        return {0: (items[0] + items[1], None), 1: (items[0] - items[1], None)}
    half = count // 2
    low, high = items[:half], items[half:]
    found = {2 * k: v for k, v in real_dft([a + b for a, b in zip(low, high)]).items()}
    found.update(odd_outputs([a - b for a, b in zip(low, high)], count))
    return found


def padded_dft(items):
    found = {2 * k: v for k, v in real_dft(items).items()}
    found.update(odd_outputs(items, 2 * len(items)))
    return found


def odd_inputs(freqs, period):
    quarter = period // 4
    items = []
    for m in range(quarter):
        freq = 4 * m + 1
        if freq > period // 2:
            real, imag = freqs[period - freq]
            items.append((real, -imag))
        else:
            items.append(freqs[freq])
    low, high = [], []
    for n, item in enumerate(complex_dft(items, -1)):
        angle = 2.0 * math.pi * n / period
        real, imag = turn(item, math.cos(angle), -math.sin(angle))
        low.append(real)
        high.append(-imag)
    return low + high


def real_inverse(freqs, count):
    if count == 1:
        return [freqs[0][0]]
    if count == 2:
        return [freqs[0][0] + freqs[1][0], freqs[0][0] - freqs[1][0]]
    even = real_inverse({k // 2: v for k, v in freqs.items() if k % 2 == 0}, count // 2)
    odd = odd_inputs(freqs, count)
    return [a + b for a, b in zip(even, odd)] + [a - b for a, b in zip(even, odd)]


def padded_inverse(freqs, count):
    even = real_inverse({k // 2: v for k, v in freqs.items() if k % 2 == 0}, count)
    return [a + b for a, b in zip(even, odd_inputs(freqs, 2 * count))]


def each(count, body):
    step = max(s for s in range(1, 18) if count % s == 0)

    def several(turn_no, carry):
        for k in range(step):
            body(turn_no * step + k)
        return carry

    if step == count:
        several(0, 0)
    else:
        lax.fori_loop(0, count // step, several, 0)


def outer_forward(source, mid, base):
    blocks, group, width = source.shape

    def body(step, carry):
        start = pl.multiple_of(step * ROWS, ROWS)
        rows = pl.ds(start, ROWS)
        found = padded_dft([source[n, rows, :].astype(jnp.float32) for n in range(blocks)])
        out_rows = pl.ds(pl.multiple_of(start + base, ROWS), ROWS)
        for freq, (real, imag) in found.items():
            if imag is None:
                imag = jnp.zeros_like(real)
            mid[freq, out_rows, 0:width] = real.astype(jnp.bfloat16)
            mid[freq, out_rows, width : 2 * width] = imag.astype(jnp.bfloat16)
        return carry

    lax.fori_loop(0, group // ROWS, body, 0)


def outer_inverse(mid, base, dest):
    blocks, group, width = dest.shape

    def body(step, carry):
        start = pl.multiple_of(step * ROWS, ROWS)
        rows = pl.ds(pl.multiple_of(start + base, ROWS), ROWS)
        freqs = {
            k: (mid[k, rows, 0:width], mid[k, rows, width : 2 * width]) for k in range(blocks + 1)
        }
        for n, item in enumerate(padded_inverse(freqs, blocks)):
            dest[n, pl.ds(start, ROWS), :] = item.astype(dest.dtype)
        return carry

    lax.fori_loop(0, group // ROWS, body, 0)


def product(left, right, width, conjugate):
    left_real, left_imag = left[:, :width], left[:, width:]
    right_real, right_imag = right[:, :width], right[:, width:]
    if conjugate:
        left_imag = -left_imag
    real = left_real * right_real - left_imag * right_imag
    imag = left_real * right_imag + left_imag * right_real
    return jnp.concatenate([real.astype(jnp.bfloat16), imag.astype(jnp.bfloat16)], 1)


def place(inner):
    here = lax.axis_index("seq")
    return here // inner, lax.rem(here, inner)


def pack_planes_kernel(inner, outer, source, *refs):
    parts, sems = refs[:outer], refs[outer]
    group = parts[0].shape[2]
    plane, _ = place(inner)
    copies = []
    for far in range(outer - 1, -1, -1):
        for low in range(inner):
            start = pl.multiple_of(((plane ^ far) * inner + low) * group, ROWS)
            rows = source.at[pl.ds(start, group), :]
            copies.append(pltpu.make_async_copy(rows, parts[far].at[0, low], sems.at[far, low]))
            copies[-1].start()
    for copy in copies:
        copy.wait()


def pack_lows_kernel(inner, outer, source, *refs):
    parts, sems = refs[:inner], refs[inner]
    group = parts[0].shape[2]
    _, low = place(inner)
    copies = []
    for mask, part in enumerate(parts):
        for plane in range(outer):
            start = pl.multiple_of((plane * inner + (low ^ mask)) * group, ROWS)
            rows = source.at[pl.ds(start, group), :]
            copies.append(pltpu.make_async_copy(rows, part.at[0, plane], sems.at[mask, plane]))
            copies[-1].start()
    for copy in copies:
        copy.wait()


def gated_kernel(inner, outer, grad_out, gate, forward, inverse, *refs):
    parts, (left, right, sems) = refs[:inner], refs[inner:]
    group = left.shape[2]
    _, low = place(inner)
    copies = []
    for mask in range(inner):
        for plane in range(outer):
            start = pl.multiple_of((plane * inner + (low ^ mask)) * group, ROWS)
            rows = pl.ds(start, group)
            pair = [
                pltpu.make_async_copy(
                    source.at[rows, :], held.at[mask, plane], sems.at[which, mask, plane]
                )
                for which, (source, held) in enumerate(((grad_out, left), (gate, right)))
            ]
            for copy in pair:
                copy.start()
            copies.append(pair)
    for mask, part in enumerate(parts):
        for plane in range(outer):
            for copy in copies[mask * outer + plane]:
                copy.wait()
            part[0, plane] = (
                left[mask, plane].astype(jnp.float32) * right[mask, plane].astype(jnp.float32)
            ).astype(jnp.bfloat16)


def turn_kernel(inner, fars, *refs):
    parts, outs = refs[:inner], refs[inner:]
    plane, low = place(inner)
    for mask, part in enumerate(parts):
        for far, out in zip(fars, outs):
            for which in range(part.shape[0]):
                out[which, low ^ mask] = part[which, plane ^ far]


def turn_back_kernel(inner, outer, *refs):
    parts, outs = refs[:outer], refs[outer:]
    plane, low = place(inner)
    for far, part in enumerate(parts):
        for mask, out in enumerate(outs):
            for which in range(part.shape[0]):
                out[which, plane ^ far] = part[which, low ^ mask]


def hold_kernel(*refs):
    half = len(refs) // 2
    for source, dest in zip(refs[:half], refs[half:]):
        dest[...] = source[...]


def gather_planes(inner, outer, parts, signal):
    plane, _ = place(inner)
    for far, part in enumerate(parts):
        for low in range(inner):
            signal[(plane ^ far) * inner + low] = part[0, low]


def gather_lows(inner, outer, parts, signal):
    _, low = place(inner)
    for mask, part in enumerate(parts):
        for plane in range(outer):
            signal[plane * inner + (low ^ mask)] = part[0, plane]


def scatter(inner, outer, signal, outs):
    _, low = place(inner)
    for mask, out in enumerate(outs):
        for plane in range(outer):
            out[0, plane] = signal[plane * inner + (low ^ mask)]


def taps_kernel(inner, outer, *refs):
    parts, (forward, spec, signal, mid) = refs[:outer], refs[outer:]
    gather_planes(inner, outer, parts, signal)
    outer_forward(signal, mid, 0)

    def body(k):
        spec[k] = jnp.dot(mid[k], forward[k], preferred_element_type=jnp.float32)

    each(mid.shape[0], body)


def conv_kernel(inner, outer, *refs):
    parts, (spec_taps, forward, inverse) = refs[:inner], refs[inner : inner + 3]
    outs, (spec, signal, mid, back) = refs[inner + 3 : -4], refs[-4:]
    width = signal.shape[2]
    gather_lows(inner, outer, parts, signal)
    outer_forward(signal, mid, 0)

    def body(k):
        value = jnp.dot(mid[k], forward[k], preferred_element_type=jnp.float32)
        spec[k] = value
        back[k] = jnp.dot(
            product(spec_taps[k], value, width, False),
            inverse[k],
            preferred_element_type=jnp.float32,
        )

    each(mid.shape[0], body)
    outer_inverse(back, 0, signal)
    plane, _ = place(inner)
    for far, out in enumerate(outs):
        for low in range(inner):
            out[0, low] = signal[(plane ^ far) * inner + low]


def grad_kernel(inner, outer, *refs):
    parts, (spec_taps, forward, inverse) = refs[:outer], refs[outer : outer + 3]
    outs, (spec, signal, mid, back) = refs[outer + 3 : -4], refs[-4:]
    width = signal.shape[2]
    gather_planes(inner, outer, parts, signal)
    outer_forward(signal, mid, 0)

    def body(k):
        gated = jnp.dot(mid[k], forward[k], preferred_element_type=jnp.float32)
        spec[k] = gated
        back[k] = jnp.dot(
            product(spec_taps[k], gated, width, True),
            inverse[k],
            preferred_element_type=jnp.float32,
        )

    each(mid.shape[0], body)
    outer_inverse(back, 0, signal)
    scatter(inner, outer, signal, outs)


def cross_kernel(ndp, factor, spec_value, spec_gated, inverse, *refs):
    sums, (cross, back) = refs[:ndp], refs[ndp:]
    blocks, _, width = cross.shape

    def body(k):
        back[k] = jnp.dot(
            product(spec_value[k], spec_gated[k], width, True),
            inverse[k],
            preferred_element_type=jnp.float32,
        )

    each(back.shape[0], body)
    outer_inverse(back, 0, cross)
    share = blocks // ndp
    for step, total in enumerate(sums):
        first = lax.rem(lax.axis_index("dp") + step, ndp) * share
        for n in range(share):
            total[:, n * width : (n + 1) * width] = (cross[first + n] * factor).astype(total.dtype)


def final_kernel(inner, outer, ndp, *refs):
    grad_parts, conv_parts, refs = refs[:outer], refs[outer : outer + inner], refs[outer + inner :]
    sums, refs = refs[:ndp], refs[ndp:]
    grad_out, grad_gate, grad_value, grad_taps, product_of, total, sems, sum_sem = refs
    group = product_of.shape[2]
    plane, low = place(inner)
    copies = []

    def send(source, dest, sem):
        copies.append(pltpu.make_async_copy(source, dest, sem))
        copies[-1].start()

    def rows_of(there, where):
        return pl.ds(pl.multiple_of((there * inner + where) * group, ROWS), group)

    for far, part in enumerate(grad_parts):
        for where in range(inner):
            rows = rows_of(plane ^ far, where)
            send(part.at[0, where], grad_value.at[rows, :], sems.at[0, far, where])
    total[...] = sums[0][...]
    for other in sums[1:]:
        total[...] += other[...].astype(jnp.float32)
    send(total, grad_taps, sum_sem.at[0])
    for mask, part in enumerate(conv_parts):
        for there in range(outer):
            rows = rows_of(there, low ^ mask)
            product_of[there, mask] = (
                grad_out[rows, :].astype(jnp.float32) * part[0, there].astype(jnp.float32)
            ).astype(jnp.bfloat16)
            send(product_of.at[there, mask], grad_gate.at[rows, :], sems.at[1, there, mask])
    for copy in copies:
        copy.wait()


def vmem(count):
    return [pl.BlockSpec(memory_space=pltpu.VMEM)] * count


def anywhere(count):
    return [pl.BlockSpec(memory_space=pl.ANY)] * count


def call(kernel, outs, scratch, operands, ins=None, dests=None, mib=4, flops=10**9, after=()):
    count = len(operands)

    def ordered(*refs):
        kernel(*refs[len(after) :])

    return pl.pallas_call(
        ordered,
        out_shape=list(outs),
        in_specs=anywhere(len(after)) + (ins or vmem(count)),
        out_specs=dests or vmem(len(outs)),
        scratch_shapes=scratch,
        compiler_params=pltpu.CompilerParams(vmem_limit_bytes=mib * 1024 * 1024),
        cost_estimate=pl.CostEstimate(flops=flops, bytes_accessed=10**6, transcendentals=0),
        name=kernel.func.__name__,
    )(*after, *operands)


def permute(array, axis, target):
    count = lax.axis_size(axis)
    return lax.ppermute(array, axis, [(i, target(i)) for i in range(count)])


def on_device(grad_out, gate, value, filter_taps):
    nseq = lax.axis_size("seq")
    ndp = lax.axis_size("dp")
    chans = grad_out.shape[1]
    width = grad_out.shape[2]
    group = chans // nseq
    blocks = nseq
    inner = 1 << (nseq.bit_length() - 1) // 2
    outer = nseq // inner
    forward, inverse = (jnp.asarray(t) for t in inner_tables(blocks, width))
    factor = 1.0 / (ndp * math.sqrt(nseq * width))
    shape = jax.ShapeDtypeStruct
    bf16, f32 = jnp.bfloat16, jnp.float32

    def by_plane(count=1):
        return [shape((count, inner, group, width), bf16)] * outer

    def by_low(count=1):
        return [shape((count, outer, group, width), bf16)] * inner

    def arrivals(parts, count=outer - 1):
        return [parts[far] for far in range(outer - 1, outer - 1 - count, -1)]

    def in_plane(parts):
        return [
            permute(part, "seq", lambda i: i ^ mask) if mask else part
            for mask, part in enumerate(parts)
        ]

    def over_planes(found):
        return {
            far: permute(part, "seq", lambda i: i ^ (far * inner)) if far else part
            for far, part in found.items()
        }

    def turned(parts, fars, after=()):
        kernel = functools.partial(turn_kernel, inner, fars)
        outs = call(kernel, by_plane()[: len(fars)], [], parts, after=list(after))
        return dict(zip(fars, outs))

    def ordered(found):
        return [found[far] for far in range(outer)]

    everywhere = tuple(range(outer))

    value_packed = call(
        functools.partial(pack_planes_kernel, inner, outer),
        by_plane(),
        [pltpu.SemaphoreType.DMA((outer, inner))],
        [value[0]],
        ins=anywhere(1),
        mib=16,
    )
    taps_packed = call(
        functools.partial(pack_lows_kernel, inner, outer),
        by_low(),
        [pltpu.SemaphoreType.DMA((inner, outer))],
        [filter_taps],
        ins=anywhere(1),
        mib=16,
        after=value_packed[:1],
    )
    value_plane = ordered(over_planes(dict(enumerate(value_packed))))
    taps_low = in_plane(taps_packed)
    gated_packed = call(
        functools.partial(gated_kernel, inner, outer),
        by_low(),
        [pltpu.VMEM((inner, outer, group, width), bf16)] * 2
        + [pltpu.SemaphoreType.DMA((2, inner, outer))],
        [grad_out[0], gate[0], forward, inverse],
        ins=anywhere(2) + vmem(2),
        mib=16,
        after=taps_packed[:1],
    )
    gated_low = in_plane(gated_packed)
    taps_turned = turned(taps_low, everywhere, arrivals(value_plane, outer // 4) + list(gated_packed[:1]))
    taps_plane = ordered(over_planes(taps_turned))
    value_low = in_plane(
        call(
            functools.partial(turn_back_kernel, inner, outer),
            by_low(),
            [],
            value_plane,
            after=[taps_turned[0]] + arrivals(value_plane),
        )
    )

    spec = shape((blocks + 1, group, 2 * width), f32)
    signal = pltpu.VMEM((blocks, group, width), bf16)
    mid = pltpu.VMEM((blocks + 1, group, 2 * width), bf16)
    back = pltpu.VMEM((blocks + 1, group, 2 * width), f32)
    gated_turned = turned(gated_low, everywhere, arrivals(taps_plane, outer // 4))
    gated_plane = ordered(over_planes(gated_turned))
    spec_taps = call(
        functools.partial(taps_kernel, inner, outer),
        [spec],
        [signal, mid],
        taps_plane + [forward],
        mib=16,
        after=[gated_turned[0]] + arrivals(taps_plane),
    )[0]
    outs = call(
        functools.partial(conv_kernel, inner, outer),
        by_plane() + [spec],
        [signal, mid, back],
        value_low + [spec_taps, forward, inverse],
        mib=16,
    )
    held = call(
        functools.partial(hold_kernel), by_plane(), [], outs[:outer], after=arrivals(gated_plane, outer // 2)
    )
    conv_plane = ordered(over_planes(dict(enumerate(held))))
    spec_value = outs[outer]
    wide = (group, blocks // ndp * width)
    outs = call(
        functools.partial(grad_kernel, inner, outer),
        by_low() + [spec],
        [signal, mid, back],
        gated_plane + [spec_taps, forward, inverse],
        mib=16,
        after=[held[0]] + arrivals(gated_plane),
    )
    grad_low, spec_gated = in_plane(outs[:inner]), outs[inner]
    sums = list(
        call(
            functools.partial(cross_kernel, ndp, factor),
            [shape(wide, f32)] + [shape(wide, bf16)] * (ndp - 1),
            [pltpu.VMEM((blocks, group, width), f32), back],
            [spec_value, spec_gated, inverse],
            mib=16,
            after=arrivals(conv_plane, outer // 4),
        )
    )
    mine = sums[0]
    for step in range(1, ndp):
        sums[step] = permute(sums[step], "dp", lambda i: (i + step) % ndp)
    grad_turned = turned(grad_low, everywhere, arrivals(conv_plane, outer // 2) + [mine])
    grad_plane = ordered(over_planes(grad_turned))
    conv_low = in_plane(
        call(
            functools.partial(turn_back_kernel, inner, outer),
            by_low(),
            [],
            conv_plane,
            after=[grad_turned[0]] + sums[1:],
        )
    )
    grad_gate, grad_value, grad_taps = call(
        functools.partial(final_kernel, inner, outer, ndp),
        [shape((chans, width), bf16)] * 2 + [shape(wide, f32)],
        [
            pltpu.VMEM((outer, inner, group, width), bf16),
            pltpu.VMEM(wide, f32),
            pltpu.SemaphoreType.DMA((2, outer, inner)),
            pltpu.SemaphoreType.DMA((1,)),
        ],
        grad_plane + conv_low + sums + [grad_out[0]],
        dests=anywhere(3),
        mib=8,
        after=arrivals(grad_plane),
    )
    return (grad_gate[None], grad_value[None], grad_taps)


def solution(mesh):
    return jax.shard_map(
        on_device,
        mesh=mesh,
        in_specs=(P("dp", None, "seq"), P("dp", None, "seq"), P("dp", None, "seq"), P(None, "seq")),
        out_specs=(P("dp", None, "seq"), P("dp", None, "seq"), P("seq", "dp")),
        check_vma=False,
    )
```
